32 devices in a mesh: theta: 4 (over y, x), state: 8 (over z, core).
Axes of the slice: x: 2, y: 2, z: 4, core: 2. Of those that a mesh axis runs over, the one named last changes fastest.
Arguments:
- states: bfloat16 [32, 4096, 256], P('theta', 'state'), may hold values from -4.875 to 4.875
- log_vol: bfloat16 [32, 4096], P('theta', 'state'), may hold values from -3 to 3
- transition: bfloat16 [32, 256, 256], P('theta'), may hold values from -0.375 to 0.375
- loading: bfloat16 [256, 128], replicated, may hold values from -0.375 to 0.375
- yields: float32 [3, 128], replicated, may hold values from -5 to 5
- state_noise: bfloat16 [3, 4096, 256], P(None, 'state'), may hold values from -5 to 5
- vol_noise: float32 [3, 4096], P(None, 'state'), may hold values from -5 to 5
- vol_mean: float32 [32], replicated, may hold values from -1.5 to 0
- vol_persist: float32 [32], replicated, may hold values from 0.3 to 0.95
- vol_scale: float32 [32], replicated, may hold values from 0.1 to 0.6
- obs_prec: float32 [32], replicated, may hold values from 0.05 to 4
- prior_loglik: float32 [32], replicated, may hold values from -12 to 12
- ancestors: int32 [32], replicated, may hold values from 0 to 31, as said below
- counts: int32 [3, 32, 8], P(None, 'theta', 'state'), may hold values from 256 to 768, as said below
- local_anc: int32 [3, 32, 6144], P(None, 'theta', 'state'), may hold values from 0 to 511
Outputs:
- final_states: bfloat16 [32, 4096, 256], P('theta', 'state')
- final_vol: bfloat16 [32, 4096], P('theta', 'state')
- loglik: float32 [32], P('theta')
The draws below stay inside these ranges and needn't reach their ends.
Inputs may be any that keep to these rules, and one draw needn't show every extreme that they name: ancestors[i] lies in the group of 8 consecutive indices that holds i or in one of the two groups beside it; at most 4 indices of one group name the group below it and at most 4 name the group above it; both bounds are reached. For each step and parameter particle the counts over the shards sum to 4096; the sum of the counts of shards 0 to j - 1 differs from j * 512 by at most 128, and for each step and particle some shard reaches + 128 and some - 128. `local_anc`: only the first counts[t, i, j] slots of shard j's block are used.
All inputs are finite; a program needn't handle non-finite values.
Results may differ from the reference program's by a relative error of at most 0.001.
The reference program's roundings to bfloat16 on the way (of `cloud`) count: a program that leaves them out, or rounds other values in their place, can miss the bound.
Values may be sent and summed in bfloat16 or wider, within the bound.
No kernel may reach another device: no remote copies, remote signals or barrier semaphores. Data moves between devices by JAX's collectives and lax.ppermute only.
A program may use at most 64 MiB of HBM per device.

```python
import math
import jax
import jax.numpy as jnp
from jax import lax

K = 256
M = 128
P_DEV = 8
S_DEV = 512
STEPS = 3
MARGIN = 128
P_SIZE = 32
S = 4096
SLOTS = 6144


def draw_states(key, part):
    slot = jnp.arange(S, dtype=jnp.float32)
    scale = 0.6 + 0.6 * slot / S
    base = jnp.clip(jax.random.normal(key, (P_SIZE, S, K), jnp.float32), -4.0, 4.0)
    return (base * scale[None, :, None]).astype(jnp.bfloat16)


def draw_obs_prec(key, part):
    low, high = (0.05, 0.2)
    unit = jax.random.uniform(key, (P_SIZE,), jnp.float32)
    return jnp.exp(jnp.log(low) + unit * (jnp.log(high) - jnp.log(low)))


def draw_ancestors(key, part):
    keys = jax.random.split(jax.random.fold_in(key, 11), 4)
    groups = P_SIZE // P_DEV
    half = P_DEV // 2
    index = jnp.arange(P_SIZE, dtype=jnp.int32)
    group = index // P_DEV
    scores = jax.random.randint(keys[0], (P_SIZE,), 0, 1 << 20) * P_SIZE + index
    ranks = jnp.argsort(jnp.argsort(scores.reshape(groups, P_DEV), axis=1), axis=1).reshape(P_SIZE)
    coin = jax.random.randint(keys[1], (P_SIZE,), 0, 2) == 1
    chosen = jax.random.randint(keys[2], (), 1, groups - 1)
    moving = coin | (group == chosen)
    offset = jnp.where(moving, jnp.where(ranks < half, -1, 1), 0)
    offset = jnp.where((group == 0) & (offset == -1), 0, offset)
    offset = jnp.where((group == groups - 1) & (offset == 1), 0, offset)
    local = jax.random.randint(keys[3], (P_SIZE,), 0, P_DEV)
    return ((group + offset) * P_DEV + local).astype(jnp.int32)


def draw_counts(key, part):
    keys = jax.random.split(jax.random.fold_in(key, 23), 2)
    shards = S // S_DEV
    margin = S_DEV // 4
    inner = jax.random.randint(keys[0], (STEPS, P_SIZE, shards - 1), -margin, margin + 1)
    first = jax.random.randint(keys[1], (STEPS, P_SIZE, 1), 0, shards - 1)
    second = (first + 1) % (shards - 1)
    place = jnp.arange(shards - 1, dtype=jnp.int32)[None, None, :]
    inner = jnp.where(place == first, margin, inner)
    inner = jnp.where(place == second, -margin, inner)
    zeros = jnp.zeros((STEPS, P_SIZE, 1), jnp.int32)
    excess = jnp.concatenate([zeros, inner.astype(jnp.int32), zeros], axis=2)
    return (S_DEV + excess[:, :, 1:] - excess[:, :, :-1]).astype(jnp.int32)


def with_ends(drawn, rng, smallest, high):
    spot = [jax.random.randint(jax.random.fold_in(rng, axis), (), 0, length) for axis, length in enumerate(drawn.shape)]
    main_axis = drawn.shape.index(max(drawn.shape))
    next_to = spot[:main_axis] + [(spot[main_axis] + 1) % drawn.shape[main_axis]] + spot[main_axis + 1:]
    return drawn.at[tuple(spot)].set(smallest).at[tuple(next_to)].set(high)


def level_of(rng, shape, cuts, least, high):
    factor_of = 1.0
    for axis_at, parts in cuts:
        draws = jax.random.uniform(jax.random.fold_in(jax.random.fold_in(rng, 6), axis_at), (parts,), jnp.float32, least / len(cuts), high / len(cuts))
        factor_of = factor_of * jnp.repeat(jnp.exp(draws), shape[axis_at] // parts).reshape((-1,) + (1,) * (len(shape) - 1 - axis_at))
    return factor_of


def gaussian(rng, extent, scale, most, cuts=(), kind=jnp.bfloat16):
    array = jax.random.normal(rng, extent, jnp.float32) * scale
    if len(cuts) > 0:
        array = level_of(rng, extent, cuts, -0.22, 0.18) * array
    return jnp.clip(array, min=-most, max=most).astype(kind)


def setup_inputs(seed: int = 0) -> dict:
    splits = jax.random.split(jax.random.key(seed), 16)
    return {
        "states": draw_states(jax.random.fold_in(splits[15], 71), 0),
        "log_vol": gaussian(splits[1], (P_SIZE, S), 0.5, 3.0, ((0, 4), (1, 8))),
        "transition": gaussian(splits[2], (P_SIZE, K, K), K ** -0.5, 0.375, ((0, 4),)),
        "loading": gaussian(splits[3], (K, M), K ** -0.5, 0.375),
        "yields": gaussian(splits[4], (STEPS, M), 1.0, 5.0, (), jnp.float32),
        "state_noise": gaussian(splits[5], (STEPS, S, K), 1.0, 5.0, ((1, 8),)),
        "vol_noise": gaussian(splits[6], (STEPS, S), 1.0, 5.0, ((1, 8),), jnp.float32),
        "vol_mean": jnp.clip(jax.random.uniform(splits[7], (P_SIZE,), jnp.float32, -1.5, 0.0), -1.5, 0.0),
        "vol_persist": jnp.clip(jax.random.uniform(splits[8], (P_SIZE,), jnp.float32, 0.3, 0.95), 0.3, 0.95),
        "vol_scale": jnp.clip(jnp.exp(jax.random.uniform(splits[9], (P_SIZE,), jnp.float32, math.log(0.1), math.log(0.6))), 0.1, 0.6),
        "obs_prec": draw_obs_prec(jax.random.fold_in(splits[15], 71), 0),
        "prior_loglik": gaussian(splits[11], (P_SIZE,), 3.0, 12.0, (), jnp.float32),
        "ancestors": draw_ancestors(jax.random.fold_in(splits[15], 71), 0),
        "counts": draw_counts(jax.random.fold_in(splits[15], 71), 0),
        "local_anc": with_ends(jax.random.randint(splits[14], (STEPS, P_SIZE, SLOTS), 0, S_DEV), jax.random.fold_in(splits[14], 1), 0, S_DEV - 1).astype(jnp.int32),
    }


def reference(states, log_vol, transition, loading, yields, state_noise, vol_noise, vol_mean, vol_persist, vol_scale, obs_prec, prior_loglik, ancestors, counts, local_anc):
    shard_slots = S_DEV + 2 * MARGIN
    positions = jnp.arange(S, dtype=jnp.int32)

    def particle(which):
        source = ancestors[which]
        cloud = states[source]
        vols = log_vol[source]
        matrix = transition[source]
        center = vol_mean[source]
        persist = vol_persist[source]
        spread = vol_scale[source]
        precision = obs_prec[source]
        total = prior_loglik[source]
        for step in range(STEPS):
            number = counts[step, which].astype(jnp.int32)
            starts = (jnp.cumsum(number) - number).astype(jnp.int32)
            owner = (jnp.sum((starts[None, :] <= positions[:, None]).astype(jnp.int32), axis=1) - 1).astype(jnp.int32)
            offset = (positions - starts[owner]).astype(jnp.int32)
            chosen = local_anc[step, which][owner * shard_slots + offset]
            anchor = (owner * S_DEV + chosen).astype(jnp.int32)
            cloud = cloud[anchor]
            vols_now = vols[anchor].astype(jnp.float32)
            vols_now = center + persist * (vols_now - center) + spread * vol_noise[step]
            drift = jnp.dot(cloud, matrix, preferred_element_type=jnp.float32)
            cloud = (drift + jnp.exp(0.5 * vols_now)[:, None] * state_noise[step].astype(jnp.float32)).astype(jnp.bfloat16)
            vols = vols_now.astype(jnp.bfloat16)
            predicted = jnp.dot(cloud, loading, preferred_element_type=jnp.float32)
            misfit = yields[step][None, :] - predicted
            weights_log = -0.5 * precision * jnp.sum(misfit * misfit, axis=1) + 0.5 * M * jnp.log(precision)
            peak = jnp.max(weights_log)
            total = total + peak + jnp.log(jnp.sum(jnp.exp(weights_log - peak))) - math.log(S)
        return cloud, vols, total

    return lax.map(particle, jnp.arange(P_SIZE, dtype=jnp.int32))
```

```python
import functools
import math

import jax
import jax.numpy as jnp
from jax import lax
from jax.experimental import pallas as pl
from jax.experimental.pallas import tpu as pltpu
from jax.sharding import PartitionSpec as P

STEPS = 3
LANES = 128
ROWS = 8
PAD = 16
VLIMIT = 48 * 1024 * 1024

VM = pltpu.VMEM
SM = pltpu.SMEM
F32 = jnp.float32
BF16 = jnp.bfloat16
I32 = jnp.int32


def vmem():
    return pl.BlockSpec(memory_space=pltpu.VMEM)


def smem():
    return pl.BlockSpec(memory_space=pltpu.SMEM)


def anywhere():
    return pl.BlockSpec(memory_space=pl.ANY)


def call(kernel, out_shape, in_specs, out_specs, name, scratch=(), flops=0, nbytes=0, aliases=None):
    return pl.pallas_call(
        kernel,
        out_shape=out_shape,
        in_specs=in_specs,
        out_specs=out_specs,
        scratch_shapes=list(scratch),
        input_output_aliases=aliases or {},
        compiler_params=pltpu.CompilerParams(vmem_limit_bytes=VLIMIT),
        cost_estimate=pl.CostEstimate(flops=flops, bytes_accessed=nbytes, transcendentals=0),
        name=name,
    )


def pack_kernel(slots, slot_rows, vol_rows, names_ref, states_ref, vols_ref, *rest):
    outs, (tail, sems) = rest[: len(slots)], rest[len(slots) :]
    copies = []
    for side, (out, chosen) in enumerate(zip(outs, slots)):
        for place, slot in enumerate(chosen):
            copy = pltpu.make_async_copy(
                states_ref.at[names_ref[side, slot]],
                out.at[pl.ds(place * slot_rows, slot_rows)],
                sems.at[side, place],
            )
            copy.start()
            copies.append(copy)
        width = out.shape[1]
        pieces = []
        for slot in chosen:
            row = vols_ref[pl.ds(names_ref[side, slot], 1), :]
            pieces += [row[:, k * width : (k + 1) * width] for k in range(vol_rows)]
        short = tail.shape[1] - len(pieces)
        pieces.append(jnp.zeros((short, width), F32))
        tail[side] = jnp.concatenate(pieces, axis=0).astype(BF16)
        copy = pltpu.make_async_copy(
            tail.at[side],
            out.at[pl.ds(len(chosen) * slot_rows, tail.shape[1])],
            sems.at[side, len(chosen)],
        )
        copy.start()
        copies.append(copy)
    for copy in copies:
        copy.wait()


def matrix_part_kernel(part_rows, names_ref, shard_ref, transition_ref, below_ref, above_ref, sems):
    side_rows = transition_ref.shape[1]
    piece = math.gcd(part_rows, side_rows)
    copies = []
    for side, out in enumerate((below_ref, above_ref)):
        for k in range(part_rows // piece):
            at = shard_ref[0] * part_rows + k * piece
            copy = pltpu.make_async_copy(
                transition_ref.at[
                    names_ref[side, at // side_rows],
                    pl.ds(pl.multiple_of(at % side_rows, piece), piece),
                ],
                out.at[pl.ds(k * piece, piece)],
                sems.at[side, k],
            )
            copy.start()
            copies.append(copy)
    for copy in copies:
        copy.wait()


def lane_pick(blocks, index):
    low = index & (LANES - 1)
    high = index >> 7
    out = None
    for k, block in blocks:
        got = jnp.take_along_axis(block, low, axis=1, mode="promise_in_bounds")
        out = got if out is None else jnp.where(high == k, got, out)
    return out


def column(scalars):
    rows = lax.broadcasted_iota(I32, (ROWS, 1), 0)
    out = jnp.zeros((ROWS, 1), scalars[0].dtype)
    for b, scalar in enumerate(scalars):
        out = jnp.where(rows == b, scalar, out)
    return out


def index_kernel(batches, s_dev, margin, meta_ref, count_ref, first_ref, shard_ref, anc_ref, *outs):
    base = shard_ref[0] * s_dev
    lanes = lax.broadcasted_iota(I32, (ROWS, LANES), 1)
    for q, batch in enumerate(batches):
        src_ref, src_t_ref, edge_ref, edge_t_ref = outs[4 * q : 4 * q + 4]
        for step in range(STEPS):
            who = [meta_ref[0, batch[b % len(batch)]] for b in range(ROWS)]
            chosen = jnp.concatenate([anc_ref[step, pl.ds(i, 1), :] for i in who], axis=0)
            blocks = [chosen[:, k * LANES : (k + 1) * LANES] for k in range(chosen.shape[1] // LANES)]
            count = column([count_ref[step, i] for i in who])
            shift = column([base - first_ref[step, i] for i in who])
            sources = []
            for o in range(s_dev // LANES):
                relative = o * LANES + lanes + shift
                near = [(k, blocks[k]) for k in range(len(blocks))]
                own = lane_pick(near, jnp.clip(relative, 0, chosen.shape[1] - 1))
                sources.append(
                    jnp.where(
                        relative < 0,
                        relative + margin,
                        jnp.where(relative < count, margin + own, margin + s_dev + relative - count),
                    )
                )
            source = jnp.concatenate(sources, axis=1)
            src_ref[step] = source
            src_t_ref[step] = source.T
            edges = [blocks[k] for k in range(margin // LANES)]
            for o in range(margin // LANES):
                edges.append(lane_pick(list(enumerate(blocks)), count - margin + o * LANES + lanes))
            edge = jnp.concatenate(edges, axis=1)
            edge_ref[step] = edge
            edge_t_ref[step] = edge.T


def one_hot(index, columns):
    return (index == lax.broadcasted_iota(I32, (index.shape[0], columns), 1)).astype(BF16)


def send_edges(batch, margin, cloud_at, vol, edge, edge_t, low_ref, high_ref):
    s_dev = vol.shape[1]
    for b in range(batch):
        rows = jnp.dot(
            one_hot(edge_t[:, b : b + 1], s_dev), cloud_at(b), preferred_element_type=F32
        ).astype(BF16)
        low_ref[pl.ds(b * margin, margin), :] = rows[:margin]
        high_ref[pl.ds(b * margin, margin), :] = rows[margin:]
    blocks = [(k, vol[:, k * LANES : (k + 1) * LANES]) for k in range(s_dev // LANES)]
    width = low_ref.shape[1]
    for out, start in ((low_ref, 0), (high_ref, margin)):
        picked = [
            lane_pick(blocks, edge[:, start + o * LANES : start + (o + 1) * LANES])
            for o in range(margin // LANES)
        ]
        picked.append(jnp.zeros((ROWS, width - margin), F32))
        flat = jnp.concatenate(picked, axis=1)
        flat = jnp.concatenate([flat, jnp.zeros((PAD - ROWS, width), F32)], axis=0)
        out[pl.ds(batch * margin, PAD), :] = flat.astype(BF16)


def fetch_kernel(batch, first_place, margin, recv_slots, p_dev, meta_ref, states_ref, vols_ref,
                 edge_ref, edge_t_ref, *rest):
    recv = rest[: len(recv_slots)]
    cloud_ref, vol_ref, low_ref, high_ref, sems = rest[len(recv_slots) :]
    s_dev = states_ref.shape[1]
    for b in range(batch):
        place = meta_ref[1, first_place + b]

        @pl.when(place < p_dev)
        def _(b=b, place=place):
            pltpu.make_async_copy(
                states_ref.at[jnp.minimum(place, p_dev - 1)], cloud_ref.at[b], sems.at[b]
            ).start()

        for ref, codes in zip(recv, recv_slots):
            for k, code in enumerate(codes):

                @pl.when(place == code)
                def _(b=b, ref=ref, k=k):
                    pltpu.make_async_copy(
                        ref.at[pl.ds(k * s_dev, s_dev)], cloud_ref.at[b], sems.at[b]
                    ).start()

    vol = jnp.concatenate(
        [vols_ref[pl.ds(meta_ref[1, first_place + b % batch], 1), :] for b in range(ROWS)], axis=0
    )
    vol_ref[...] = vol
    for b in range(batch):
        pltpu.make_async_copy(states_ref.at[0], cloud_ref.at[b], sems.at[b]).wait()
    send_edges(batch, margin, lambda b: cloud_ref[b], vol, edge_ref[0], edge_t_ref[0], low_ref, high_ref)


def matrix_kernel(p_dev, meta_ref, transition_ref, moved_ref, out_ref, sems):
    for b in range(p_dev):
        place = meta_ref[1, b]

        @pl.when(place < p_dev)
        def _(b=b, place=place):
            pltpu.make_async_copy(
                transition_ref.at[jnp.minimum(place, p_dev - 1)], out_ref.at[b], sems.at[b]
            ).start()

        @pl.when(place >= p_dev)
        def _(b=b, place=place):
            pltpu.make_async_copy(
                moved_ref.at[jnp.maximum(place - p_dev, 0)], out_ref.at[b], sems.at[b]
            ).start()

    for b in range(p_dev):
        pltpu.make_async_copy(transition_ref.at[0], out_ref.at[b], sems.at[b]).wait()


def own_kernel(batch, step, margin, src_t_ref, cloud_ref, out_ref):
    s_dev = cloud_ref.shape[1]
    for b in range(batch):
        index = src_t_ref[step][:, b : b + 1] - margin
        out_ref[b] = jnp.dot(
            one_hot(index, s_dev), cloud_ref[b], preferred_element_type=F32
        ).astype(BF16)


def step_kernel(batch, first_place, step, margin, par_ref, meta_ref, own_ref, low_ref, high_ref, vol_ref,
                src_ref, src_t_ref, edge_ref, edge_t_ref, matrix_ref, noise_ref, vnoise_ref,
                loading_ref, yields_ref, *rest):
    last = step == STEPS - 1
    s_dev = vol_ref.shape[1]
    if last:
        *_, final_ref, vol_out, stat_ref, cloud_out, sems = rest
    else:
        cloud_out, vol_out, stat_ref, low_out, high_out = rest
    source = src_ref[step]
    vol = vol_ref[...]
    blocks = [(k, vol[:, k * LANES : (k + 1) * LANES]) for k in range(s_dev // LANES)]

    def edge_vols(ref):
        return ref[pl.ds(batch * margin, PAD), :].astype(F32)[:ROWS]

    low_v, high_v = edge_vols(low_ref), edge_vols(high_ref)
    picked = []
    for o in range(s_dev // LANES):
        index = source[:, o * LANES : (o + 1) * LANES]
        own = lane_pick(blocks, jnp.clip(index - margin, 0, s_dev - 1))
        if o < margin // LANES:
            low = [(k, low_v[:, k * LANES : (k + 1) * LANES]) for k in range(margin // LANES)]
            own = jnp.where(index < margin, lane_pick(low, index), own)
        if o >= (s_dev - margin) // LANES:
            high = [(k, high_v[:, k * LANES : (k + 1) * LANES]) for k in range(margin // LANES)]
            above = jnp.clip(index - margin - s_dev, 0, margin - 1)
            own = jnp.where(index >= margin + s_dev, lane_pick(high, above), own)
        picked.append(own)
    picked = jnp.concatenate(picked, axis=1)

    def param(k):
        return column([par_ref[k, first_place + b % batch] for b in range(ROWS)])

    center, persist, spread = param(0), param(1), param(2)
    h = center + persist * (picked - center) + spread * vnoise_ref[...]
    scale_t = jnp.exp(0.5 * h).T
    vol_new = h.astype(BF16).astype(F32)
    vol_out[...] = vol_new

    src_t = src_t_ref[step]
    noise = noise_ref[...].astype(F32)
    loading_t = loading_ref[...]
    wanted = yields_ref[...]
    squares = []
    for b in range(batch):
        index = src_t[:, b : b + 1]
        low = jnp.dot(
            one_hot(index[:margin], margin),
            low_ref[pl.ds(b * margin, margin), :],
            preferred_element_type=F32,
        )
        high = jnp.dot(
            one_hot(index[s_dev - margin :] - (margin + s_dev), margin),
            high_ref[pl.ds(b * margin, margin), :],
            preferred_element_type=F32,
        )
        own = own_ref[b]
        cloud = jnp.concatenate(
            [
                (own[:margin].astype(F32) + low).astype(BF16),
                own[margin : s_dev - margin],
                (own[s_dev - margin :].astype(F32) + high).astype(BF16),
            ],
            axis=0,
        )
        drift = jnp.dot(cloud, matrix_ref[first_place + b], preferred_element_type=F32)
        cloud = (drift + scale_t[:, b : b + 1] * noise).astype(BF16)
        cloud_out[b] = cloud
        if last:
            pltpu.make_async_copy(
                cloud_out.at[b], final_ref.at[meta_ref[0, first_place + b]], sems.at[b]
            ).start()
        predicted = lax.dot_general(
            loading_t, cloud, (((1,), (1,)), ((), ())), preferred_element_type=F32
        )
        misfit = wanted - predicted
        squares.append(jnp.sum(misfit * misfit, axis=0, keepdims=True))
    squares += [squares[0]] * (ROWS - batch)
    square = jnp.concatenate(squares, axis=0)
    precision = param(3)
    maturities = yields_ref.shape[0]
    weights = -0.5 * precision * square + 0.5 * maturities * jnp.log(precision)
    peak = jnp.max(weights, axis=1, keepdims=True)
    mass = jnp.sum(jnp.exp(weights - peak), axis=1, keepdims=True)
    lane = lax.broadcasted_iota(I32, (ROWS, LANES), 1)
    stat_ref[...] = jnp.where(lane == 0, peak, mass)
    if last:
        for b in range(batch):
            pltpu.make_async_copy(cloud_out.at[b], final_ref.at[0], sems.at[b]).wait()
    else:
        send_edges(
            batch, margin, lambda b: cloud_out[b], vol_new, edge_ref[step + 1], edge_t_ref[step + 1],
            low_out, high_out,
        )


def shifts(count):
    forward = [(i, i + 1) for i in range(count - 1)]
    return forward, [(target, source) for source, target in forward]


def doubling(count):
    distance = 1
    while distance < count:
        yield distance, [(i, i ^ distance) for i in range(count)]
        distance *= 2


def prefix_counts(number):
    count, here = lax.axis_size("state"), lax.axis_index("state")
    if count & (count - 1):
        every = lax.all_gather(number, "state")
        before = jnp.arange(count) < here
        return jnp.sum(jnp.where(before[:, None, None], every, 0), axis=0)
    before, total = jnp.zeros_like(number), number
    for distance, pairs in doubling(count):
        other = lax.ppermute(total, "state", pairs)
        before = before + jnp.where((here & distance) != 0, other, 0)
        total = total + other
    return before


def join_mass(peak, mass, other_peak, other_mass):
    top = jnp.maximum(peak, other_peak)
    return top, mass * jnp.exp(peak - top) + other_mass * jnp.exp(other_peak - top)


def combined_mass(peak, mass):
    count = lax.axis_size("state")
    if count & (count - 1):
        peaks, masses = lax.all_gather(peak, "state"), lax.all_gather(mass, "state")
        top = jnp.max(peaks, axis=0)
        return top, jnp.sum(masses * jnp.exp(peaks - top), axis=0)
    for _, pairs in doubling(count):
        other = lax.ppermute(jnp.stack([peak, mass]), "state", pairs)
        peak, mass = join_mass(peak, mass, other[0], other[1])
    return peak, mass


def pick(index, table):
    hit = index[:, None] == jnp.arange(table.shape[0], dtype=I32)[None, :]
    return jnp.sum(jnp.where(hit, table[None, :], jnp.zeros((), table.dtype)), axis=1)


def local(
    states,
    log_vol,
    transition,
    loading,
    yields,
    state_noise,
    vol_noise,
    vol_mean,
    vol_persist,
    vol_scale,
    obs_prec,
    prior_loglik,
    ancestors,
    counts,
    local_anc,
):
    p_dev, s_dev, width = states.shape
    maturities = loading.shape[1]
    groups, shards = lax.axis_size("theta"), lax.axis_size("state")
    group, shard = lax.axis_index("theta"), lax.axis_index("state")
    half = p_dev // 2
    margin = s_dev // 4
    batch = p_dev // 2
    batches = [tuple(range(q * batch, (q + 1) * batch)) for q in range(p_dev // batch)]
    early = half // 2
    chunks = [tuple(range(0, early)), tuple(range(early, half))]

    table = ancestors.reshape(groups, p_dev)
    ids = jnp.arange(p_dev, dtype=I32)

    def named(row_group):
        row = lax.dynamic_index_in_dim(table, jnp.clip(row_group, 0, groups - 1), 0, keepdims=False)
        offset = row // p_dev - jnp.clip(row_group, 0, groups - 1)
        ahead = ids[None, :] < ids[:, None]

        def rank(flag):
            return jnp.sum((ahead & flag[None, :]).astype(I32), axis=1)

        return row, row % p_dev, offset, rank(offset == -1), rank(offset == 1)

    mine, source, offset, rank_low, rank_high = named(group)
    slot_ids = jnp.arange(half, dtype=I32)

    def wanted(row_group, side):
        _, row_source, row_offset, low, high = named(row_group)
        rank = low if side == -1 else high
        hit = (row_offset == side)[None, :] & (rank[None, :] == slot_ids[:, None])
        return jnp.sum(jnp.where(hit, row_source[None, :], 0), axis=1)

    names = jnp.stack([wanted(group + 1, -1), wanted(group - 1, 1)]).astype(I32)
    place = jnp.where(
        offset == 0, source, jnp.where(offset == -1, p_dev + rank_low, p_dev + half + rank_high)
    )
    late = ((offset == -1) & (rank_low >= early)) | ((offset == 1) & (rank_high >= early))
    key = late.astype(I32) * p_dev + ids
    position = jnp.sum((key[None, :] < key[:, None]).astype(I32), axis=1)
    hit = position[None, :] == ids[:, None]
    order = jnp.sum(jnp.where(hit, ids[None, :], 0), axis=1)
    meta = jnp.stack([order, jnp.sum(jnp.where(hit, place[None, :], 0), axis=1)]).astype(I32)
    mine_ordered = jnp.sum(jnp.where(hit, mine[None, :], 0), axis=1)
    par = jnp.stack([pick(mine_ordered, x) for x in (vol_mean, vol_persist, vol_scale, obs_prec)])
    shard_arr = shard.astype(I32).reshape(1)
    vols_own = log_vol.astype(F32)

    forward, backward = shifts(groups)
    sides = (forward, backward)

    part_rows = half * width // shards
    part_shape = jax.ShapeDtypeStruct((part_rows, width), BF16)
    piece = math.gcd(part_rows, width)
    parts = call(
        functools.partial(matrix_part_kernel, part_rows),
        [part_shape, part_shape],
        [smem(), smem(), anywhere()],
        [anywhere(), anywhere()],
        "matrix_part",
        [pltpu.SemaphoreType.DMA((2, part_rows // piece))],
        nbytes=4 * part_rows * width * 2,
    )(names, shard_arr, transition)
    part_in = jnp.stack([lax.ppermute(part, "theta", pairs) for part, pairs in zip(parts, sides)])
    moved = lax.all_gather(part_in, "state", axis=1, tiled=True).reshape(2 * half, width, width)

    vol_rows = s_dev // width
    chunk_in = []
    for chunk in chunks:
        tail = -(-len(chunk) * vol_rows // PAD) * PAD
        shape = jax.ShapeDtypeStruct((len(chunk) * s_dev + tail, width), BF16)
        packed = call(
            functools.partial(pack_kernel, (chunk, chunk), s_dev, vol_rows),
            [shape, shape],
            [smem(), anywhere(), vmem()],
            [anywhere(), anywhere()],
            "pack",
            [pltpu.VMEM((2, tail, width), BF16), pltpu.SemaphoreType.DMA((2, len(chunk) + 1))],
            nbytes=4 * len(chunk) * s_dev * width * 2,
        )(names, states, vols_own)
        chunk_in.append([lax.ppermute(x, "theta", pairs) for x, pairs in zip(packed, sides)])

    number = counts[:, :, 0]
    first = prefix_counts(number)
    index_shapes = [
        jax.ShapeDtypeStruct((STEPS, ROWS, s_dev), I32),
        jax.ShapeDtypeStruct((STEPS, s_dev, ROWS), I32),
        jax.ShapeDtypeStruct((STEPS, ROWS, 2 * margin), I32),
        jax.ShapeDtypeStruct((STEPS, 2 * margin, ROWS), I32),
    ]
    indices = call(
        functools.partial(index_kernel, batches, s_dev, margin),
        index_shapes * len(batches),
        [smem(), smem(), smem(), smem(), vmem()],
        [vmem()] * (4 * len(batches)),
        "indices",
        nbytes=1 << 18,
    )(meta, number, first, shard_arr, local_anc)

    matrices = call(
        functools.partial(matrix_kernel, p_dev),
        jax.ShapeDtypeStruct((p_dev, width, width), BF16),
        [smem(), anywhere(), anywhere()],
        vmem(),
        "matrices",
        [pltpu.SemaphoreType.DMA((p_dev,))],
        nbytes=p_dev * width * width * 4,
    )(meta, transition, moved)

    loading_t = loading.T
    wanted_yields = [yields[step].reshape(maturities, 1) for step in range(STEPS)]
    up, down = shifts(shards)
    edge_shape = jax.ShapeDtypeStruct((batch * margin + PAD, width), BF16)
    cloud_shape = jax.ShapeDtypeStruct((batch, s_dev, width), BF16)
    vol_shape = jax.ShapeDtypeStruct((ROWS, s_dev), F32)
    stat_shape = jax.ShapeDtypeStruct((ROWS, LANES), F32)
    final = None
    vols_out, stats_out = [], []
    for q in range(len(batches)):
        src, src_t, edge, edge_t = indices[4 * q : 4 * q + 4]
        used = range(q + 1)
        recv, recv_slots = [], []
        vol_tables = []
        for side in range(2):
            rows = []
            for c in range(len(chunks)):
                if c in used:
                    buffer = chunk_in[c][side]
                    recv.append(buffer)
                    recv_slots.append(tuple(p_dev + side * half + k for k in chunks[c]))
                    size = len(chunks[c])
                    got = buffer[size * s_dev : size * s_dev + size * vol_rows]
                    rows.append(got.reshape(size, s_dev).astype(F32))
                else:
                    rows.append(jnp.zeros((len(chunks[c]), s_dev), F32))
            vol_tables += rows
        vol_table = jnp.concatenate([vols_own] + vol_tables, axis=0)
        cloud, vol, low, high = call(
            functools.partial(fetch_kernel, batch, q * batch, margin, tuple(recv_slots), p_dev),
            [cloud_shape, vol_shape, edge_shape, edge_shape],
            [smem(), anywhere(), vmem(), vmem(), vmem()] + [anywhere()] * len(recv),
            [vmem()] * 4,
            "fetch",
            [pltpu.SemaphoreType.DMA((batch,))],
            flops=2 * batch * 2 * margin * s_dev * width,
            nbytes=2 * batch * s_dev * width * 2,
        )(meta, states, vol_table, edge, edge_t, *recv)
        stats = []
        for step in range(STEPS):
            last = step == STEPS - 1
            low_in = lax.ppermute(high, "state", up)
            high_in = lax.ppermute(low, "state", down)
            own = call(
                functools.partial(own_kernel, batch, step, margin),
                cloud_shape,
                [vmem(), vmem()],
                vmem(),
                "own_rows",
                flops=2 * batch * s_dev * s_dev * width,
                nbytes=batch * s_dev * width * 4,
            )(src_t, cloud)
            operands = [
                par, meta, own, low_in, high_in, vol, src, src_t, edge, edge_t, matrices,
                state_noise[step], vol_noise[step].reshape(1, s_dev), loading_t, wanted_yields[step],
            ]
            specs = [smem(), smem()] + [vmem()] * (len(operands) - 2)
            aliases, scratch = None, []
            if last:
                out_shape = [jax.ShapeDtypeStruct(states.shape, BF16), vol_shape, stat_shape]
                out_specs = [anywhere(), vmem(), vmem()]
                scratch = [
                    pltpu.VMEM((batch, s_dev, width), BF16),
                    pltpu.SemaphoreType.DMA((batch,)),
                ]
                if final is not None:
                    aliases = {len(operands): 0}
                    operands.append(final)
                    specs.append(anywhere())
            else:
                out_shape = [cloud_shape, vol_shape, stat_shape, edge_shape, edge_shape]
                out_specs = [vmem()] * 5
            results = call(
                functools.partial(step_kernel, batch, q * batch, step, margin),
                out_shape,
                specs,
                out_specs,
                "step",
                scratch,
                flops=2 * batch * s_dev * width * (width + maturities + margin),
                nbytes=batch * s_dev * width * 8,
                aliases=aliases,
            )(*operands)
            if last:
                final, vol, stat = results
            else:
                cloud, vol, stat, low, high = results
            stats.append(stat[:batch, :2])
        vols_out.append(vol[:batch])
        stats_out.append(jnp.stack(stats))

    stats = jnp.concatenate(stats_out, axis=1)
    peak, mass = combined_mass(stats[:, :, 0], stats[:, :, 1])
    whole_rows = s_dev * shards
    gained = jnp.sum(peak + jnp.log(mass) - math.log(whole_rows), axis=0)
    back = position[:, None] == ids[None, :]
    gained = jnp.sum(jnp.where(back, gained[None, :], 0.0), axis=1)
    total = pick(mine, prior_loglik) + gained
    vols = jnp.concatenate(vols_out, axis=0)
    vols = jnp.sum(jnp.where(back[:, :, None], vols[None], 0.0), axis=1).astype(BF16)
    return (final, vols, total)


def solution(mesh):
    placed = (
        P("theta", "state", None),
        P("theta", "state"),
        P("theta", None, None),
        P(),
        P(),
        P(None, "state", None),
        P(None, "state"),
        P(),
        P(),
        P(),
        P(),
        P(),
        P(),
        P(None, "theta", "state"),
        P(None, "theta", "state"),
    )
    return jax.shard_map(
        local,
        mesh=mesh,
        in_specs=placed,
        out_specs=(P("theta", "state", None), P("theta", "state"), P("theta")),
        check_vma=False,
    )
```

```python
import functools
import math

import jax
import jax.numpy as jnp
from jax import lax
from jax.experimental import pallas as pl
from jax.experimental.pallas import tpu as pltpu
from jax.sharding import PartitionSpec as P

STEPS = 3
LANES = 128
ROWS = 8
PAD = 16
VLIMIT = 16 * 1024 * 1024

VM = pltpu.VMEM
SM = pltpu.SMEM
F32 = jnp.float32
BF16 = jnp.bfloat16
I32 = jnp.int32


def vmem():
    return pl.BlockSpec(memory_space=pltpu.VMEM)


def smem():
    return pl.BlockSpec(memory_space=pltpu.SMEM)


def anywhere():
    return pl.BlockSpec(memory_space=pl.ANY)


def hbm():
    return pl.BlockSpec(memory_space=pltpu.HBM)


def call(kernel, out_shape, in_specs, out_specs, name, scratch=(), flops=0, nbytes=0, aliases=None):
    return pl.pallas_call(
        kernel,
        out_shape=out_shape,
        in_specs=in_specs,
        out_specs=out_specs,
        scratch_shapes=list(scratch),
        input_output_aliases=aliases or {},
        compiler_params=pltpu.CompilerParams(vmem_limit_bytes=VLIMIT),
        cost_estimate=pl.CostEstimate(flops=flops, bytes_accessed=nbytes, transcendentals=0),
        name=name,
    )


def plan_kernel(groups, shards, chunks, batches, part_rows, vol_rows, where_ref, anc_ref, *rest):
    tables, (states_ref, vols_ref, transition_ref), rest = rest[:5], rest[5:8], rest[8:]
    part_outs, rest = rest[:2], rest[2:]
    chunk_outs, rest = rest[: 2 * len(chunks)], rest[2 * len(chunks) :]
    meta_ref, cols_ref, prior_ref, names, table, tails, part_sems, sems = rest
    p_dev, s_dev, width = states_ref.shape
    half = p_dev // 2
    early = half // 2
    group, shard = where_ref[0], where_ref[1]

    for side in range(2):
        other = jnp.clip(group + 1 - 2 * side, 0, groups - 1)
        wanted = jnp.int32(2 * side - 1)
        for k in range(half):
            names[side, k] = 0
        rank = jnp.int32(0)
        for i in range(p_dev):
            a = anc_ref[other * p_dev + i]
            hit = lax.div(a, p_dev) - other == wanted

            @pl.when(hit)
            def _(side=side, rank=rank, a=a):
                names[side, rank] = lax.rem(a, p_dev)

            rank = rank + hit.astype(I32)

    piece = math.gcd(part_rows, width)
    copies = []
    for side, out in enumerate(part_outs):
        for k in range(part_rows // piece):
            at = shard * part_rows + k * piece
            copy = pltpu.make_async_copy(
                transition_ref.at[
                    names[side, lax.div(at, width)],
                    pl.ds(pl.multiple_of(lax.rem(at, width), piece), piece),
                ],
                out.at[pl.ds(k * piece, piece)],
                part_sems.at[side, k],
            )
            copy.start()
            copies.append(copy)
    for c, chunk in enumerate(chunks):
        for side in range(2):
            for k, slot in enumerate(chunk):
                copy = pltpu.make_async_copy(
                    states_ref.at[names[side, slot]],
                    chunk_outs[2 * c + side].at[pl.ds(k * s_dev, s_dev)],
                    sems.at[c, side, k],
                )
                copy.start()
                copies.append(copy)

    table[...] = vols_ref[...].astype(F32)
    for c, chunk in enumerate(chunks):
        for side in range(2):
            pieces = []
            for slot in chunk:
                row = table[pl.ds(names[side, slot], 1), :]
                pieces += [row[:, k * width : (k + 1) * width] for k in range(vol_rows)]
            pieces.append(jnp.zeros((tails.shape[2] - len(pieces), width), F32))
            tails[c, side] = jnp.concatenate(pieces, axis=0).astype(BF16)
            copy = pltpu.make_async_copy(
                tails.at[c, side],
                chunk_outs[2 * c + side].at[pl.ds(len(chunk) * s_dev, tails.shape[2])],
                sems.at[c, side, len(chunk)],
            )
            copy.start()
            copies.append(copy)

    rank_low, rank_high = jnp.int32(0), jnp.int32(0)
    front, back = jnp.int32(0), jnp.int32(p_dev - 1)
    for i in range(p_dev):
        a = anc_ref[group * p_dev + i]
        offset = lax.div(a, p_dev) - group
        low, high = offset == -1, offset == 1
        late = (low & (rank_low >= early)) | (high & (rank_high >= early))
        place = jnp.where(
            low, p_dev + rank_low, jnp.where(high, p_dev + half + rank_high, lax.rem(a, p_dev))
        )
        position = jnp.where(late, back, front)
        meta_ref[0, position] = i
        meta_ref[1, position] = place
        meta_ref[2, position] = a
        front = front + jnp.where(late, 0, 1)
        back = back - jnp.where(late, 1, 0)
        rank_low = rank_low + low.astype(I32)
        rank_high = rank_high + high.astype(I32)
    for q, batch in enumerate(batches):
        for k in range(4):
            value = column([tables[k][meta_ref[2, batch[b % len(batch)]]] for b in range(ROWS)])
            cols_ref[q, k] = jnp.broadcast_to(value, (ROWS, LANES))
    prior = column([tables[4][anc_ref[group * p_dev + i]] for i in range(p_dev)])
    prior_ref[...] = jnp.broadcast_to(prior, (ROWS, LANES))
    for copy in copies:
        copy.wait()


def lane_pick(blocks, index):
    low = index & (LANES - 1)
    high = index >> 7
    out = None
    for k, block in blocks:
        got = jnp.take_along_axis(block, low, axis=1, mode="promise_in_bounds")
        out = got if out is None else jnp.where(high == k, got, out)
    return out


def column(scalars):
    rows = lax.broadcasted_iota(I32, (ROWS, 1), 0)
    out = jnp.zeros((ROWS, 1), scalars[0].dtype)
    for b, scalar in enumerate(scalars):
        out = jnp.where(rows == b, scalar, out)
    return out


def index_kernel(batches, s_dev, margin, meta_ref, count_ref, first_ref, where_ref, anc_ref,
                 loading_ref, yields_ref, *outs):
    base = where_ref[1] * s_dev
    lanes = lax.broadcasted_iota(I32, (ROWS, LANES), 1)
    for q, batch in enumerate(batches):
        src_ref, src_t_ref, edge_ref, edge_t_ref = outs[4 * q : 4 * q + 4]
        for step in range(STEPS):
            who = [meta_ref[0, batch[b % len(batch)]] for b in range(ROWS)]
            chosen = jnp.concatenate([anc_ref[step, pl.ds(i, 1), :] for i in who], axis=0)
            blocks = [chosen[:, k * LANES : (k + 1) * LANES] for k in range(chosen.shape[1] // LANES)]
            count = column([count_ref[step, i] for i in who])
            shift = column([base - first_ref[step, i] for i in who])
            sources = []
            for o in range(s_dev // LANES):
                relative = o * LANES + lanes + shift
                own = lane_pick(list(enumerate(blocks)), jnp.clip(relative, 0, chosen.shape[1] - 1))
                sources.append(
                    jnp.where(
                        relative < 0,
                        relative + margin,
                        jnp.where(relative < count, margin + own, margin + s_dev + relative - count),
                    )
                )
            source = jnp.concatenate(sources, axis=1)
            src_ref[step] = source
            src_t_ref[step] = source.T
            edges = [blocks[k] for k in range(margin // LANES)]
            for o in range(margin // LANES):
                edges.append(lane_pick(list(enumerate(blocks)), count - margin + o * LANES + lanes))
            edge = jnp.concatenate(edges, axis=1)
            edge_ref[step] = edge
            edge_t_ref[step] = edge.T
    loading_t_ref, wanted_ref = outs[4 * len(batches) :]
    loading_t_ref[...] = loading_ref[...].astype(F32).T.astype(BF16)
    rows = yields_ref[...]
    rows = jnp.concatenate([rows, jnp.zeros((ROWS - STEPS, rows.shape[1]), F32)], axis=0)
    wanted_ref[...] = rows.T


def one_hot(index, columns):
    index = index.astype(jnp.int16)
    lanes = lax.broadcasted_iota(jnp.int16, (index.shape[0], columns), 1)
    return jnp.where(index == lanes, BF16(1), BF16(0))


def send_edges(batch, margin, cloud_at, vol, edge, edge_t, low_ref, high_ref):
    s_dev = vol.shape[1]
    blocks = [(k, vol[:, k * LANES : (k + 1) * LANES]) for k in range(s_dev // LANES)]
    width = low_ref.shape[1]
    for out, start in ((low_ref, 0), (high_ref, margin)):
        picked = [
            lane_pick(blocks, edge[:, start + o * LANES : start + (o + 1) * LANES])
            for o in range(margin // LANES)
        ]
        picked.append(jnp.zeros((ROWS, width - margin), F32))
        flat = jnp.concatenate(picked, axis=1)
        flat = jnp.concatenate([flat, jnp.zeros((PAD - ROWS, width), F32)], axis=0)
        out[pl.ds(batch * margin, PAD), :] = flat.astype(BF16)
    for b in range(batch):
        rows = jnp.dot(
            one_hot(edge_t[:, b : b + 1], s_dev), cloud_at(b), preferred_element_type=F32
        ).astype(BF16)
        low_ref[pl.ds(b * margin, margin), :] = rows[:margin]
        high_ref[pl.ds(b * margin, margin), :] = rows[margin:]


def fetch_kernel(batch, first_place, margin, vol_rows, recv_slots, meta_ref, states_ref, vols_ref,
                 edge_ref, edge_t_ref, *rest):
    recv = rest[: len(recv_slots)]
    cloud_ref, vol_ref, low_ref, high_ref, table, sems = rest[-6:]
    p_dev, s_dev, _ = states_ref.shape
    for b in range(batch):
        place = meta_ref[1, first_place + b]

        @pl.when(place < p_dev)
        def _(b=b, place=place):
            pltpu.make_async_copy(
                states_ref.at[jnp.minimum(place, p_dev - 1)], cloud_ref.at[b], sems.at[b]
            ).start()

        for ref, codes in zip(recv, recv_slots):
            for k, code in enumerate(codes):

                @pl.when(place == code)
                def _(b=b, ref=ref, k=k):
                    pltpu.make_async_copy(
                        ref.at[pl.ds(k * s_dev, s_dev)], cloud_ref.at[b], sems.at[b]
                    ).start()

    table[...] = jnp.zeros(table.shape, F32)
    table[pl.ds(0, p_dev), :] = vols_ref[...].astype(F32)
    for ref, codes in zip(recv, recv_slots):
        tail = -(-len(codes) * vol_rows // PAD) * PAD
        rows = ref[pl.ds(len(codes) * s_dev, tail), :].astype(F32)
        for k, code in enumerate(codes):
            pieces = [rows[k * vol_rows + r : k * vol_rows + r + 1] for r in range(vol_rows)]
            table[pl.ds(code, 1), :] = jnp.concatenate(pieces, axis=1)
    vol = jnp.concatenate(
        [table[pl.ds(meta_ref[1, first_place + b % batch], 1), :] for b in range(ROWS)], axis=0
    )
    vol_ref[...] = vol
    for b in range(batch):
        pltpu.make_async_copy(states_ref.at[0], cloud_ref.at[b], sems.at[b]).wait()
    send_edges(batch, margin, lambda b: cloud_ref[b], vol, edge_ref[0], edge_t_ref[0], low_ref, high_ref)


def matrix_kernel(p_dev, meta_ref, transition_ref, moved_ref, out_ref, sems):
    for b in range(p_dev):
        place = meta_ref[1, b]

        @pl.when(place < p_dev)
        def _(b=b, place=place):
            pltpu.make_async_copy(
                transition_ref.at[jnp.minimum(place, p_dev - 1)], out_ref.at[b], sems.at[b]
            ).start()

        @pl.when(place >= p_dev)
        def _(b=b, place=place):
            pltpu.make_async_copy(
                moved_ref.at[jnp.maximum(place - p_dev, 0)], out_ref.at[b], sems.at[b]
            ).start()

    for b in range(p_dev):
        pltpu.make_async_copy(transition_ref.at[0], out_ref.at[b], sems.at[b]).wait()


def own_kernel(batch, step, margin, src_t_ref, cloud_ref, out_ref):
    s_dev = cloud_ref.shape[1]
    for b in range(batch):
        index = src_t_ref[step][:, b : b + 1] - margin
        out_ref[b] = jnp.dot(
            one_hot(index, s_dev), cloud_ref[b], preferred_element_type=F32
        ).astype(BF16)


def step_kernel(batch, first_place, step, margin, merge, cols_ref, own_ref, low_ref, high_ref, vol_ref,
                src_ref, src_t_ref, edge_ref, edge_t_ref, matrix_ref, noise_ref, vnoise_ref,
                loading_ref, wanted_ref, *rest):
    last = step == STEPS - 1
    s_dev = vol_ref.shape[1]
    rest = list(rest)
    stat_in = rest.pop(0) if step else None
    if last:
        meta_ref = rest.pop(0)
        if merge:
            _, vol_before, stat_before = rest[:3]
            rest = rest[3:]
        final_ref, vol_out, stat_ref, cloud_out, sems = rest
    else:
        cloud_out, vol_out, stat_ref, low_out, high_out = rest
    source = src_ref[step]
    vol = vol_ref[...]
    blocks = [(k, vol[:, k * LANES : (k + 1) * LANES]) for k in range(s_dev // LANES)]

    def edge_vols(ref):
        return ref[pl.ds(batch * margin, PAD), :].astype(F32)[:ROWS]

    low_v, high_v = edge_vols(low_ref), edge_vols(high_ref)
    picked = []
    for o in range(s_dev // LANES):
        index = source[:, o * LANES : (o + 1) * LANES]
        own = lane_pick(blocks, jnp.clip(index - margin, 0, s_dev - 1))
        if o < margin // LANES:
            low = [(k, low_v[:, k * LANES : (k + 1) * LANES]) for k in range(margin // LANES)]
            own = jnp.where(index < margin, lane_pick(low, index), own)
        if o >= (s_dev - margin) // LANES:
            high = [(k, high_v[:, k * LANES : (k + 1) * LANES]) for k in range(margin // LANES)]
            above = jnp.clip(index - margin - s_dev, 0, margin - 1)
            own = jnp.where(index >= margin + s_dev, lane_pick(high, above), own)
        picked.append(own)
    picked = jnp.concatenate(picked, axis=1)

    def param(k):
        return cols_ref[k][:, :1]

    center, persist, spread = param(0), param(1), param(2)
    h = center + persist * (picked - center) + spread * vnoise_ref[pl.ds(step, 1), :]
    scale_t = jnp.exp(0.5 * h).T
    vol_new = h.astype(BF16).astype(F32)
    if not last:
        vol_out[...] = vol_new

    wanted = wanted_ref[:, step : step + 1]
    tile = s_dev // 2
    squares = []
    for b in range(batch):
        row = []
        for r in range(2):
            span = pl.ds(r * tile, tile)
            index = src_t_ref[step, span, :][:, b : b + 1]
            own = own_ref[b, span, :]
            if r == 0:
                patch = jnp.dot(
                    one_hot(index[:margin], margin),
                    low_ref[pl.ds(b * margin, margin), :],
                    preferred_element_type=F32,
                )
                cloud = jnp.concatenate(
                    [(own[:margin].astype(F32) + patch).astype(BF16), own[margin:]], axis=0
                )
            else:
                patch = jnp.dot(
                    one_hot(index[tile - margin :] - (margin + s_dev), margin),
                    high_ref[pl.ds(b * margin, margin), :],
                    preferred_element_type=F32,
                )
                cloud = jnp.concatenate(
                    [own[: tile - margin], (own[tile - margin :].astype(F32) + patch).astype(BF16)],
                    axis=0,
                )
            drift = jnp.dot(cloud, matrix_ref[first_place + b], preferred_element_type=F32)
            noise = noise_ref[step, span, :].astype(F32)
            cloud = (drift + scale_t[r * tile : (r + 1) * tile, b : b + 1] * noise).astype(BF16)
            cloud_out[b, span, :] = cloud
            predicted = lax.dot_general(
                loading_ref[...], cloud, (((1,), (1,)), ((), ())), preferred_element_type=F32
            )
            misfit = wanted - predicted
            row.append(jnp.sum(misfit * misfit, axis=0, keepdims=True))
        squares.append(jnp.concatenate(row, axis=1))
        if last:
            pltpu.make_async_copy(
                cloud_out.at[b], final_ref.at[meta_ref[0, first_place + b]], sems.at[b]
            ).start()
    if not last:
        send_edges(
            batch, margin, lambda b: cloud_out[b], vol_new, edge_ref[step + 1], edge_t_ref[step + 1],
            low_out, high_out,
        )
    squares += [squares[0]] * (ROWS - batch)
    square = jnp.concatenate(squares, axis=0)
    precision = param(3)
    maturities = wanted_ref.shape[0]
    weights = -0.5 * precision * square + 0.5 * maturities * jnp.log(precision)
    peak = jnp.max(weights, axis=1, keepdims=True)
    mass = jnp.sum(jnp.exp(weights - peak), axis=1, keepdims=True)
    lane = lax.broadcasted_iota(I32, (ROWS, LANES), 1)
    before = [stat_in[0], stat_in[1]] if step else [jnp.zeros((ROWS, LANES), F32)] * 2
    stats = [jnp.where(lane == step, new, old) for new, old in zip((peak, mass), before)]
    if last:
        rows = lax.broadcasted_iota(I32, (ROWS, 1), 0)
        vol_all = vol_before[...].astype(F32) if merge else jnp.zeros(vol_new.shape, F32)
        placed = [stat_before[0], stat_before[1]] if merge else [jnp.zeros((ROWS, LANES), F32)] * 2
        for b in range(batch):
            here = rows == meta_ref[0, first_place + b]
            vol_all = jnp.where(here, vol_new[b : b + 1], vol_all)
            placed = [jnp.where(here, new[b : b + 1], old) for new, old in zip(stats, placed)]
        vol_out[...] = vol_all.astype(BF16)
        stats = placed
    stat_ref[0] = stats[0]
    stat_ref[1] = stats[1]
    if last:
        for b in range(batch):
            pltpu.make_async_copy(cloud_out.at[b], final_ref.at[0], sems.at[b]).wait()


def join_kernel(finish, whole_rows, *refs):
    mine_ref, others, (out_ref,) = refs[0], refs[1:-1], refs[-1:]
    if finish:
        prior_ref, others = others[0], others[1:]
    peak, mass = mine_ref[0], mine_ref[1]
    for other in others:
        other_peak = other[0]
        top = jnp.maximum(peak, other_peak)
        mass = mass * jnp.exp(peak - top) + other[1] * jnp.exp(other_peak - top)
        peak = top
    if not finish:
        out_ref[0] = peak
        out_ref[1] = mass
        return
    lane = lax.broadcasted_iota(I32, (ROWS, LANES), 1)
    gained = peak + jnp.log(jnp.where(lane < STEPS, mass, 1.0)) - math.log(whole_rows)
    gained = jnp.sum(jnp.where(lane < STEPS, gained, 0.0), axis=1, keepdims=True)
    total = jnp.broadcast_to(prior_ref[:, :1] + gained, (ROWS, LANES))
    out_ref[...] = total.T[:1, :]


def join(stats, others, whole_rows, prior=None):
    operands = [stats] + ([] if prior is None else [prior]) + list(others)
    shape = stats.shape if prior is None else (1, ROWS)
    return call(
        functools.partial(join_kernel, prior is not None, whole_rows),
        jax.ShapeDtypeStruct(shape, F32),
        [vmem()] * len(operands),
        vmem(),
        "join",
        nbytes=1 << 14,
    )(*operands)


def shifts(count):
    forward = [(i, i + 1) for i in range(count - 1)]
    return forward, [(target, source) for source, target in forward]


def doubling(count):
    distance = 1
    while distance < count:
        yield distance, [(i, i ^ distance) for i in range(count)]
        distance *= 2


def prefix_counts(number):
    count, here = lax.axis_size("state"), lax.axis_index("state")
    if count & (count - 1):
        every = lax.all_gather(number, "state")
        before = jnp.arange(count) < here
        return jnp.sum(jnp.where(before[:, None, None], every, 0), axis=0)
    before, total = jnp.zeros_like(number), number
    for distance, pairs in doubling(count):
        other = lax.ppermute(total, "state", pairs)
        before = before + jnp.where((here & distance) != 0, other, 0)
        total = total + other
    return before


def combined_mass(stats, prior, whole_rows):
    count = lax.axis_size("state")
    if count & (count - 1):
        every = lax.all_gather(stats, "state")
        return join(every[0], [every[k] for k in range(1, count)], whole_rows, prior)
    rounds = [pairs for _, pairs in doubling(count)]
    if not rounds:
        return join(stats, [], whole_rows, prior)
    for k, pairs in enumerate(rounds):
        other = lax.ppermute(stats, "state", pairs)
        stats = join(stats, [other], whole_rows, prior if k == len(rounds) - 1 else None)
    return stats


def local(
    states,
    log_vol,
    transition,
    loading,
    yields,
    state_noise,
    vol_noise,
    vol_mean,
    vol_persist,
    vol_scale,
    obs_prec,
    prior_loglik,
    ancestors,
    counts,
    local_anc,
):
    p_dev, s_dev, width = states.shape
    maturities = loading.shape[1]
    groups, shards = lax.axis_size("theta"), lax.axis_size("state")
    group, shard = lax.axis_index("theta"), lax.axis_index("state")
    half = p_dev // 2
    margin = s_dev // 4
    batch = p_dev // 2
    batches = [tuple(range(q * batch, (q + 1) * batch)) for q in range(p_dev // batch)]
    early = half // 2
    chunks = [tuple(range(0, early)), tuple(range(early, half))]
    vol_rows = s_dev // width
    part_rows = half * width // shards
    where = jnp.stack([group, shard]).astype(I32)

    tail = -(-early * vol_rows // PAD) * PAD
    part_shape = jax.ShapeDtypeStruct((part_rows, width), BF16)
    chunk_shape = jax.ShapeDtypeStruct((early * s_dev + tail, width), BF16)
    cols_shape = jax.ShapeDtypeStruct((len(batches), 4, ROWS, LANES), F32)
    planned = call(
        functools.partial(plan_kernel, groups, shards, chunks, batches, part_rows, vol_rows),
        [part_shape] * 2
        + [chunk_shape] * 4
        + [
            jax.ShapeDtypeStruct((3, p_dev), I32),
            cols_shape,
            jax.ShapeDtypeStruct((ROWS, LANES), F32),
        ],
        [smem()] * 7 + [hbm(), vmem(), hbm()],
        [anywhere()] * 6 + [smem(), vmem(), vmem()],
        "plan",
        [
            pltpu.SMEM((2, half), I32),
            pltpu.VMEM((p_dev, s_dev), F32),
            pltpu.VMEM((2, 2, tail, width), BF16),
            pltpu.SemaphoreType.DMA((2, part_rows // math.gcd(part_rows, width))),
            pltpu.SemaphoreType.DMA((2, 2, early + 1)),
        ],
        nbytes=4 * half * s_dev * width * 2,
    )(where, ancestors, vol_mean, vol_persist, vol_scale, obs_prec, prior_loglik, states, log_vol, transition)
    parts, packed, (meta, cols, prior) = planned[:2], planned[2:6], planned[6:]

    sides = shifts(groups)
    part_in = jnp.stack([lax.ppermute(part, "theta", pairs) for part, pairs in zip(parts, sides)])
    moved = lax.all_gather(part_in, "state", axis=1, tiled=True).reshape(2 * half, width, width)
    chunk_in = [
        [lax.ppermute(packed[2 * c + side], "theta", sides[side]) for side in range(2)]
        for c in range(len(chunks))
    ]

    number = counts[:, :, 0]
    first = prefix_counts(number)
    index_shapes = [
        jax.ShapeDtypeStruct((STEPS, ROWS, s_dev), I32),
        jax.ShapeDtypeStruct((STEPS, s_dev, ROWS), I32),
        jax.ShapeDtypeStruct((STEPS, ROWS, 2 * margin), I32),
        jax.ShapeDtypeStruct((STEPS, 2 * margin, ROWS), I32),
    ] * len(batches) + [
        jax.ShapeDtypeStruct((maturities, width), BF16),
        jax.ShapeDtypeStruct((maturities, ROWS), F32),
    ]
    indices = call(
        functools.partial(index_kernel, batches, s_dev, margin),
        index_shapes,
        [smem()] * 4 + [vmem()] * 3,
        [vmem()] * len(index_shapes),
        "indices",
        nbytes=1 << 18,
    )(meta, number, first, where, local_anc, loading, yields)
    loading_t, wanted = indices[-2:]

    matrices = call(
        functools.partial(matrix_kernel, p_dev),
        jax.ShapeDtypeStruct((p_dev, width, width), BF16),
        [smem(), hbm(), hbm()],
        vmem(),
        "matrices",
        [pltpu.SemaphoreType.DMA((p_dev,))],
        nbytes=p_dev * width * width * 4,
    )(meta, transition, moved)

    up, down = shifts(shards)
    edge_shape = jax.ShapeDtypeStruct((batch * margin + PAD, width), BF16)
    cloud_shape = jax.ShapeDtypeStruct((batch, s_dev, width), BF16)
    vol_shape = jax.ShapeDtypeStruct((ROWS, s_dev), F32)
    stat_shape = jax.ShapeDtypeStruct((2, ROWS, LANES), F32)
    before = None
    follow = []
    for q in range(len(batches)):
        src, src_t, edge, edge_t = indices[4 * q : 4 * q + 4]
        recv, recv_slots = [], []
        for c in range(q + 1):
            for side in range(2):
                recv.append(chunk_in[c][side])
                recv_slots.append(tuple(p_dev + side * half + k for k in chunks[c]))
        cloud, vol, low, high = call(
            functools.partial(fetch_kernel, batch, q * batch, margin, vol_rows, tuple(recv_slots)),
            [cloud_shape, vol_shape, edge_shape, edge_shape],
            [smem(), hbm()] + [vmem()] * (3 + len(recv) + len(follow)),
            [vmem()] * 4,
            "fetch",
            [pltpu.VMEM((2 * p_dev, s_dev), F32), pltpu.SemaphoreType.DMA((batch,))],
            flops=2 * batch * 2 * margin * s_dev * width,
            nbytes=2 * batch * s_dev * width * 2,
        )(meta, states, log_vol, edge, edge_t, *recv, *follow)
        stat = None
        for step in range(STEPS):
            last = step == STEPS - 1
            low_in = lax.ppermute(high, "state", up)
            high_in = lax.ppermute(low, "state", down)
            own = call(
                functools.partial(own_kernel, batch, step, margin),
                cloud_shape,
                [vmem(), vmem()],
                vmem(),
                "own_rows",
                flops=2 * batch * s_dev * s_dev * width,
                nbytes=batch * s_dev * width * 4,
            )(src_t, cloud)
            operands = [
                cols[q], own, low_in, high_in, vol, src, src_t, edge, edge_t, matrices,
                state_noise, vol_noise, loading_t, wanted,
            ]
            specs = [vmem()] * len(operands)
            if step:
                operands.append(stat)
                specs.append(vmem())
            aliases, scratch = None, []
            if last:
                operands.append(meta)
                specs.append(smem())
                out_shape = [
                    jax.ShapeDtypeStruct(states.shape, BF16),
                    jax.ShapeDtypeStruct(log_vol.shape, BF16),
                    stat_shape,
                ]
                out_specs = [hbm(), vmem(), vmem()]
                scratch = [
                    pltpu.VMEM((batch, s_dev, width), BF16),
                    pltpu.SemaphoreType.DMA((batch,)),
                ]
                if before is not None:
                    aliases = {len(operands): 0}
                    operands += before
                    specs += [hbm(), vmem(), vmem()]
            else:
                out_shape = [cloud_shape, vol_shape, stat_shape, edge_shape, edge_shape]
                out_specs = [vmem()] * 5
            results = call(
                functools.partial(step_kernel, batch, q * batch, step, margin, before is not None),
                out_shape,
                specs,
                out_specs,
                "step",
                scratch,
                flops=2 * batch * s_dev * width * (width + maturities + margin),
                nbytes=batch * s_dev * width * 8,
                aliases=aliases,
            )(*operands)
            if last:
                before = list(results)
            else:
                cloud, vol, stat, low, high = results
                follow = [stat]
    final, vols, stats = before
    total = combined_mass(stats, prior, s_dev * shards)
    return (final, vols, total.reshape(p_dev))


def solution(mesh):
    placed = (
        P("theta", "state", None),
        P("theta", "state"),
        P("theta", None, None),
        P(),
        P(),
        P(None, "state", None),
        P(None, "state"),
        P(),
        P(),
        P(),
        P(),
        P(),
        P(),
        P(None, "theta", "state"),
        P(None, "theta", "state"),
    )
    return jax.shard_map(
        local,
        mesh=mesh,
        in_specs=placed,
        out_specs=(P("theta", "state", None), P("theta", "state"), P("theta")),
        check_vma=False,
    )
```

```python
import functools
import math

import jax
import jax.numpy as jnp
from jax import lax
from jax.experimental import pallas as pl
from jax.experimental.pallas import tpu as pltpu
from jax.sharding import PartitionSpec as P

STEPS = 3
LANES = 128
ROWS = 8
PAD = 16
VLIMIT = 8 * 1024 * 1024
PACK_LIMIT = 64 * 1024 * 1024

VM = pltpu.VMEM
SM = pltpu.SMEM
F32 = jnp.float32
BF16 = jnp.bfloat16
I32 = jnp.int32


def vmem():
    return pl.BlockSpec(memory_space=pltpu.VMEM)


def smem():
    return pl.BlockSpec(memory_space=pltpu.SMEM)


def anywhere():
    return pl.BlockSpec(memory_space=pl.ANY)


def hbm():
    return pl.BlockSpec(memory_space=pltpu.HBM)


def call(kernel, out_shape, in_specs, out_specs, name, scratch=(), flops=0, nbytes=0, aliases=None,
         limit=VLIMIT):
    return pl.pallas_call(
        kernel,
        out_shape=out_shape,
        in_specs=in_specs,
        out_specs=out_specs,
        scratch_shapes=list(scratch),
        input_output_aliases=aliases or {},
        compiler_params=pltpu.CompilerParams(vmem_limit_bytes=limit),
        cost_estimate=pl.CostEstimate(flops=flops, bytes_accessed=nbytes, transcendentals=0),
        name=name,
    )


def pack_kernel(groups, chunks, ways, vol_rows, anc_hbm, vols_hbm, states_ref, transition_ref, *rest):
    part_outs, rest = rest[:2], rest[2:]
    chunk_outs, rest = rest[: 2 * len(chunks)], rest[2 * len(chunks) :]
    anc_ref, names, vols_ref, table, tails, load_sems, part_sems, sems = rest
    p_dev, s_dev, width = states_ref.shape
    half = p_dev // 2
    per_part = half // ways
    group, shard = lax.axis_index("theta"), lax.axis_index("state")
    load_anc = pltpu.make_async_copy(anc_hbm, anc_ref, load_sems.at[0])
    load_vols = pltpu.make_async_copy(vols_hbm, vols_ref, load_sems.at[1])
    load_anc.start()
    load_vols.start()
    load_anc.wait()

    odd = lax.rem(group, 2)
    for side in range(2):
        other = group + (1 - 2 * odd if side == 0 else 2 * odd - 1)
        valid = (other >= 0) & (other < groups)
        other = jnp.clip(other, 0, groups - 1)
        for k in range(half):
            names[side, k] = 0
        rank = jnp.int32(0)
        for i in range(p_dev):
            a = anc_ref[other * p_dev + i]
            hit = valid & (lax.div(a, p_dev) == group) & (rank < half)

            @pl.when(hit)
            def _(side=side, rank=rank, a=a):
                names[side, rank] = lax.rem(a, p_dev)

            rank = rank + hit.astype(I32)

    copies = []
    for side, out in enumerate(part_outs):
        for k in range(per_part):
            copy = pltpu.make_async_copy(
                transition_ref.at[names[side, lax.rem(shard, ways) * per_part + k]],
                out.at[pl.ds(k * width, width)],
                part_sems.at[side, k],
            )
            copy.start()
            copies.append(copy)
    for c, chunk in enumerate(chunks):
        for side in range(2):
            for k, slot in enumerate(chunk):
                copy = pltpu.make_async_copy(
                    states_ref.at[names[side, slot]],
                    chunk_outs[2 * c + side].at[pl.ds(k * s_dev, s_dev)],
                    sems.at[c, side, k],
                )
                copy.start()
                copies.append(copy)

    load_vols.wait()
    table[...] = vols_ref[...].astype(F32)
    for c, chunk in enumerate(chunks):
        for side in range(2):
            pieces = []
            for slot in chunk:
                row = table[pl.ds(names[side, slot], 1), :]
                pieces += [row[:, k * width : (k + 1) * width] for k in range(vol_rows)]
            pieces.append(jnp.zeros((tails.shape[2] - len(pieces), width), F32))
            tails[c, side] = jnp.concatenate(pieces, axis=0).astype(BF16)
            copy = pltpu.make_async_copy(
                tails.at[c, side],
                chunk_outs[2 * c + side].at[pl.ds(len(chunk) * s_dev, tails.shape[2])],
                sems.at[c, side, len(chunk)],
            )
            copy.start()
            copies.append(copy)
    for copy in copies:
        copy.wait()


def plan_kernel(p_dev, early, batches, anc_ref, *rest):
    tables, (meta_ref, cols_ref, prior_ref) = rest[:5], rest[5:]
    half = p_dev // 2
    group = lax.axis_index("theta")
    even = lax.rem(group, 2) == 0
    low_side, high_side = jnp.where(even, half, 0), jnp.where(even, 0, half)
    rank_low, rank_high = jnp.int32(0), jnp.int32(0)
    front, back = jnp.int32(0), jnp.int32(p_dev - 1)
    for i in range(p_dev):
        a = anc_ref[group * p_dev + i]
        offset = lax.div(a, p_dev) - group
        low, high = offset == -1, offset == 1
        late = (low & (rank_low >= early)) | (high & (rank_high >= early))
        moved = p_dev + jnp.where(low, low_side + rank_low, high_side + rank_high)
        position = jnp.where(late, back, front)
        meta_ref[0, position] = i
        meta_ref[1, position] = jnp.where(low | high, moved, lax.rem(a, p_dev))
        meta_ref[2, position] = a
        front = front + jnp.where(late, 0, 1)
        back = back - jnp.where(late, 1, 0)
        rank_low = rank_low + low.astype(I32)
        rank_high = rank_high + high.astype(I32)
    for q, batch in enumerate(batches):
        for k in range(4):
            value = column([tables[k][meta_ref[2, batch[b % len(batch)]]] for b in range(ROWS)])
            cols_ref[q, k] = jnp.broadcast_to(value, (ROWS, LANES))
    prior = column([tables[4][anc_ref[group * p_dev + i]] for i in range(p_dev)])
    prior_ref[...] = jnp.broadcast_to(prior, (ROWS, LANES))


def lane_pick(blocks, index):
    low = index & (LANES - 1)
    high = index >> 7
    out = None
    for k, block in blocks:
        got = jnp.take_along_axis(block, low, axis=1, mode="promise_in_bounds")
        out = got if out is None else jnp.where(high == k, got, out)
    return out


def column(scalars):
    rows = lax.broadcasted_iota(I32, (ROWS, 1), 0)
    out = jnp.zeros((ROWS, 1), scalars[0].dtype)
    for b, scalar in enumerate(scalars):
        out = jnp.where(rows == b, scalar, out)
    return out


def index_kernel(batches, s_dev, margin, meta_ref, count_ref, first_ref, anc_ref,
                 loading_ref, yields_ref, *outs):
    shard = lax.axis_index("state")
    base = shard * s_dev
    even = lax.rem(shard, 2) == 0
    lanes = lax.broadcasted_iota(I32, (ROWS, LANES), 1)
    for q, batch in enumerate(batches):
        src_ref, src_t_ref, edge_ref, edge_t_ref = outs[4 * q : 4 * q + 4]
        for step in range(STEPS):
            who = [meta_ref[0, batch[b % len(batch)]] for b in range(ROWS)]
            chosen = jnp.concatenate([anc_ref[step, pl.ds(i, 1), :] for i in who], axis=0)
            blocks = [chosen[:, k * LANES : (k + 1) * LANES] for k in range(chosen.shape[1] // LANES)]
            count = column([count_ref[step, i] for i in who])
            shift = column([base - first_ref[step, i] for i in who])
            sources = []
            for o in range(s_dev // LANES):
                relative = o * LANES + lanes + shift
                own = lane_pick(list(enumerate(blocks)), jnp.clip(relative, 0, chosen.shape[1] - 1))
                sources.append(
                    jnp.where(
                        relative < 0,
                        relative + margin,
                        jnp.where(relative < count, margin + own, margin + s_dev + relative - count),
                    )
                )
            source = jnp.concatenate(sources, axis=1)
            src_ref[step] = source
            src_t_ref[step] = source.T
            head = jnp.concatenate(blocks[: margin // LANES], axis=1)
            tail = [
                lane_pick(list(enumerate(blocks)), count - margin + o * LANES + lanes)
                for o in range(margin // LANES)
            ]
            tail = jnp.concatenate(tail, axis=1)
            edge = jnp.concatenate([jnp.where(even, tail, head), jnp.where(even, head, tail)], axis=1)
            edge_ref[step] = edge
            edge_t_ref[step] = edge.T
    loading_t_ref, wanted_ref = outs[4 * len(batches) :]
    loading_t_ref[...] = loading_ref[...].astype(F32).T.astype(BF16)
    rows = yields_ref[...]
    rows = jnp.concatenate([rows, jnp.zeros((ROWS - STEPS, rows.shape[1]), F32)], axis=0)
    wanted_ref[...] = rows.T


def one_hot(index, columns):
    index = index.astype(jnp.int16)
    lanes = lax.broadcasted_iota(jnp.int16, (index.shape[0], columns), 1)
    return jnp.where(index == lanes, BF16(1), BF16(0))


def send_edges(batch, margin, cloud_at, vol, edge, edge_t, pair_ref, other_ref):
    s_dev = vol.shape[1]
    blocks = [(k, vol[:, k * LANES : (k + 1) * LANES]) for k in range(s_dev // LANES)]
    width = pair_ref.shape[1]
    for out, start in ((pair_ref, 0), (other_ref, margin)):
        picked = [
            lane_pick(blocks, edge[:, start + o * LANES : start + (o + 1) * LANES])
            for o in range(margin // LANES)
        ]
        picked.append(jnp.zeros((ROWS, width - margin), F32))
        flat = jnp.concatenate(picked, axis=1)
        flat = jnp.concatenate([flat, jnp.zeros((PAD - ROWS, width), F32)], axis=0)
        out[pl.ds(batch * margin, PAD), :] = flat.astype(BF16)
    for b in range(batch):
        rows = jnp.dot(
            one_hot(edge_t[:, b : b + 1], s_dev), cloud_at(b), preferred_element_type=F32
        ).astype(BF16)
        pair_ref[pl.ds(b * margin, margin), :] = rows[:margin]
        other_ref[pl.ds(b * margin, margin), :] = rows[margin:]


def fetch_kernel(batch, first_place, margin, vol_rows, recv_slots, meta_ref, states_ref, vols_ref,
                 edge_ref, edge_t_ref, *rest):
    recv = rest[: len(recv_slots)]
    cloud_ref, vol_ref, pair_ref, other_ref, table, sems = rest[-6:]
    p_dev, s_dev, _ = states_ref.shape
    for b in range(batch):
        place = meta_ref[1, first_place + b]

        @pl.when(place < p_dev)
        def _(b=b, place=place):
            pltpu.make_async_copy(
                states_ref.at[jnp.minimum(place, p_dev - 1)], cloud_ref.at[b], sems.at[b]
            ).start()

        for ref, codes in zip(recv, recv_slots):
            for k, code in enumerate(codes):

                @pl.when(place == code)
                def _(b=b, ref=ref, k=k):
                    pltpu.make_async_copy(
                        ref.at[pl.ds(k * s_dev, s_dev)], cloud_ref.at[b], sems.at[b]
                    ).start()

    table[...] = jnp.zeros(table.shape, F32)
    table[pl.ds(0, p_dev), :] = vols_ref[...].astype(F32)
    for ref, codes in zip(recv, recv_slots):
        tail = -(-len(codes) * vol_rows // PAD) * PAD
        rows = ref[pl.ds(len(codes) * s_dev, tail), :].astype(F32)
        for k, code in enumerate(codes):
            pieces = [rows[k * vol_rows + r : k * vol_rows + r + 1] for r in range(vol_rows)]
            table[pl.ds(code, 1), :] = jnp.concatenate(pieces, axis=1)
    vol = jnp.concatenate(
        [table[pl.ds(meta_ref[1, first_place + b % batch], 1), :] for b in range(ROWS)], axis=0
    )
    vol_ref[...] = vol
    for b in range(batch):
        pltpu.make_async_copy(states_ref.at[0], cloud_ref.at[b], sems.at[b]).wait()
    send_edges(batch, margin, lambda b: cloud_ref[b], vol, edge_ref[0], edge_t_ref[0], pair_ref, other_ref)


def matrix_kernel(p_dev, ways, meta_ref, transition_ref, gathered_ref, out_ref, sems):
    half = p_dev // 2
    per_part = half // ways
    mine = lax.rem(lax.axis_index("state"), ways)
    for b in range(p_dev):
        place = meta_ref[1, b]

        @pl.when(place < p_dev)
        def _(b=b, place=place):
            pltpu.make_async_copy(
                transition_ref.at[jnp.minimum(place, p_dev - 1)], out_ref.at[b], sems.at[b]
            ).start()

        @pl.when(place >= p_dev)
        def _(b=b, place=place):
            moved = jnp.maximum(place - p_dev, 0)
            side, slot = lax.div(moved, half), lax.rem(moved, half)
            apart = lax.div(slot, per_part) ^ mine
            index, size, distance = jnp.int32(0), 1, ways // 2
            while distance:
                index = index + jnp.where((apart & distance) != 0, size, 0)
                size, distance = 2 * size, distance // 2
            at = (index * 2 + side) * per_part + lax.rem(slot, per_part)
            pltpu.make_async_copy(gathered_ref.at[at], out_ref.at[b], sems.at[b]).start()

    for b in range(p_dev):
        pltpu.make_async_copy(transition_ref.at[0], out_ref.at[b], sems.at[b]).wait()


def own_kernel(batch, step, margin, src_t_ref, cloud_ref, out_ref):
    s_dev = cloud_ref.shape[1]
    for b in range(batch):
        index = src_t_ref[step][:, b : b + 1] - margin
        out_ref[b] = jnp.dot(
            one_hot(index, s_dev), cloud_ref[b], preferred_element_type=F32
        ).astype(BF16)


def step_kernel(batch, first_place, step, margin, merge, cols_ref, own_ref, pair_ref, other_ref, vol_ref,
                src_ref, src_t_ref, edge_ref, edge_t_ref, matrix_ref, noise_ref, vnoise_ref,
                loading_ref, wanted_ref, *rest):
    last = step == STEPS - 1
    s_dev = vol_ref.shape[1]
    rest = list(rest)
    stat_in = rest.pop(0) if step else None
    if last:
        meta_ref = rest.pop(0)
        if merge:
            _, vol_before, stat_before = rest[:3]
            rest = rest[3:]
        final_ref, vol_out, stat_ref, cloud_out, sems = rest
    else:
        cloud_out, vol_out, stat_ref, pair_out, other_out = rest
    even = lax.rem(lax.axis_index("state"), 2) == 0
    source = src_ref[step]
    vol = vol_ref[...]
    blocks = [(k, vol[:, k * LANES : (k + 1) * LANES]) for k in range(s_dev // LANES)]

    def edge_vols(ref):
        return ref[pl.ds(batch * margin, PAD), :].astype(F32)[:ROWS]

    pair_v, other_v = edge_vols(pair_ref), edge_vols(other_ref)
    low_v, high_v = jnp.where(even, other_v, pair_v), jnp.where(even, pair_v, other_v)
    picked = []
    for o in range(s_dev // LANES):
        index = source[:, o * LANES : (o + 1) * LANES]
        own = lane_pick(blocks, jnp.clip(index - margin, 0, s_dev - 1))
        if o < margin // LANES:
            low = [(k, low_v[:, k * LANES : (k + 1) * LANES]) for k in range(margin // LANES)]
            own = jnp.where(index < margin, lane_pick(low, index), own)
        if o >= (s_dev - margin) // LANES:
            high = [(k, high_v[:, k * LANES : (k + 1) * LANES]) for k in range(margin // LANES)]
            above = jnp.clip(index - margin - s_dev, 0, margin - 1)
            own = jnp.where(index >= margin + s_dev, lane_pick(high, above), own)
        picked.append(own)
    picked = jnp.concatenate(picked, axis=1)

    def param(k):
        return cols_ref[k][:, :1]

    center, persist, spread = param(0), param(1), param(2)
    h = center + persist * (picked - center) + spread * vnoise_ref[pl.ds(step, 1), :]
    scale_t = jnp.exp(0.5 * h).T
    vol_new = h.astype(BF16).astype(F32)
    if not last:
        vol_out[...] = vol_new

    wanted = wanted_ref[:, step : step + 1]
    tile = s_dev // 2
    squares = []
    for b in range(batch):
        row = []
        for r in range(2):
            span = pl.ds(r * tile, tile)
            index = src_t_ref[step, span, :][:, b : b + 1]
            own = own_ref[b, span, :]
            pair, other = pair_ref[pl.ds(b * margin, margin), :], other_ref[pl.ds(b * margin, margin), :]
            if r == 0:
                patch = jnp.dot(
                    one_hot(index[:margin], margin),
                    jnp.where(even, other, pair),
                    preferred_element_type=F32,
                )
                cloud = jnp.concatenate(
                    [(own[:margin].astype(F32) + patch).astype(BF16), own[margin:]], axis=0
                )
            else:
                patch = jnp.dot(
                    one_hot(index[tile - margin :] - (margin + s_dev), margin),
                    jnp.where(even, pair, other),
                    preferred_element_type=F32,
                )
                cloud = jnp.concatenate(
                    [own[: tile - margin], (own[tile - margin :].astype(F32) + patch).astype(BF16)],
                    axis=0,
                )
            drift = jnp.dot(cloud, matrix_ref[first_place + b], preferred_element_type=F32)
            noise = noise_ref[step, span, :].astype(F32)
            cloud = (drift + scale_t[r * tile : (r + 1) * tile, b : b + 1] * noise).astype(BF16)
            cloud_out[b, span, :] = cloud
            predicted = lax.dot_general(
                loading_ref[...], cloud, (((1,), (1,)), ((), ())), preferred_element_type=F32
            )
            misfit = wanted - predicted
            row.append(jnp.sum(misfit * misfit, axis=0, keepdims=True))
        squares.append(jnp.concatenate(row, axis=1))
        if last:
            pltpu.make_async_copy(
                cloud_out.at[b], final_ref.at[meta_ref[0, first_place + b]], sems.at[b]
            ).start()
    if not last:
        send_edges(
            batch, margin, lambda b: cloud_out[b], vol_new, edge_ref[step + 1], edge_t_ref[step + 1],
            pair_out, other_out,
        )
    squares += [squares[0]] * (ROWS - batch)
    square = jnp.concatenate(squares, axis=0)
    precision = param(3)
    maturities = wanted_ref.shape[0]
    weights = -0.5 * precision * square + 0.5 * maturities * jnp.log(precision)
    peak = jnp.max(weights, axis=1, keepdims=True)
    mass = jnp.sum(jnp.exp(weights - peak), axis=1, keepdims=True)
    lane = lax.broadcasted_iota(I32, (ROWS, LANES), 1)
    before = [stat_in[0], stat_in[1]] if step else [jnp.zeros((ROWS, LANES), F32)] * 2
    stats = [jnp.where(lane == step, new, old) for new, old in zip((peak, mass), before)]
    if last:
        rows = lax.broadcasted_iota(I32, (ROWS, 1), 0)
        vol_all = vol_before[...].astype(F32) if merge else jnp.zeros(vol_new.shape, F32)
        placed = [stat_before[0], stat_before[1]] if merge else [jnp.zeros((ROWS, LANES), F32)] * 2
        for b in range(batch):
            here = rows == meta_ref[0, first_place + b]
            vol_all = jnp.where(here, vol_new[b : b + 1], vol_all)
            placed = [jnp.where(here, new[b : b + 1], old) for new, old in zip(stats, placed)]
        vol_out[...] = vol_all.astype(BF16)
        stats = placed
    stat_ref[0] = stats[0]
    stat_ref[1] = stats[1]
    if last:
        for b in range(batch):
            pltpu.make_async_copy(cloud_out.at[b], final_ref.at[0], sems.at[b]).wait()


def join_kernel(finish, whole_rows, *refs):
    mine_ref, others, (out_ref,) = refs[0], refs[1:-1], refs[-1:]
    if finish:
        prior_ref, others = others[0], others[1:]
    peak, mass = mine_ref[0], mine_ref[1]
    for other in others:
        other_peak = other[0]
        top = jnp.maximum(peak, other_peak)
        mass = mass * jnp.exp(peak - top) + other[1] * jnp.exp(other_peak - top)
        peak = top
    if not finish:
        out_ref[0] = peak
        out_ref[1] = mass
        return
    lane = lax.broadcasted_iota(I32, (ROWS, LANES), 1)
    gained = peak + jnp.log(jnp.where(lane < STEPS, mass, 1.0)) - math.log(whole_rows)
    gained = jnp.sum(jnp.where(lane < STEPS, gained, 0.0), axis=1, keepdims=True)
    total = jnp.broadcast_to(prior_ref[:, :1] + gained, (ROWS, LANES))
    out_ref[...] = total.T[:1, :]


def join(stats, others, whole_rows, prior=None):
    operands = [stats] + ([] if prior is None else [prior]) + list(others)
    shape = stats.shape if prior is None else (1, ROWS)
    return call(
        functools.partial(join_kernel, prior is not None, whole_rows),
        jax.ShapeDtypeStruct(shape, F32),
        [vmem()] * len(operands),
        vmem(),
        "join",
        nbytes=1 << 14,
    )(*operands)


def swaps(count):
    rounds = []
    for offset in (0, 1):
        partner = [(i - offset ^ 1) + offset for i in range(count)]
        rounds.append([(i, p if 0 <= p < count else i) for i, p in enumerate(partner)])
    return rounds


def doubling(count):
    distance = 1
    while distance < count:
        yield distance, [(i, i ^ distance) for i in range(count)]
        distance *= 2


def prefix_counts(number):
    count, here = lax.axis_size("state"), lax.axis_index("state")
    if count & (count - 1):
        every = lax.all_gather(number, "state")
        before = jnp.arange(count) < here
        return jnp.sum(jnp.where(before[:, None, None], every, 0), axis=0)
    before, total = jnp.zeros_like(number), number
    for distance, pairs in doubling(count):
        other = lax.ppermute(total, "state", pairs)
        before = before + jnp.where((here & distance) != 0, other, 0)
        total = total + other
    return before


def combined_mass(stats, prior, whole_rows):
    count = lax.axis_size("state")
    if count & (count - 1):
        every = lax.all_gather(stats, "state")
        return join(every[0], [every[k] for k in range(1, count)], whole_rows, prior)
    rounds = [pairs for _, pairs in doubling(count)]
    if not rounds:
        return join(stats, [], whole_rows, prior)
    for k, pairs in enumerate(rounds):
        other = lax.ppermute(stats, "state", pairs)
        stats = join(stats, [other], whole_rows, prior if k == len(rounds) - 1 else None)
    return stats


def local(
    states,
    log_vol,
    transition,
    loading,
    yields,
    state_noise,
    vol_noise,
    vol_mean,
    vol_persist,
    vol_scale,
    obs_prec,
    prior_loglik,
    ancestors,
    counts,
    local_anc,
):
    p_dev, s_dev, width = states.shape
    maturities = loading.shape[1]
    groups, shards = lax.axis_size("theta"), lax.axis_size("state")
    half = p_dev // 2
    margin = s_dev // 4
    batch = p_dev // 2
    batches = [tuple(range(q * batch, (q + 1) * batch)) for q in range(p_dev // batch)]
    early = half // 2
    chunks = [tuple(range(0, early)), tuple(range(early, half))]
    vol_rows = s_dev // width
    ways = next(w for w in (4, 2, 1) if half % w == 0 and shards % w == 0)
    per_part = half // ways

    tail = -(-early * vol_rows // PAD) * PAD
    part_shape = jax.ShapeDtypeStruct((per_part * width, width), BF16)
    chunk_shape = jax.ShapeDtypeStruct((early * s_dev + tail, width), BF16)
    packed = call(
        functools.partial(pack_kernel, groups, chunks, ways, vol_rows),
        [part_shape] * 2 + [chunk_shape] * 4,
        [anywhere()] * 4,
        [anywhere()] * 6,
        "pack",
        [
            pltpu.SMEM(ancestors.shape, I32),
            pltpu.SMEM((2, half), I32),
            pltpu.VMEM((p_dev, s_dev), BF16),
            pltpu.VMEM((p_dev, s_dev), F32),
            pltpu.VMEM((2, 2, tail, width), BF16),
            pltpu.SemaphoreType.DMA((2,)),
            pltpu.SemaphoreType.DMA((2, per_part)),
            pltpu.SemaphoreType.DMA((2, 2, early + 1)),
        ],
        nbytes=4 * half * s_dev * width * 2,
        limit=PACK_LIMIT,
    )(ancestors, log_vol, states, transition)
    parts, packed = packed[:2], packed[2:]

    sides = swaps(groups)
    gathered = jnp.concatenate([lax.ppermute(part, "theta", pairs) for part, pairs in zip(parts, sides)])
    chunk_in = [
        [lax.ppermute(packed[2 * c + side], "theta", sides[side]) for side in range(2)]
        for c in range(len(chunks))
    ]
    distance = ways // 2
    while distance:
        pairs = [(i, i ^ distance) for i in range(shards)]
        gathered = jnp.concatenate([gathered, lax.ppermute(gathered, "state", pairs)])
        distance //= 2
    gathered = gathered.reshape(2 * half, width, width)

    cols_shape = jax.ShapeDtypeStruct((len(batches), 4, ROWS, LANES), F32)
    meta, cols, prior = call(
        functools.partial(plan_kernel, p_dev, early, batches),
        [
            jax.ShapeDtypeStruct((3, p_dev), I32),
            cols_shape,
            jax.ShapeDtypeStruct((ROWS, LANES), F32),
        ],
        [smem()] * 6,
        [smem(), vmem(), vmem()],
        "plan",
        nbytes=1 << 14,
    )(ancestors, vol_mean, vol_persist, vol_scale, obs_prec, prior_loglik)

    number = counts[:, :, 0]
    first = prefix_counts(number)
    index_shapes = [
        jax.ShapeDtypeStruct((STEPS, ROWS, s_dev), I32),
        jax.ShapeDtypeStruct((STEPS, s_dev, ROWS), I32),
        jax.ShapeDtypeStruct((STEPS, ROWS, 2 * margin), I32),
        jax.ShapeDtypeStruct((STEPS, 2 * margin, ROWS), I32),
    ] * len(batches) + [
        jax.ShapeDtypeStruct((maturities, width), BF16),
        jax.ShapeDtypeStruct((maturities, ROWS), F32),
    ]
    indices = call(
        functools.partial(index_kernel, batches, s_dev, margin),
        index_shapes,
        [smem()] * 3 + [vmem()] * 3,
        [vmem()] * len(index_shapes),
        "indices",
        nbytes=1 << 18,
    )(meta, number, first, local_anc, loading, yields)
    loading_t, wanted = indices[-2:]

    matrices = call(
        functools.partial(matrix_kernel, p_dev, ways),
        jax.ShapeDtypeStruct((p_dev, width, width), BF16),
        [smem(), hbm(), hbm()],
        vmem(),
        "matrices",
        [pltpu.SemaphoreType.DMA((p_dev,))],
        nbytes=p_dev * width * width * 4,
    )(meta, transition, gathered)

    pair_round, other_round = swaps(shards)
    edge_shape = jax.ShapeDtypeStruct((batch * margin + PAD, width), BF16)
    cloud_shape = jax.ShapeDtypeStruct((batch, s_dev, width), BF16)
    vol_shape = jax.ShapeDtypeStruct((ROWS, s_dev), F32)
    stat_shape = jax.ShapeDtypeStruct((2, ROWS, LANES), F32)
    before = None
    follow = []
    for q in range(len(batches)):
        src, src_t, edge, edge_t = indices[4 * q : 4 * q + 4]
        recv, recv_slots = [], []
        for c in range(q + 1):
            for side in range(2):
                recv.append(chunk_in[c][side])
                recv_slots.append(tuple(p_dev + side * half + k for k in chunks[c]))
        cloud, vol, pair, other = call(
            functools.partial(fetch_kernel, batch, q * batch, margin, vol_rows, tuple(recv_slots)),
            [cloud_shape, vol_shape, edge_shape, edge_shape],
            [smem(), hbm()] + [vmem()] * (3 + len(recv) + len(follow)),
            [vmem()] * 4,
            "fetch",
            [pltpu.VMEM((2 * p_dev, s_dev), F32), pltpu.SemaphoreType.DMA((batch,))],
            flops=2 * batch * 2 * margin * s_dev * width,
            nbytes=2 * batch * s_dev * width * 2,
        )(meta, states, log_vol, edge, edge_t, *recv, *follow)
        stat = None
        for step in range(STEPS):
            last = step == STEPS - 1
            pair_in = lax.ppermute(pair, "state", pair_round)
            other_in = lax.ppermute(other, "state", other_round)
            own = call(
                functools.partial(own_kernel, batch, step, margin),
                cloud_shape,
                [vmem(), vmem()],
                vmem(),
                "own_rows",
                flops=2 * batch * s_dev * s_dev * width,
                nbytes=batch * s_dev * width * 4,
            )(src_t, cloud)
            operands = [
                cols[q], own, pair_in, other_in, vol, src, src_t, edge, edge_t, matrices,
                state_noise, vol_noise, loading_t, wanted,
            ]
            specs = [vmem()] * len(operands)
            if step:
                operands.append(stat)
                specs.append(vmem())
            aliases, scratch = None, []
            if last:
                operands.append(meta)
                specs.append(smem())
                out_shape = [
                    jax.ShapeDtypeStruct(states.shape, BF16),
                    jax.ShapeDtypeStruct(log_vol.shape, BF16),
                    stat_shape,
                ]
                out_specs = [hbm(), vmem(), vmem()]
                scratch = [
                    pltpu.VMEM((batch, s_dev, width), BF16),
                    pltpu.SemaphoreType.DMA((batch,)),
                ]
                if before is not None:
                    aliases = {len(operands): 0}
                    operands += before
                    specs += [hbm(), vmem(), vmem()]
            else:
                out_shape = [cloud_shape, vol_shape, stat_shape, edge_shape, edge_shape]
                out_specs = [vmem()] * 5
            results = call(
                functools.partial(step_kernel, batch, q * batch, step, margin, before is not None),
                out_shape,
                specs,
                out_specs,
                "step",
                scratch,
                flops=2 * batch * s_dev * width * (width + maturities + margin),
                nbytes=batch * s_dev * width * 8,
                aliases=aliases,
            )(*operands)
            if last:
                before = list(results)
            else:
                cloud, vol, stat, pair, other = results
                follow = [stat]
    final, vols, stats = before
    total = combined_mass(stats, prior, s_dev * shards)
    return (final, vols, total.reshape(p_dev))


def solution(mesh):
    placed = (
        P("theta", "state", None),
        P("theta", "state"),
        P("theta", None, None),
        P(),
        P(),
        P(None, "state", None),
        P(None, "state"),
        P(),
        P(),
        P(),
        P(),
        P(),
        P(),
        P(None, "theta", "state"),
        P(None, "theta", "state"),
    )
    return jax.shard_map(
        local,
        mesh=mesh,
        in_specs=placed,
        out_specs=(P("theta", "state", None), P("theta", "state"), P("theta")),
        check_vma=False,
    )
```

```python
import functools
import math

import jax
import jax.numpy as jnp
from jax import lax
from jax.experimental import pallas as pl
from jax.experimental.pallas import tpu as pltpu
from jax.sharding import PartitionSpec as P

STEPS = 3
LANES = 128
ROWS = 8
PAD = 16
VLIMIT = 8 * 1024 * 1024
PACK_LIMIT = 64 * 1024 * 1024

VM = pltpu.VMEM
SM = pltpu.SMEM
F32 = jnp.float32
BF16 = jnp.bfloat16
I32 = jnp.int32


def vmem():
    return pl.BlockSpec(memory_space=pltpu.VMEM)


def smem():
    return pl.BlockSpec(memory_space=pltpu.SMEM)


def anywhere():
    return pl.BlockSpec(memory_space=pl.ANY)


def hbm():
    return pl.BlockSpec(memory_space=pltpu.HBM)


def call(kernel, out_shape, in_specs, out_specs, name, scratch=(), flops=0, nbytes=0, aliases=None,
         limit=VLIMIT):
    return pl.pallas_call(
        kernel,
        out_shape=out_shape,
        in_specs=in_specs,
        out_specs=out_specs,
        scratch_shapes=list(scratch),
        input_output_aliases=aliases or {},
        compiler_params=pltpu.CompilerParams(vmem_limit_bytes=limit),
        cost_estimate=pl.CostEstimate(flops=flops // 64, bytes_accessed=nbytes // 64, transcendentals=0),
        name=name,
    )


def pack_kernel(groups, batches, ways, vol_rows, anc_hbm, *rest):
    tables_hbm, (vols_hbm, states_ref, transition_ref), rest = rest[:5], rest[5:8], rest[8:]
    *side_outs, part_out = rest[:3]
    rest = rest[3:]
    meta_ref, cols_ref, prior_ref, anc_ref, *rest = rest
    tables, (names, vols_ref, load_sems, part_sems, sems) = rest[:5], rest[5:]
    p_dev, s_dev, width = states_ref.shape
    half = p_dev // 2
    per_part = half // ways
    group, shard = lax.axis_index("theta"), lax.axis_index("state")
    loads = [(anc_hbm, anc_ref), (vols_hbm, vols_ref)] + list(zip(tables_hbm, tables))
    loads = [pltpu.make_async_copy(src, dst, load_sems.at[k]) for k, (src, dst) in enumerate(loads)]
    for load in loads:
        load.start()
    loads[0].wait()

    odd = lax.rem(group, 2)
    for side in range(2):
        other = group + (1 - 2 * odd if side == 0 else 2 * odd - 1)
        valid = (other >= 0) & (other < groups)
        other = jnp.clip(other, 0, groups - 1)
        for k in range(half):
            names[side, k] = 0
        rank = jnp.int32(0)
        for i in range(p_dev):
            a = anc_ref[other * p_dev + i]
            hit = valid & (lax.div(a, p_dev) == group) & (rank < half)

            @pl.when(hit)
            def _(side=side, rank=rank, a=a):
                names[side, rank] = lax.rem(a, p_dev)

            rank = rank + hit.astype(I32)

    copies = []
    tail = -(-half * vol_rows // PAD) * PAD
    for side, out in enumerate(side_outs):
        parts, at = (out, half * s_dev + tail) if side == 0 else (part_out, 0)
        for k in range(per_part):
            copies.append(
                pltpu.make_async_copy(
                    transition_ref.at[names[side, lax.rem(shard, ways) * per_part + k]],
                    parts.at[pl.ds(at + k * width, width)],
                    part_sems.at[side, k],
                )
            )
        for slot in range(half):
            copies.append(
                pltpu.make_async_copy(
                    states_ref.at[names[side, slot]],
                    out.at[pl.ds(slot * s_dev, s_dev)],
                    sems.at[side, slot],
                )
            )
    for copy in copies:
        copy.start()

    for load in loads[1:]:
        load.wait()
    rows = lax.broadcasted_iota(I32, (p_dev, 1), 0)
    table = vols_ref[...].astype(F32)
    for side, out in enumerate(side_outs):
        pieces = []
        for slot in range(half):
            here = rows == names[side, slot]
            row = jnp.sum(jnp.where(here, table, 0.0), axis=0, keepdims=True)
            pieces += [row[:, k * width : (k + 1) * width] for k in range(vol_rows)]
        pieces += [jnp.zeros((1, width), F32)] * (tail - len(pieces))
        out[pl.ds(half * s_dev, tail), :] = jnp.concatenate(pieces, axis=0).astype(BF16)

    even = odd == 0
    low_side, high_side = jnp.where(even, half, 0), jnp.where(even, 0, half)
    rank_low, rank_high = jnp.int32(0), jnp.int32(0)
    front, back = jnp.int32(0), jnp.int32(p_dev - 1)
    for i in range(p_dev):
        a = anc_ref[group * p_dev + i]
        offset = lax.div(a, p_dev) - group
        low, high = offset == -1, offset == 1
        late = jnp.where(even, low, high)
        moved = p_dev + jnp.where(low, low_side + rank_low, high_side + rank_high)
        position = jnp.where(late, back, front)
        meta_ref[0, position] = i
        meta_ref[1, position] = jnp.where(low | high, moved, lax.rem(a, p_dev))
        meta_ref[2, position] = a
        front = front + jnp.where(late, 0, 1)
        back = back - jnp.where(late, 1, 0)
        rank_low = rank_low + low.astype(I32)
        rank_high = rank_high + high.astype(I32)
    for q, batch in enumerate(batches):
        for k in range(4):
            value = column([tables[k][meta_ref[2, batch[b % len(batch)]]] for b in range(ROWS)])
            cols_ref[q, k] = jnp.broadcast_to(value, (ROWS, LANES))
    prior = column([tables[4][anc_ref[group * p_dev + i]] for i in range(p_dev)])
    prior_ref[...] = jnp.broadcast_to(prior, (ROWS, LANES))
    for copy in copies:
        copy.wait()


def lane_pick(blocks, index):
    low = index & (LANES - 1)
    high = index >> 7
    out = None
    for k, block in blocks:
        got = jnp.take_along_axis(block, low, axis=1, mode="promise_in_bounds")
        out = got if out is None else jnp.where(high == k, got, out)
    return out


def column(scalars):
    rows = lax.broadcasted_iota(I32, (ROWS, 1), 0)
    out = jnp.zeros((ROWS, 1), scalars[0].dtype)
    for b, scalar in enumerate(scalars):
        out = jnp.where(rows == b, scalar, out)
    return out


def index_kernel(batches, s_dev, margin, meta_ref, count_ref, first_ref, anc_ref,
                 loading_ref, yields_ref, *outs):
    shard = lax.axis_index("state")
    base = shard * s_dev
    even = lax.rem(shard, 2) == 0
    lanes = lax.broadcasted_iota(I32, (ROWS, LANES), 1)
    for q, batch in enumerate(batches):
        src_ref, src_t_ref, edge_ref, edge_t_ref = outs[4 * q : 4 * q + 4]
        for step in range(STEPS):
            who = [meta_ref[0, batch[b % len(batch)]] for b in range(ROWS)]
            chosen = jnp.concatenate([anc_ref[step, pl.ds(i, 1), :] for i in who], axis=0)
            blocks = [chosen[:, k * LANES : (k + 1) * LANES] for k in range(chosen.shape[1] // LANES)]
            count = column([count_ref[step, i] for i in who])
            shift = column([base - first_ref[step, i] for i in who])
            sources = []
            for o in range(s_dev // LANES):
                relative = o * LANES + lanes + shift
                own = lane_pick(list(enumerate(blocks)), jnp.clip(relative, 0, chosen.shape[1] - 1))
                sources.append(
                    jnp.where(
                        relative < 0,
                        relative + margin,
                        jnp.where(relative < count, margin + own, margin + s_dev + relative - count),
                    )
                )
            source = jnp.concatenate(sources, axis=1)
            src_ref[step] = source
            src_t_ref[step] = source.T
            head = jnp.concatenate(blocks[: margin // LANES], axis=1)
            tail = [
                lane_pick(list(enumerate(blocks)), count - margin + o * LANES + lanes)
                for o in range(margin // LANES)
            ]
            tail = jnp.concatenate(tail, axis=1)
            edge = jnp.concatenate([jnp.where(even, tail, head), jnp.where(even, head, tail)], axis=1)
            edge_ref[step] = edge
            edge_t_ref[step] = edge.T
    loading_t_ref, wanted_ref = outs[4 * len(batches) :]
    loading_t_ref[...] = loading_ref[...].astype(F32).T.astype(BF16)
    rows = yields_ref[...]
    rows = jnp.concatenate([rows, jnp.zeros((ROWS - STEPS, rows.shape[1]), F32)], axis=0)
    wanted_ref[...] = rows.T


def one_hot(index, columns):
    index = index.astype(jnp.int16)
    lanes = lax.broadcasted_iota(jnp.int16, (index.shape[0], columns), 1)
    return jnp.where(index == lanes, BF16(1), BF16(0))


def send_edges(batch, margin, cloud_at, vol, edge, edge_t, pair_ref, other_ref):
    s_dev = vol.shape[1]
    blocks = [(k, vol[:, k * LANES : (k + 1) * LANES]) for k in range(s_dev // LANES)]
    width = pair_ref.shape[1]
    for out, start in ((pair_ref, 0), (other_ref, margin)):
        picked = [
            lane_pick(blocks, edge[:, start + o * LANES : start + (o + 1) * LANES])
            for o in range(margin // LANES)
        ]
        picked.append(jnp.zeros((ROWS, width - margin), F32))
        flat = jnp.concatenate(picked, axis=1)
        flat = jnp.concatenate([flat, jnp.zeros((PAD - ROWS, width), F32)], axis=0)
        out[pl.ds(batch * margin, PAD), :] = flat.astype(BF16)
    for b in range(batch):
        rows = jnp.dot(
            one_hot(edge_t[:, b : b + 1], s_dev), cloud_at(b), preferred_element_type=F32
        ).astype(BF16)
        pair_ref[pl.ds(b * margin, margin), :] = rows[:margin]
        other_ref[pl.ds(b * margin, margin), :] = rows[margin:]


def fetch_kernel(batch, first_place, margin, vol_rows, recv_slots, meta_ref, states_ref, vols_ref,
                 edge_ref, edge_t_ref, *rest):
    recv = rest[: len(recv_slots)]
    cloud_ref, vol_ref, pair_ref, other_ref, table, sems = rest[-6:]
    p_dev, s_dev, _ = states_ref.shape
    for b in range(batch):
        place = meta_ref[1, first_place + b]

        @pl.when(place < p_dev)
        def _(b=b, place=place):
            pltpu.make_async_copy(
                states_ref.at[jnp.minimum(place, p_dev - 1)], cloud_ref.at[b], sems.at[b]
            ).start()

        for ref, codes in zip(recv, recv_slots):
            for k, code in enumerate(codes):

                @pl.when(place == code)
                def _(b=b, ref=ref, k=k):
                    pltpu.make_async_copy(
                        ref.at[pl.ds(k * s_dev, s_dev)], cloud_ref.at[b], sems.at[b]
                    ).start()

    table[...] = jnp.zeros(table.shape, F32)
    table[pl.ds(0, p_dev), :] = vols_ref[...].astype(F32)
    for ref, codes in zip(recv, recv_slots):
        tail = -(-len(codes) * vol_rows // PAD) * PAD
        rows = ref[pl.ds(len(codes) * s_dev, tail), :].astype(F32)
        for k, code in enumerate(codes):
            pieces = [rows[k * vol_rows + r : k * vol_rows + r + 1] for r in range(vol_rows)]
            table[pl.ds(code, 1), :] = jnp.concatenate(pieces, axis=1)
    vol = jnp.concatenate(
        [table[pl.ds(meta_ref[1, first_place + b % batch], 1), :] for b in range(ROWS)], axis=0
    )
    vol_ref[...] = vol
    for b in range(batch):
        pltpu.make_async_copy(states_ref.at[0], cloud_ref.at[b], sems.at[b]).wait()
    send_edges(batch, margin, lambda b: cloud_ref[b], vol, edge_ref[0], edge_t_ref[0], pair_ref, other_ref)


def matrix_kernel(p_dev, ways, meta_ref, transition_ref, gathered_ref, out_ref, sems):
    half = p_dev // 2
    per_part = half // ways
    mine = lax.rem(lax.axis_index("state"), ways)
    for b in range(p_dev):
        place = meta_ref[1, b]

        @pl.when(place < p_dev)
        def _(b=b, place=place):
            pltpu.make_async_copy(
                transition_ref.at[jnp.minimum(place, p_dev - 1)], out_ref.at[b], sems.at[b]
            ).start()

        @pl.when(place >= p_dev)
        def _(b=b, place=place):
            moved = jnp.maximum(place - p_dev, 0)
            side, slot = lax.div(moved, half), lax.rem(moved, half)
            apart = lax.div(slot, per_part) ^ mine
            index, size, distance = jnp.int32(0), 1, ways // 2
            while distance:
                index = index + jnp.where((apart & distance) != 0, size, 0)
                size, distance = 2 * size, distance // 2
            at = (index * 2 + side) * per_part + lax.rem(slot, per_part)
            pltpu.make_async_copy(gathered_ref.at[at], out_ref.at[b], sems.at[b]).start()

    for b in range(p_dev):
        pltpu.make_async_copy(transition_ref.at[0], out_ref.at[b], sems.at[b]).wait()


def own_kernel(batch, step, margin, src_t_ref, cloud_ref, out_ref):
    s_dev = cloud_ref.shape[1]
    for b in range(batch):
        index = src_t_ref[step][:, b : b + 1] - margin
        out_ref[b] = jnp.dot(
            one_hot(index, s_dev), cloud_ref[b], preferred_element_type=F32
        ).astype(BF16)


def step_kernel(batch, first_place, step, margin, merge, cols_ref, own_ref, pair_ref, other_ref, vol_ref,
                src_ref, src_t_ref, edge_ref, edge_t_ref, matrix_ref, noise_ref, vnoise_ref,
                loading_ref, wanted_ref, *rest):
    last = step == STEPS - 1
    s_dev = vol_ref.shape[1]
    rest = list(rest)
    stat_in = rest.pop(0) if step else None
    if last:
        meta_ref = rest.pop(0)
        if merge:
            _, vol_before, stat_before = rest[:3]
            rest = rest[3:]
        final_ref, vol_out, stat_ref, cloud_out, sems = rest
    else:
        cloud_out, vol_out, stat_ref, pair_out, other_out = rest
    even = lax.rem(lax.axis_index("state"), 2) == 0
    source = src_ref[step]
    vol = vol_ref[...]
    blocks = [(k, vol[:, k * LANES : (k + 1) * LANES]) for k in range(s_dev // LANES)]

    def edge_vols(ref):
        return ref[pl.ds(batch * margin, PAD), :].astype(F32)[:ROWS]

    pair_v, other_v = edge_vols(pair_ref), edge_vols(other_ref)
    low_v, high_v = jnp.where(even, other_v, pair_v), jnp.where(even, pair_v, other_v)
    picked = []
    for o in range(s_dev // LANES):
        index = source[:, o * LANES : (o + 1) * LANES]
        own = lane_pick(blocks, jnp.clip(index - margin, 0, s_dev - 1))
        if o < margin // LANES:
            low = [(k, low_v[:, k * LANES : (k + 1) * LANES]) for k in range(margin // LANES)]
            own = jnp.where(index < margin, lane_pick(low, index), own)
        if o >= (s_dev - margin) // LANES:
            high = [(k, high_v[:, k * LANES : (k + 1) * LANES]) for k in range(margin // LANES)]
            above = jnp.clip(index - margin - s_dev, 0, margin - 1)
            own = jnp.where(index >= margin + s_dev, lane_pick(high, above), own)
        picked.append(own)
    picked = jnp.concatenate(picked, axis=1)

    def param(k):
        return cols_ref[k][:, :1]

    center, persist, spread = param(0), param(1), param(2)
    h = center + persist * (picked - center) + spread * vnoise_ref[pl.ds(step, 1), :]
    scale_t = jnp.exp(0.5 * h).T
    vol_new = h.astype(BF16).astype(F32)
    if not last:
        vol_out[...] = vol_new

    wanted = wanted_ref[:, step : step + 1]
    tile = s_dev // 2
    squares = []
    for b in range(batch):
        row = []
        for r in range(2):
            span = pl.ds(r * tile, tile)
            index = src_t_ref[step, span, :][:, b : b + 1]
            own = own_ref[b, span, :]
            pair, other = pair_ref[pl.ds(b * margin, margin), :], other_ref[pl.ds(b * margin, margin), :]
            if r == 0:
                patch = jnp.dot(
                    one_hot(index[:margin], margin),
                    jnp.where(even, other, pair),
                    preferred_element_type=F32,
                )
                cloud = jnp.concatenate(
                    [(own[:margin].astype(F32) + patch).astype(BF16), own[margin:]], axis=0
                )
            else:
                patch = jnp.dot(
                    one_hot(index[tile - margin :] - (margin + s_dev), margin),
                    jnp.where(even, pair, other),
                    preferred_element_type=F32,
                )
                cloud = jnp.concatenate(
                    [own[: tile - margin], (own[tile - margin :].astype(F32) + patch).astype(BF16)],
                    axis=0,
                )
            drift = jnp.dot(cloud, matrix_ref[first_place + b], preferred_element_type=F32)
            noise = noise_ref[step, span, :].astype(F32)
            cloud = (drift + scale_t[r * tile : (r + 1) * tile, b : b + 1] * noise).astype(BF16)
            cloud_out[b, span, :] = cloud
            predicted = lax.dot_general(
                loading_ref[...], cloud, (((1,), (1,)), ((), ())), preferred_element_type=F32
            )
            misfit = wanted - predicted
            row.append(jnp.sum(misfit * misfit, axis=0, keepdims=True))
        squares.append(jnp.concatenate(row, axis=1))
        if last:
            pltpu.make_async_copy(
                cloud_out.at[b], final_ref.at[meta_ref[0, first_place + b]], sems.at[b]
            ).start()
    if not last:
        send_edges(
            batch, margin, lambda b: cloud_out[b], vol_new, edge_ref[step + 1], edge_t_ref[step + 1],
            pair_out, other_out,
        )
    squares += [squares[0]] * (ROWS - batch)
    square = jnp.concatenate(squares, axis=0)
    precision = param(3)
    maturities = wanted_ref.shape[0]
    weights = -0.5 * precision * square + 0.5 * maturities * jnp.log(precision)
    peak = jnp.max(weights, axis=1, keepdims=True)
    mass = jnp.sum(jnp.exp(weights - peak), axis=1, keepdims=True)
    lane = lax.broadcasted_iota(I32, (ROWS, LANES), 1)
    before = [stat_in[0], stat_in[1]] if step else [jnp.zeros((ROWS, LANES), F32)] * 2
    stats = [jnp.where(lane == step, new, old) for new, old in zip((peak, mass), before)]
    if last:
        rows = lax.broadcasted_iota(I32, (ROWS, 1), 0)
        vol_all = vol_before[...].astype(F32) if merge else jnp.zeros(vol_new.shape, F32)
        placed = [stat_before[0], stat_before[1]] if merge else [jnp.zeros((ROWS, LANES), F32)] * 2
        for b in range(batch):
            here = rows == meta_ref[0, first_place + b]
            vol_all = jnp.where(here, vol_new[b : b + 1], vol_all)
            placed = [jnp.where(here, new[b : b + 1], old) for new, old in zip(stats, placed)]
        vol_out[...] = vol_all.astype(BF16)
        stats = placed
    stat_ref[0] = stats[0]
    stat_ref[1] = stats[1]
    if last:
        for b in range(batch):
            pltpu.make_async_copy(cloud_out.at[b], final_ref.at[0], sems.at[b]).wait()


def join_kernel(finish, whole_rows, *refs):
    mine_ref, others, (out_ref,) = refs[0], refs[1:-1], refs[-1:]
    if finish:
        prior_ref, others = others[0], others[1:]
    peak, mass = mine_ref[0], mine_ref[1]
    for other in others:
        other_peak = other[0]
        top = jnp.maximum(peak, other_peak)
        mass = mass * jnp.exp(peak - top) + other[1] * jnp.exp(other_peak - top)
        peak = top
    if not finish:
        out_ref[0] = peak
        out_ref[1] = mass
        return
    lane = lax.broadcasted_iota(I32, (ROWS, LANES), 1)
    gained = peak + jnp.log(jnp.where(lane < STEPS, mass, 1.0)) - math.log(whole_rows)
    gained = jnp.sum(jnp.where(lane < STEPS, gained, 0.0), axis=1, keepdims=True)
    total = jnp.broadcast_to(prior_ref[:, :1] + gained, (ROWS, LANES))
    out_ref[...] = total.T[:1, :]


def join(stats, others, whole_rows, prior=None):
    operands = [stats] + ([] if prior is None else [prior]) + list(others)
    shape = stats.shape if prior is None else (1, ROWS)
    return call(
        functools.partial(join_kernel, prior is not None, whole_rows),
        jax.ShapeDtypeStruct(shape, F32),
        [vmem()] * len(operands),
        vmem(),
        "join",
        nbytes=1 << 14,
    )(*operands)


def swaps(count):
    rounds = []
    for offset in (0, 1):
        partner = [(i - offset ^ 1) + offset for i in range(count)]
        rounds.append([(i, p if 0 <= p < count else i) for i, p in enumerate(partner)])
    return rounds


def doubling(count):
    distance = 1
    while distance < count:
        yield distance, [(i, i ^ distance) for i in range(count)]
        distance *= 2


def prefix_counts(number):
    count, here = lax.axis_size("state"), lax.axis_index("state")
    if count & (count - 1):
        every = lax.all_gather(number, "state")
        before = jnp.arange(count) < here
        return jnp.sum(jnp.where(before[:, None, None], every, 0), axis=0)
    before, total = jnp.zeros_like(number), number
    for distance, pairs in doubling(count):
        other = lax.ppermute(total, "state", pairs)
        before = before + jnp.where((here & distance) != 0, other, 0)
        total = total + other
    return before


def combined_mass(stats, prior, whole_rows):
    count = lax.axis_size("state")
    if count & (count - 1):
        every = lax.all_gather(stats, "state")
        return join(every[0], [every[k] for k in range(1, count)], whole_rows, prior)
    rounds = [pairs for _, pairs in doubling(count)]
    if not rounds:
        return join(stats, [], whole_rows, prior)
    for k, pairs in enumerate(rounds):
        other = lax.ppermute(stats, "state", pairs)
        stats = join(stats, [other], whole_rows, prior if k == len(rounds) - 1 else None)
    return stats


def local(
    states,
    log_vol,
    transition,
    loading,
    yields,
    state_noise,
    vol_noise,
    vol_mean,
    vol_persist,
    vol_scale,
    obs_prec,
    prior_loglik,
    ancestors,
    counts,
    local_anc,
):
    p_dev, s_dev, width = states.shape
    maturities = loading.shape[1]
    groups, shards = lax.axis_size("theta"), lax.axis_size("state")
    half = p_dev // 2
    margin = s_dev // 4
    batch = p_dev // 2
    batches = [tuple(range(q * batch, (q + 1) * batch)) for q in range(p_dev // batch)]
    vol_rows = s_dev // width
    ways = next(w for w in (4, 2, 1) if half % w == 0 and shards % w == 0)
    per_part = half // ways

    tail = -(-half * vol_rows // PAD) * PAD
    cloud_rows = half * s_dev + tail
    packed_shapes = [
        jax.ShapeDtypeStruct((rows, width), BF16)
        for rows in (cloud_rows + per_part * width, cloud_rows, per_part * width)
    ]
    small = ancestors.shape
    near, far, far_part, meta, cols, prior = call(
        functools.partial(pack_kernel, groups, batches, ways, vol_rows),
        packed_shapes
        + [
            jax.ShapeDtypeStruct((3, p_dev), I32),
            jax.ShapeDtypeStruct((len(batches), 4, ROWS, LANES), F32),
            jax.ShapeDtypeStruct((ROWS, LANES), F32),
        ],
        [anywhere()] * 9,
        [vmem()] * 3 + [smem(), vmem(), vmem()],
        "pack",
        [pltpu.SMEM(small, I32)]
        + [pltpu.SMEM(small, F32)] * 5
        + [
            pltpu.SMEM((2, half), I32),
            pltpu.VMEM((p_dev, s_dev), BF16),
            pltpu.SemaphoreType.DMA((7,)),
            pltpu.SemaphoreType.DMA((2, per_part)),
            pltpu.SemaphoreType.DMA((2, half)),
        ],
        nbytes=4 * half * s_dev * width * 2,
        limit=PACK_LIMIT,
    )(ancestors, vol_mean, vol_persist, vol_scale, obs_prec, prior_loglik, log_vol, states, transition)

    sides = swaps(groups)
    far_part = lax.ppermute(far_part, "theta", sides[1])
    near = lax.ppermute(near, "theta", sides[0])
    far = lax.ppermute(far, "theta", sides[1])

    number = counts[:, :, 0]
    first = prefix_counts(number)
    index_shapes = [
        jax.ShapeDtypeStruct((STEPS, ROWS, s_dev), I32),
        jax.ShapeDtypeStruct((STEPS, s_dev, ROWS), I32),
        jax.ShapeDtypeStruct((STEPS, ROWS, 2 * margin), I32),
        jax.ShapeDtypeStruct((STEPS, 2 * margin, ROWS), I32),
    ] * len(batches) + [
        jax.ShapeDtypeStruct((maturities, width), BF16),
        jax.ShapeDtypeStruct((maturities, ROWS), F32),
    ]
    indices = call(
        functools.partial(index_kernel, batches, s_dev, margin),
        index_shapes,
        [smem()] * 3 + [vmem()] * 3,
        [vmem()] * len(index_shapes),
        "indices",
        nbytes=1 << 18,
    )(meta, number, first, local_anc, loading, yields)
    loading_t, wanted = indices[-2:]

    arrived, far_part, _ = lax.optimization_barrier((near, far_part, indices[-1]))
    gathered = jnp.concatenate([arrived[cloud_rows:], far_part])
    distance = ways // 2
    while distance:
        pairs = [(i, i ^ distance) for i in range(shards)]
        gathered = jnp.concatenate([gathered, lax.ppermute(gathered, "state", pairs)])
        distance //= 2
    gathered = gathered.reshape(2 * half, width, width)

    matrices = call(
        functools.partial(matrix_kernel, p_dev, ways),
        jax.ShapeDtypeStruct((p_dev, width, width), BF16),
        [smem(), hbm(), hbm()],
        vmem(),
        "matrices",
        [pltpu.SemaphoreType.DMA((p_dev,))],
        nbytes=p_dev * width * width * 4,
    )(meta, transition, gathered)

    pair_round, other_round = swaps(shards)
    edge_shape = jax.ShapeDtypeStruct((batch * margin + PAD, width), BF16)
    cloud_shape = jax.ShapeDtypeStruct((batch, s_dev, width), BF16)
    vol_shape = jax.ShapeDtypeStruct((ROWS, s_dev), F32)
    stat_shape = jax.ShapeDtypeStruct((2, ROWS, LANES), F32)
    before = None
    follow = []
    for q in range(len(batches)):
        src, src_t, edge, edge_t = indices[4 * q : 4 * q + 4]
        recv = [near, far][: q + 1]
        recv_slots = [tuple(p_dev + side * half + k for k in range(half)) for side in range(q + 1)]
        cloud, vol, pair, other = call(
            functools.partial(fetch_kernel, batch, q * batch, margin, vol_rows, tuple(recv_slots)),
            [cloud_shape, vol_shape, edge_shape, edge_shape],
            [smem(), hbm()] + [vmem()] * (3 + len(recv) + len(follow)),
            [vmem()] * 4,
            "fetch",
            [pltpu.VMEM((2 * p_dev, s_dev), F32), pltpu.SemaphoreType.DMA((batch,))],
            flops=2 * batch * 2 * margin * s_dev * width,
            nbytes=2 * batch * s_dev * width * 2,
        )(meta, states, log_vol, edge, edge_t, *recv, *follow)
        stat = None
        for step in range(STEPS):
            last = step == STEPS - 1
            other_in = lax.ppermute(other, "state", other_round)
            pair_in = lax.ppermute(pair, "state", pair_round)
            own = call(
                functools.partial(own_kernel, batch, step, margin),
                cloud_shape,
                [vmem(), vmem()],
                vmem(),
                "own_rows",
                flops=2 * batch * s_dev * s_dev * width,
                nbytes=batch * s_dev * width * 4,
            )(src_t, cloud)
            operands = [
                cols[q], own, pair_in, other_in, vol, src, src_t, edge, edge_t, matrices,
                state_noise, vol_noise, loading_t, wanted,
            ]
            specs = [vmem()] * len(operands)
            if step:
                operands.append(stat)
                specs.append(vmem())
            aliases, scratch = None, []
            if last:
                operands.append(meta)
                specs.append(smem())
                out_shape = [
                    jax.ShapeDtypeStruct(states.shape, BF16),
                    jax.ShapeDtypeStruct(log_vol.shape, BF16),
                    stat_shape,
                ]
                out_specs = [hbm(), vmem(), vmem()]
                scratch = [
                    pltpu.VMEM((batch, s_dev, width), BF16),
                    pltpu.SemaphoreType.DMA((batch,)),
                ]
                if before is not None:
                    aliases = {len(operands): 0}
                    operands += before
                    specs += [hbm(), vmem(), vmem()]
            else:
                out_shape = [cloud_shape, vol_shape, stat_shape, edge_shape, edge_shape]
                out_specs = [vmem()] * 5
            results = call(
                functools.partial(step_kernel, batch, q * batch, step, margin, before is not None),
                out_shape,
                specs,
                out_specs,
                "step",
                scratch,
                flops=2 * batch * s_dev * width * (width + maturities + margin),
                nbytes=batch * s_dev * width * 8,
                aliases=aliases,
            )(*operands)
            if last:
                before = list(results)
            else:
                cloud, vol, stat, pair, other = results
                follow = [stat]
    final, vols, stats = before
    total = combined_mass(stats, prior, s_dev * shards)
    return (final, vols, total.reshape(p_dev))


def solution(mesh):
    placed = (
        P("theta", "state", None),
        P("theta", "state"),
        P("theta", None, None),
        P(),
        P(),
        P(None, "state", None),
        P(None, "state"),
        P(),
        P(),
        P(),
        P(),
        P(),
        P(),
        P(None, "theta", "state"),
        P(None, "theta", "state"),
    )
    return jax.shard_map(
        local,
        mesh=mesh,
        in_specs=placed,
        out_specs=(P("theta", "state", None), P("theta", "state"), P("theta")),
        check_vma=False,
    )
```

```python
import functools
import math

import jax
import jax.numpy as jnp
from jax import lax
from jax.experimental import pallas as pl
from jax.experimental.pallas import tpu as pltpu
from jax.sharding import PartitionSpec as P

STEPS = 3
LANES = 128
ROWS = 8
PAD = 16
VLIMIT = 8 * 1024 * 1024
PACK_LIMIT = 64 * 1024 * 1024

VM = pltpu.VMEM
SM = pltpu.SMEM
F32 = jnp.float32
BF16 = jnp.bfloat16
I32 = jnp.int32


def vmem():
    return pl.BlockSpec(memory_space=pltpu.VMEM)


def smem():
    return pl.BlockSpec(memory_space=pltpu.SMEM)


def anywhere():
    return pl.BlockSpec(memory_space=pl.ANY)


def hbm():
    return pl.BlockSpec(memory_space=pltpu.HBM)


def call(kernel, out_shape, in_specs, out_specs, name, scratch=(), flops=0, nbytes=0, aliases=None,
         limit=VLIMIT):
    return pl.pallas_call(
        kernel,
        out_shape=out_shape,
        in_specs=in_specs,
        out_specs=out_specs,
        scratch_shapes=list(scratch),
        input_output_aliases=aliases or {},
        compiler_params=pltpu.CompilerParams(vmem_limit_bytes=limit),
        cost_estimate=pl.CostEstimate(flops=flops // 64, bytes_accessed=nbytes // 64, transcendentals=0),
        name=name,
    )


def pack_kernel(groups, relayed, batches, ways, vol_rows, anc_hbm, *rest):
    tables_hbm, (vols_hbm, states_ref, transition_ref), rest = rest[:5], rest[5:8], rest[8:]
    first_out, second_out, third_out, part_out = rest[:4]
    rest = rest[4:]
    meta_ref, cols_ref, prior_ref, anc_ref, *rest = rest
    tables, (names, vols_ref, load_sems, part_sems, sems) = rest[:5], rest[5:]
    p_dev, s_dev, width = states_ref.shape
    half = p_dev // 2
    per_part = half // ways
    group, shard = lax.axis_index("theta"), lax.axis_index("state")
    loads = [(anc_hbm, anc_ref), (vols_hbm, vols_ref)] + list(zip(tables_hbm, tables))
    loads = [pltpu.make_async_copy(src, dst, load_sems.at[k]) for k, (src, dst) in enumerate(loads)]
    for load in loads:
        load.start()
    loads[0].wait()

    odd = lax.rem(group, 2)
    for side in range(2):
        other = group + (1 - 2 * odd if side == 0 else 2 * odd - 1)
        valid = (other >= 0) & (other < groups)
        other = jnp.clip(other, 0, groups - 1)
        for k in range(half):
            names[side, k] = 0
        rank = jnp.int32(0)
        for i in range(p_dev):
            a = anc_ref[other * p_dev + i]
            hit = valid & (lax.div(a, p_dev) == group) & (rank < half)

            @pl.when(hit)
            def _(side=side, rank=rank, a=a):
                names[side, rank] = lax.rem(a, p_dev)

            rank = rank + hit.astype(I32)

    early = half // 2
    inner = (group > 0) & (group < groups - 1)
    if relayed:
        takes = [((1, 0), (0, 0)), ((0, 0), (0, early)), ((1, early), (0, 0)), ((0, early), (0, 0))]
    else:
        takes = [((0, 0),) * 2, ((0, early),) * 2, ((1, 0),) * 2, ((1, early),) * 2]
    takes = [
        (jnp.where(inner, ours[0], theirs[0]), jnp.where(inner, ours[1], theirs[1]))
        for ours, theirs in takes
    ]
    copies = []
    tail = -(-half * vol_rows // PAD) * PAD
    block = early * s_dev + tail
    outs = [(first_out, 0), (first_out, block), (second_out, 0), (third_out, 0)]
    for hop, ((out, at), (side, first)) in enumerate(zip(outs, takes)):
        for k in range(early):
            copies.append(
                pltpu.make_async_copy(
                    states_ref.at[names[side, first + k]],
                    out.at[pl.ds(at + k * s_dev, s_dev)],
                    sems.at[hop, k],
                )
            )
    for side in range(2):
        parts, at = (first_out, block + early * s_dev) if side == 0 else (part_out, 0)
        for k in range(per_part):
            copies.append(
                pltpu.make_async_copy(
                    transition_ref.at[names[side, lax.rem(shard, ways) * per_part + k]],
                    parts.at[pl.ds(at + k * width, width)],
                    part_sems.at[side, k],
                )
            )
    for copy in copies:
        copy.start()

    for load in loads[1:]:
        load.wait()
    rows = lax.broadcasted_iota(I32, (p_dev, 1), 0)
    table = vols_ref[...].astype(F32)
    for out, hops in ((first_out, takes[:2]), (second_out, takes[2:3]), (third_out, takes[3:])):
        pieces = []
        for side, first in hops:
            for k in range(early):
                here = rows == names[side, first + k]
                row = jnp.sum(jnp.where(here, table, 0.0), axis=0, keepdims=True)
                pieces += [row[:, r * width : (r + 1) * width] for r in range(vol_rows)]
        pieces += [jnp.zeros((1, width), F32)] * (tail - len(pieces))
        out[pl.ds(early * s_dev, tail), :] = jnp.concatenate(pieces, axis=0).astype(BF16)

    even = odd == 0
    rank_near, rank_far = jnp.int32(0), jnp.int32(0)
    front, back = jnp.int32(0), jnp.int32(p_dev - 1)
    for i in range(p_dev):
        a = anc_ref[group * p_dev + i]
        offset = lax.div(a, p_dev) - group
        near = jnp.where(even, offset == 1, offset == -1)
        far = jnp.where(even, offset == -1, offset == 1)
        late = far
        came = rank_near
        if relayed:
            late = far | (near & ~inner)
            came = jnp.where(inner, rank_near, rank_near + jnp.where(rank_near < early, early, half))
        came = jnp.where(far, half + rank_far, came)
        moved = jnp.where(far, half + rank_far, rank_near)
        position = jnp.where(late, back, front)
        meta_ref[0, position] = i
        meta_ref[1, position] = jnp.where(near | far, p_dev + came, lax.rem(a, p_dev))
        meta_ref[2, position] = a
        meta_ref[3, position] = jnp.where(near | far, p_dev + moved, lax.rem(a, p_dev))
        front = front + jnp.where(late, 0, 1)
        back = back - jnp.where(late, 1, 0)
        rank_near = rank_near + near.astype(I32)
        rank_far = rank_far + far.astype(I32)
    for q, batch in enumerate(batches):
        for k in range(4):
            value = column([tables[k][meta_ref[2, batch[b % len(batch)]]] for b in range(ROWS)])
            cols_ref[q, k] = jnp.broadcast_to(value, (ROWS, LANES))
    prior = column([tables[4][anc_ref[group * p_dev + i]] for i in range(p_dev)])
    prior_ref[...] = jnp.broadcast_to(prior, (ROWS, LANES))
    for copy in copies:
        copy.wait()


def lane_pick(blocks, index):
    low = index & (LANES - 1)
    high = index >> 7
    out = None
    for k, block in blocks:
        got = jnp.take_along_axis(block, low, axis=1, mode="promise_in_bounds")
        out = got if out is None else jnp.where(high == k, got, out)
    return out


def column(scalars):
    rows = lax.broadcasted_iota(I32, (ROWS, 1), 0)
    out = jnp.zeros((ROWS, 1), scalars[0].dtype)
    for b, scalar in enumerate(scalars):
        out = jnp.where(rows == b, scalar, out)
    return out


def index_kernel(batches, s_dev, margin, meta_ref, count_ref, first_ref, anc_ref,
                 loading_ref, yields_ref, *outs):
    shard = lax.axis_index("state")
    base = shard * s_dev
    even = lax.rem(shard, 2) == 0
    lanes = lax.broadcasted_iota(I32, (ROWS, LANES), 1)
    for q, batch in enumerate(batches):
        src_ref, src_t_ref, edge_ref, edge_t_ref = outs[4 * q : 4 * q + 4]
        for step in range(STEPS):
            who = [meta_ref[0, batch[b % len(batch)]] for b in range(ROWS)]
            chosen = jnp.concatenate([anc_ref[step, pl.ds(i, 1), :] for i in who], axis=0)
            blocks = [chosen[:, k * LANES : (k + 1) * LANES] for k in range(chosen.shape[1] // LANES)]
            count = column([count_ref[step, i] for i in who])
            shift = column([base - first_ref[step, i] for i in who])
            sources = []
            for o in range(s_dev // LANES):
                relative = o * LANES + lanes + shift
                own = lane_pick(list(enumerate(blocks)), jnp.clip(relative, 0, chosen.shape[1] - 1))
                sources.append(
                    jnp.where(
                        relative < 0,
                        relative + margin,
                        jnp.where(relative < count, margin + own, margin + s_dev + relative - count),
                    )
                )
            source = jnp.concatenate(sources, axis=1)
            src_ref[step] = source
            src_t_ref[step] = source.T
            head = jnp.concatenate(blocks[: margin // LANES], axis=1)
            tail = [
                lane_pick(list(enumerate(blocks)), count - margin + o * LANES + lanes)
                for o in range(margin // LANES)
            ]
            tail = jnp.concatenate(tail, axis=1)
            edge = jnp.concatenate([jnp.where(even, tail, head), jnp.where(even, head, tail)], axis=1)
            edge_ref[step] = edge
            edge_t_ref[step] = edge.T
    loading_t_ref, wanted_ref = outs[4 * len(batches) :]
    loading_t_ref[...] = loading_ref[...].astype(F32).T.astype(BF16)
    rows = yields_ref[...]
    rows = jnp.concatenate([rows, jnp.zeros((ROWS - STEPS, rows.shape[1]), F32)], axis=0)
    wanted_ref[...] = rows.T


def one_hot(index, columns):
    index = index.astype(jnp.int16)
    lanes = lax.broadcasted_iota(jnp.int16, (index.shape[0], columns), 1)
    return jnp.where(index == lanes, BF16(1), BF16(0))


def send_edges(batch, margin, cloud_at, vol, edge, edge_t, pair_ref, other_ref):
    s_dev = vol.shape[1]
    blocks = [(k, vol[:, k * LANES : (k + 1) * LANES]) for k in range(s_dev // LANES)]
    width = pair_ref.shape[1]
    for out, start in ((pair_ref, 0), (other_ref, margin)):
        picked = [
            lane_pick(blocks, edge[:, start + o * LANES : start + (o + 1) * LANES])
            for o in range(margin // LANES)
        ]
        picked.append(jnp.zeros((ROWS, width - margin), F32))
        flat = jnp.concatenate(picked, axis=1)
        flat = jnp.concatenate([flat, jnp.zeros((PAD - ROWS, width), F32)], axis=0)
        out[pl.ds(batch * margin, PAD), :] = flat.astype(BF16)
    for b in range(batch):
        rows = jnp.dot(
            one_hot(edge_t[:, b : b + 1], s_dev), cloud_at(b), preferred_element_type=F32
        ).astype(BF16)
        pair_ref[pl.ds(b * margin, margin), :] = rows[:margin]
        other_ref[pl.ds(b * margin, margin), :] = rows[margin:]


def fetch_kernel(batch, first_place, margin, vol_rows, recv_slots, meta_ref, states_ref, vols_ref,
                 edge_ref, edge_t_ref, *rest):
    recv = rest[: len(recv_slots)]
    cloud_ref, vol_ref, pair_ref, other_ref, table, sems = rest[-6:]
    p_dev, s_dev, _ = states_ref.shape
    for b in range(batch):
        place = meta_ref[1, first_place + b]

        @pl.when(place < p_dev)
        def _(b=b, place=place):
            pltpu.make_async_copy(
                states_ref.at[jnp.minimum(place, p_dev - 1)], cloud_ref.at[b], sems.at[b]
            ).start()

        for ref, codes in zip(recv, recv_slots):
            for code, at, _ in codes:

                @pl.when(place == code)
                def _(b=b, ref=ref, at=at):
                    pltpu.make_async_copy(
                        ref.at[pl.ds(at, s_dev)], cloud_ref.at[b], sems.at[b]
                    ).start()

    table[...] = jnp.zeros(table.shape, F32)
    table[pl.ds(0, p_dev), :] = vols_ref[...].astype(F32)
    for ref, codes in zip(recv, recv_slots):
        start = codes[0][2]
        length = -(-len(codes) * vol_rows // PAD) * PAD
        rows = ref[pl.ds(start, length), :].astype(F32)
        for code, _, at in codes:
            pieces = [rows[at - start + r : at - start + r + 1] for r in range(vol_rows)]
            table[pl.ds(code, 1), :] = jnp.concatenate(pieces, axis=1)
    vol = jnp.concatenate(
        [table[pl.ds(meta_ref[1, first_place + b % batch], 1), :] for b in range(ROWS)], axis=0
    )
    vol_ref[...] = vol
    for b in range(batch):
        pltpu.make_async_copy(states_ref.at[0], cloud_ref.at[b], sems.at[b]).wait()
    send_edges(batch, margin, lambda b: cloud_ref[b], vol, edge_ref[0], edge_t_ref[0], pair_ref, other_ref)


def matrix_kernel(p_dev, ways, meta_ref, transition_ref, gathered_ref, out_ref, sems):
    half = p_dev // 2
    per_part = half // ways
    mine = lax.rem(lax.axis_index("state"), ways)
    for b in range(p_dev):
        place = meta_ref[3, b]

        @pl.when(place < p_dev)
        def _(b=b, place=place):
            pltpu.make_async_copy(
                transition_ref.at[jnp.minimum(place, p_dev - 1)], out_ref.at[b], sems.at[b]
            ).start()

        @pl.when(place >= p_dev)
        def _(b=b, place=place):
            moved = jnp.maximum(place - p_dev, 0)
            side, slot = lax.div(moved, half), lax.rem(moved, half)
            apart = lax.div(slot, per_part) ^ mine
            index, size, distance = jnp.int32(0), 1, ways // 2
            while distance:
                index = index + jnp.where((apart & distance) != 0, size, 0)
                size, distance = 2 * size, distance // 2
            at = (index * 2 + side) * per_part + lax.rem(slot, per_part)
            pltpu.make_async_copy(gathered_ref.at[at], out_ref.at[b], sems.at[b]).start()

    for b in range(p_dev):
        pltpu.make_async_copy(transition_ref.at[0], out_ref.at[b], sems.at[b]).wait()


def own_kernel(batch, step, margin, src_t_ref, cloud_ref, out_ref):
    s_dev = cloud_ref.shape[1]
    for b in range(batch):
        index = src_t_ref[step][:, b : b + 1] - margin
        out_ref[b] = jnp.dot(
            one_hot(index, s_dev), cloud_ref[b], preferred_element_type=F32
        ).astype(BF16)


def step_kernel(batch, first_place, step, margin, merge, cols_ref, own_ref, pair_ref, other_ref, vol_ref,
                src_ref, src_t_ref, edge_ref, edge_t_ref, matrix_ref, noise_ref, vnoise_ref,
                loading_ref, wanted_ref, *rest):
    last = step == STEPS - 1
    s_dev = vol_ref.shape[1]
    rest = list(rest)
    stat_in = rest.pop(0) if step else None
    if last:
        meta_ref = rest.pop(0)
        if merge:
            _, vol_before, stat_before = rest[:3]
            rest = rest[3:]
        final_ref, vol_out, stat_ref, cloud_out, sems = rest
    else:
        cloud_out, vol_out, stat_ref, pair_out, other_out = rest
    even = lax.rem(lax.axis_index("state"), 2) == 0
    source = src_ref[step]
    vol = vol_ref[...]
    blocks = [(k, vol[:, k * LANES : (k + 1) * LANES]) for k in range(s_dev // LANES)]

    def edge_vols(ref):
        return ref[pl.ds(batch * margin, PAD), :].astype(F32)[:ROWS]

    pair_v, other_v = edge_vols(pair_ref), edge_vols(other_ref)
    low_v, high_v = jnp.where(even, other_v, pair_v), jnp.where(even, pair_v, other_v)
    picked = []
    for o in range(s_dev // LANES):
        index = source[:, o * LANES : (o + 1) * LANES]
        own = lane_pick(blocks, jnp.clip(index - margin, 0, s_dev - 1))
        if o < margin // LANES:
            low = [(k, low_v[:, k * LANES : (k + 1) * LANES]) for k in range(margin // LANES)]
            own = jnp.where(index < margin, lane_pick(low, index), own)
        if o >= (s_dev - margin) // LANES:
            high = [(k, high_v[:, k * LANES : (k + 1) * LANES]) for k in range(margin // LANES)]
            above = jnp.clip(index - margin - s_dev, 0, margin - 1)
            own = jnp.where(index >= margin + s_dev, lane_pick(high, above), own)
        picked.append(own)
    picked = jnp.concatenate(picked, axis=1)

    def param(k):
        return cols_ref[k][:, :1]

    center, persist, spread = param(0), param(1), param(2)
    h = center + persist * (picked - center) + spread * vnoise_ref[pl.ds(step, 1), :]
    scale_t = jnp.exp(0.5 * h).T
    vol_new = h.astype(BF16).astype(F32)
    if not last:
        vol_out[...] = vol_new

    wanted = wanted_ref[:, step : step + 1]
    tile = s_dev // 2
    squares = []
    for b in range(batch):
        row = []
        for r in range(2):
            span = pl.ds(r * tile, tile)
            index = src_t_ref[step, span, :][:, b : b + 1]
            own = own_ref[b, span, :]
            pair, other = pair_ref[pl.ds(b * margin, margin), :], other_ref[pl.ds(b * margin, margin), :]
            if r == 0:
                patch = jnp.dot(
                    one_hot(index[:margin], margin),
                    jnp.where(even, other, pair),
                    preferred_element_type=F32,
                )
                cloud = jnp.concatenate(
                    [(own[:margin].astype(F32) + patch).astype(BF16), own[margin:]], axis=0
                )
            else:
                patch = jnp.dot(
                    one_hot(index[tile - margin :] - (margin + s_dev), margin),
                    jnp.where(even, pair, other),
                    preferred_element_type=F32,
                )
                cloud = jnp.concatenate(
                    [own[: tile - margin], (own[tile - margin :].astype(F32) + patch).astype(BF16)],
                    axis=0,
                )
            drift = jnp.dot(cloud, matrix_ref[first_place + b], preferred_element_type=F32)
            noise = noise_ref[step, span, :].astype(F32)
            cloud = (drift + scale_t[r * tile : (r + 1) * tile, b : b + 1] * noise).astype(BF16)
            cloud_out[b, span, :] = cloud
            predicted = lax.dot_general(
                loading_ref[...], cloud, (((1,), (1,)), ((), ())), preferred_element_type=F32
            )
            misfit = wanted - predicted
            row.append(jnp.sum(misfit * misfit, axis=0, keepdims=True))
        squares.append(jnp.concatenate(row, axis=1))
        if last:
            pltpu.make_async_copy(
                cloud_out.at[b], final_ref.at[meta_ref[0, first_place + b]], sems.at[b]
            ).start()
    if not last:
        send_edges(
            batch, margin, lambda b: cloud_out[b], vol_new, edge_ref[step + 1], edge_t_ref[step + 1],
            pair_out, other_out,
        )
    squares += [squares[0]] * (ROWS - batch)
    square = jnp.concatenate(squares, axis=0)
    precision = param(3)
    maturities = wanted_ref.shape[0]
    weights = -0.5 * precision * square + 0.5 * maturities * jnp.log(precision)
    peak = jnp.max(weights, axis=1, keepdims=True)
    mass = jnp.sum(jnp.exp(weights - peak), axis=1, keepdims=True)
    lane = lax.broadcasted_iota(I32, (ROWS, LANES), 1)
    before = [stat_in[0], stat_in[1]] if step else [jnp.zeros((ROWS, LANES), F32)] * 2
    stats = [jnp.where(lane == step, new, old) for new, old in zip((peak, mass), before)]
    if last:
        rows = lax.broadcasted_iota(I32, (ROWS, 1), 0)
        vol_all = vol_before[...].astype(F32) if merge else jnp.zeros(vol_new.shape, F32)
        placed = [stat_before[0], stat_before[1]] if merge else [jnp.zeros((ROWS, LANES), F32)] * 2
        for b in range(batch):
            here = rows == meta_ref[0, first_place + b]
            vol_all = jnp.where(here, vol_new[b : b + 1], vol_all)
            placed = [jnp.where(here, new[b : b + 1], old) for new, old in zip(stats, placed)]
        vol_out[...] = vol_all.astype(BF16)
        stats = placed
    stat_ref[0] = stats[0]
    stat_ref[1] = stats[1]
    if last:
        for b in range(batch):
            pltpu.make_async_copy(cloud_out.at[b], final_ref.at[0], sems.at[b]).wait()


def join_kernel(finish, whole_rows, *refs):
    mine_ref, others, (out_ref,) = refs[0], refs[1:-1], refs[-1:]
    if finish:
        prior_ref, others = others[0], others[1:]
    peak, mass = mine_ref[0], mine_ref[1]
    for other in others:
        other_peak = other[0]
        top = jnp.maximum(peak, other_peak)
        mass = mass * jnp.exp(peak - top) + other[1] * jnp.exp(other_peak - top)
        peak = top
    if not finish:
        out_ref[0] = peak
        out_ref[1] = mass
        return
    lane = lax.broadcasted_iota(I32, (ROWS, LANES), 1)
    gained = peak + jnp.log(jnp.where(lane < STEPS, mass, 1.0)) - math.log(whole_rows)
    gained = jnp.sum(jnp.where(lane < STEPS, gained, 0.0), axis=1, keepdims=True)
    total = jnp.broadcast_to(prior_ref[:, :1] + gained, (ROWS, LANES))
    out_ref[...] = total.T[:1, :]


def join(stats, others, whole_rows, prior=None):
    operands = [stats] + ([] if prior is None else [prior]) + list(others)
    shape = stats.shape if prior is None else (1, ROWS)
    return call(
        functools.partial(join_kernel, prior is not None, whole_rows),
        jax.ShapeDtypeStruct(shape, F32),
        [vmem()] * len(operands),
        vmem(),
        "join",
        nbytes=1 << 14,
    )(*operands)


def swaps(count):
    rounds = []
    for offset in (0, 1):
        partner = [(i - offset ^ 1) + offset for i in range(count)]
        rounds.append([(i, p if 0 <= p < count else i) for i, p in enumerate(partner)])
    return rounds


def doubling(count):
    distance = 1
    while distance < count:
        yield distance, [(i, i ^ distance) for i in range(count)]
        distance *= 2


def prefix_counts(number):
    count, here = lax.axis_size("state"), lax.axis_index("state")
    if count & (count - 1):
        every = lax.all_gather(number, "state")
        before = jnp.arange(count) < here
        return jnp.sum(jnp.where(before[:, None, None], every, 0), axis=0)
    before, total = jnp.zeros_like(number), number
    for distance, pairs in doubling(count):
        other = lax.ppermute(total, "state", pairs)
        before = before + jnp.where((here & distance) != 0, other, 0)
        total = total + other
    return before


def combined_mass(stats, prior, whole_rows):
    count = lax.axis_size("state")
    if count & (count - 1):
        every = lax.all_gather(stats, "state")
        return join(every[0], [every[k] for k in range(1, count)], whole_rows, prior)
    if count == 1:
        return join(stats, [], whole_rows, prior)
    distances = [distance for distance, _ in doubling(count)]
    while distances:
        now, distances = distances[:3], distances[3:]
        apart = [sum(d for j, d in enumerate(now) if k >> j & 1) for k in range(1, 1 << len(now))]
        others = [lax.ppermute(stats, "state", [(i, i ^ d) for i in range(count)]) for d in apart]
        stats = join(stats, others, whole_rows, None if distances else prior)
    return stats


def local(
    states,
    log_vol,
    transition,
    loading,
    yields,
    state_noise,
    vol_noise,
    vol_mean,
    vol_persist,
    vol_scale,
    obs_prec,
    prior_loglik,
    ancestors,
    counts,
    local_anc,
):
    p_dev, s_dev, width = states.shape
    maturities = loading.shape[1]
    groups, shards = lax.axis_size("theta"), lax.axis_size("state")
    half = p_dev // 2
    margin = s_dev // 4
    batch = p_dev // 2
    batches = [tuple(range(q * batch, (q + 1) * batch)) for q in range(p_dev // batch)]
    vol_rows = s_dev // width
    ways = next(w for w in (4, 2, 1) if half % w == 0 and shards % w == 0)
    per_part = half // ways

    early = half // 2
    relayed = groups == 4
    tail = -(-half * vol_rows // PAD) * PAD
    block = early * s_dev + tail
    near_rows = block + early * s_dev
    part_rows = per_part * width
    packed_shapes = [
        jax.ShapeDtypeStruct((rows, width), BF16)
        for rows in (near_rows + part_rows, block, block, part_rows)
    ]
    small = ancestors.shape
    first_hop, second_hop, third_hop, far_part, meta, cols, prior = call(
        functools.partial(pack_kernel, groups, relayed, batches, ways, vol_rows),
        packed_shapes
        + [
            jax.ShapeDtypeStruct((4, p_dev), I32),
            jax.ShapeDtypeStruct((len(batches), 4, ROWS, LANES), F32),
            jax.ShapeDtypeStruct((ROWS, LANES), F32),
        ],
        [anywhere()] * 9,
        [vmem()] * 4 + [smem(), vmem(), vmem()],
        "pack",
        [pltpu.SMEM(small, I32)]
        + [pltpu.SMEM(small, F32)] * 5
        + [
            pltpu.SMEM((2, half), I32),
            pltpu.VMEM((p_dev, s_dev), BF16),
            pltpu.SemaphoreType.DMA((7,)),
            pltpu.SemaphoreType.DMA((2, per_part)),
            pltpu.SemaphoreType.DMA((4, early)),
        ],
        nbytes=4 * half * s_dev * width * 2,
        limit=PACK_LIMIT,
    )(ancestors, vol_mean, vol_persist, vol_scale, obs_prec, prior_loglik, log_vol, states, transition)

    near_pairs, far_pairs = swaps(groups)
    far_part = lax.ppermute(far_part, "theta", far_pairs)
    near = lax.ppermute(first_hop, "theta", near_pairs)
    if relayed:
        cross_pairs = [(i, i ^ 2) for i in range(groups)]
        across = lax.ppermute(second_hop, "theta", cross_pairs)
        far_first = lax.ppermute(near[:block], "theta", cross_pairs)
        group = lax.axis_index("theta")
        inner = (group > 0) & (group < groups - 1)
        far_last = lax.ppermute(jnp.where(inner, third_hop, across), "theta", near_pairs)
    else:
        far_first = lax.ppermute(second_hop, "theta", far_pairs)
        far_last = lax.ppermute(third_hop, "theta", far_pairs)

    vols_at = early * s_dev
    arrivals = [
        (near, 0, [(k // early) * block + (k % early) * s_dev for k in range(half)]),
        (far_first, half, [k * s_dev for k in range(early)]),
        (far_last, half + early, [k * s_dev for k in range(early)]),
    ]
    arrivals = [
        (x, tuple((p_dev + code + k, at, vols_at + k * vol_rows) for k, at in enumerate(rows)))
        for x, code, rows in arrivals
    ]

    number = counts[:, :, 0]
    first = prefix_counts(number)
    index_shapes = [
        jax.ShapeDtypeStruct((STEPS, ROWS, s_dev), I32),
        jax.ShapeDtypeStruct((STEPS, s_dev, ROWS), I32),
        jax.ShapeDtypeStruct((STEPS, ROWS, 2 * margin), I32),
        jax.ShapeDtypeStruct((STEPS, 2 * margin, ROWS), I32),
    ] * len(batches) + [
        jax.ShapeDtypeStruct((maturities, width), BF16),
        jax.ShapeDtypeStruct((maturities, ROWS), F32),
    ]
    indices = call(
        functools.partial(index_kernel, batches, s_dev, margin),
        index_shapes,
        [smem()] * 3 + [vmem()] * 3,
        [vmem()] * len(index_shapes),
        "indices",
        nbytes=1 << 18,
    )(meta, number, first, local_anc, loading, yields)
    loading_t, wanted = indices[-2:]

    arrived, far_part, _ = lax.optimization_barrier((near, far_part, indices[-1]))
    gathered = jnp.concatenate([arrived[near_rows:], far_part])
    distance = ways // 2
    while distance:
        pairs = [(i, i ^ distance) for i in range(shards)]
        gathered = jnp.concatenate([gathered, lax.ppermute(gathered, "state", pairs)])
        distance //= 2
    gathered = gathered.reshape(2 * half, width, width)

    matrices = call(
        functools.partial(matrix_kernel, p_dev, ways),
        jax.ShapeDtypeStruct((p_dev, width, width), BF16),
        [smem(), hbm(), hbm()],
        vmem(),
        "matrices",
        [pltpu.SemaphoreType.DMA((p_dev,))],
        nbytes=p_dev * width * width * 4,
    )(meta, transition, gathered)

    pair_round, other_round = swaps(shards)
    edge_shape = jax.ShapeDtypeStruct((batch * margin + PAD, width), BF16)
    cloud_shape = jax.ShapeDtypeStruct((batch, s_dev, width), BF16)
    vol_shape = jax.ShapeDtypeStruct((ROWS, s_dev), F32)
    stat_shape = jax.ShapeDtypeStruct((2, ROWS, LANES), F32)
    before = None
    follow = []
    for q in range(len(batches)):
        src, src_t, edge, edge_t = indices[4 * q : 4 * q + 4]
        recv, recv_slots = zip(*(arrivals if q else arrivals[:1]))
        cloud, vol, pair, other = call(
            functools.partial(fetch_kernel, batch, q * batch, margin, vol_rows, recv_slots),
            [cloud_shape, vol_shape, edge_shape, edge_shape],
            [smem(), hbm()] + [vmem()] * (3 + len(recv) + len(follow)),
            [vmem()] * 4,
            "fetch",
            [pltpu.VMEM((2 * p_dev, s_dev), F32), pltpu.SemaphoreType.DMA((batch,))],
            flops=2 * batch * 2 * margin * s_dev * width,
            nbytes=2 * batch * s_dev * width * 2,
        )(meta, states, log_vol, edge, edge_t, *recv, *follow)
        stat = None
        for step in range(STEPS):
            last = step == STEPS - 1
            other_in = lax.ppermute(other, "state", other_round)
            pair_in = lax.ppermute(pair, "state", pair_round)
            own = call(
                functools.partial(own_kernel, batch, step, margin),
                cloud_shape,
                [vmem(), vmem()],
                vmem(),
                "own_rows",
                flops=2 * batch * s_dev * s_dev * width,
                nbytes=batch * s_dev * width * 4,
            )(src_t, cloud)
            operands = [
                cols[q], own, pair_in, other_in, vol, src, src_t, edge, edge_t, matrices,
                state_noise, vol_noise, loading_t, wanted,
            ]
            specs = [vmem()] * len(operands)
            if step:
                operands.append(stat)
                specs.append(vmem())
            aliases, scratch = None, []
            if last:
                operands.append(meta)
                specs.append(smem())
                out_shape = [
                    jax.ShapeDtypeStruct(states.shape, BF16),
                    jax.ShapeDtypeStruct(log_vol.shape, BF16),
                    stat_shape,
                ]
                out_specs = [hbm(), vmem(), vmem()]
                scratch = [
                    pltpu.VMEM((batch, s_dev, width), BF16),
                    pltpu.SemaphoreType.DMA((batch,)),
                ]
                if before is not None:
                    aliases = {len(operands): 0}
                    operands += before
                    specs += [hbm(), vmem(), vmem()]
            else:
                out_shape = [cloud_shape, vol_shape, stat_shape, edge_shape, edge_shape]
                out_specs = [vmem()] * 5
            results = call(
                functools.partial(step_kernel, batch, q * batch, step, margin, before is not None),
                out_shape,
                specs,
                out_specs,
                "step",
                scratch,
                flops=2 * batch * s_dev * width * (width + maturities + margin),
                nbytes=batch * s_dev * width * 8,
                aliases=aliases,
            )(*operands)
            if last:
                before = list(results)
            else:
                cloud, vol, stat, pair, other = results
                follow = [stat] if step == 0 else follow
    final, vols, stats = before
    total = combined_mass(stats, prior, s_dev * shards)
    return (final, vols, total.reshape(p_dev))


def solution(mesh):
    placed = (
        P("theta", "state", None),
        P("theta", "state"),
        P("theta", None, None),
        P(),
        P(),
        P(None, "state", None),
        P(None, "state"),
        P(),
        P(),
        P(),
        P(),
        P(),
        P(),
        P(None, "theta", "state"),
        P(None, "theta", "state"),
    )
    return jax.shard_map(
        local,
        mesh=mesh,
        in_specs=placed,
        out_specs=(P("theta", "state", None), P("theta", "state"), P("theta")),
        check_vma=False,
    )
```

```python
import functools
import math

import jax
import jax.numpy as jnp
from jax import lax
from jax.experimental import pallas as pl
from jax.experimental.pallas import tpu as pltpu
from jax.sharding import PartitionSpec as P

STEPS = 3
LANES = 128
ROWS = 8
PAD = 16
VLIMIT = 8 * 1024 * 1024
PACK_LIMIT = 64 * 1024 * 1024

VM = pltpu.VMEM
SM = pltpu.SMEM
F32 = jnp.float32
BF16 = jnp.bfloat16
I32 = jnp.int32


def vmem():
    return pl.BlockSpec(memory_space=pltpu.VMEM)


def smem():
    return pl.BlockSpec(memory_space=pltpu.SMEM)


def anywhere():
    return pl.BlockSpec(memory_space=pl.ANY)


def hbm():
    return pl.BlockSpec(memory_space=pltpu.HBM)


def call(kernel, out_shape, in_specs, out_specs, name, scratch=(), flops=0, nbytes=0, aliases=None,
         limit=VLIMIT):
    return pl.pallas_call(
        kernel,
        out_shape=out_shape,
        in_specs=in_specs,
        out_specs=out_specs,
        scratch_shapes=list(scratch),
        input_output_aliases=aliases or {},
        compiler_params=pltpu.CompilerParams(vmem_limit_bytes=limit),
        cost_estimate=pl.CostEstimate(flops=flops // 64, bytes_accessed=nbytes // 64, transcendentals=0),
        name=name,
    )


def pack_kernel(groups, relayed, batches, ways, vol_rows, anc_hbm, *rest):
    tables_hbm, (vols_hbm, states_ref, transition_ref), rest = rest[:5], rest[5:8], rest[8:]
    first_out, second_out, third_out, part_out = rest[:4]
    rest = rest[4:]
    meta_ref, cols_ref, prior_ref, anc_ref, *rest = rest
    tables, (names, vols_ref, load_sems, part_sems, sems) = rest[:5], rest[5:]
    p_dev, s_dev, width = states_ref.shape
    half = p_dev // 2
    per_part = half // ways
    group, shard = lax.axis_index("theta"), lax.axis_index("state")
    loads = [(anc_hbm, anc_ref), (vols_hbm, vols_ref)] + list(zip(tables_hbm, tables))
    loads = [pltpu.make_async_copy(src, dst, load_sems.at[k]) for k, (src, dst) in enumerate(loads)]
    for load in loads:
        load.start()
    loads[0].wait()

    odd = lax.rem(group, 2)
    for side in range(2):
        other = group + (1 - 2 * odd if side == 0 else 2 * odd - 1)
        valid = (other >= 0) & (other < groups)
        other = jnp.clip(other, 0, groups - 1)
        for k in range(half):
            names[side, k] = 0
        rank = jnp.int32(0)
        for i in range(p_dev):
            a = anc_ref[other * p_dev + i]
            hit = valid & (lax.div(a, p_dev) == group) & (rank < half)

            @pl.when(hit)
            def _(side=side, rank=rank, a=a):
                names[side, rank] = lax.rem(a, p_dev)

            rank = rank + hit.astype(I32)

    early = half // 2
    inner = (group > 0) & (group < groups - 1)
    if relayed:
        takes = [((1, 0), (0, 0)), ((0, 0), (0, early)), ((1, early), (0, 0)), ((0, early), (0, 0))]
    else:
        takes = [((0, 0),) * 2, ((0, early),) * 2, ((1, 0),) * 2, ((1, early),) * 2]
    takes = [
        (jnp.where(inner, ours[0], theirs[0]), jnp.where(inner, ours[1], theirs[1]))
        for ours, theirs in takes
    ]
    copies = []
    tail = -(-half * vol_rows // PAD) * PAD
    block = early * s_dev + tail
    outs = [(first_out, 0), (first_out, block), (second_out, 0), (third_out, 0)]
    for hop, ((out, at), (side, first)) in enumerate(zip(outs, takes)):
        for k in range(early):
            copies.append(
                pltpu.make_async_copy(
                    states_ref.at[names[side, first + k]],
                    out.at[pl.ds(at + k * s_dev, s_dev)],
                    sems.at[hop, k],
                )
            )
    for side in range(2):
        parts, at = (first_out, block + early * s_dev) if side == 0 else (part_out, 0)
        for k in range(per_part):
            copies.append(
                pltpu.make_async_copy(
                    transition_ref.at[names[side, lax.rem(shard, ways) * per_part + k]],
                    parts.at[pl.ds(at + k * width, width)],
                    part_sems.at[side, k],
                )
            )
    for copy in copies:
        copy.start()

    for load in loads[1:]:
        load.wait()
    rows = lax.broadcasted_iota(I32, (p_dev, 1), 0)
    table = vols_ref[...].astype(F32)
    for out, hops in ((first_out, takes[:2]), (second_out, takes[2:3]), (third_out, takes[3:])):
        pieces = []
        for side, first in hops:
            for k in range(early):
                here = rows == names[side, first + k]
                row = jnp.sum(jnp.where(here, table, 0.0), axis=0, keepdims=True)
                pieces += [row[:, r * width : (r + 1) * width] for r in range(vol_rows)]
        pieces += [jnp.zeros((1, width), F32)] * (tail - len(pieces))
        out[pl.ds(early * s_dev, tail), :] = jnp.concatenate(pieces, axis=0).astype(BF16)

    even = odd == 0
    rank_near, rank_far = jnp.int32(0), jnp.int32(0)
    front, back = jnp.int32(0), jnp.int32(p_dev - 1)
    for i in range(p_dev):
        a = anc_ref[group * p_dev + i]
        offset = lax.div(a, p_dev) - group
        near = jnp.where(even, offset == 1, offset == -1)
        far = jnp.where(even, offset == -1, offset == 1)
        late = far
        came = rank_near
        if relayed:
            late = far | (near & ~inner)
            came = jnp.where(inner, rank_near, rank_near + jnp.where(rank_near < early, early, half))
        came = jnp.where(far, half + rank_far, came)
        moved = jnp.where(far, half + rank_far, rank_near)
        position = jnp.where(late, back, front)
        meta_ref[0, position] = i
        meta_ref[1, position] = jnp.where(near | far, p_dev + came, lax.rem(a, p_dev))
        meta_ref[2, position] = a
        meta_ref[3, position] = jnp.where(near | far, p_dev + moved, lax.rem(a, p_dev))
        front = front + jnp.where(late, 0, 1)
        back = back - jnp.where(late, 1, 0)
        rank_near = rank_near + near.astype(I32)
        rank_far = rank_far + far.astype(I32)
    for q, batch in enumerate(batches):
        for k in range(4):
            value = column([tables[k][meta_ref[2, batch[b % len(batch)]]] for b in range(ROWS)])
            cols_ref[q, k] = jnp.broadcast_to(value, (ROWS, LANES))
    prior = column([tables[4][anc_ref[group * p_dev + i]] for i in range(p_dev)])
    prior_ref[...] = jnp.broadcast_to(prior, (ROWS, LANES))
    for copy in copies:
        copy.wait()


def lane_pick(blocks, index):
    low = index & (LANES - 1)
    high = index >> 7
    out = None
    for k, block in blocks:
        got = jnp.take_along_axis(block, low, axis=1, mode="promise_in_bounds")
        out = got if out is None else jnp.where(high == k, got, out)
    return out


def column(scalars):
    rows = lax.broadcasted_iota(I32, (ROWS, 1), 0)
    out = jnp.zeros((ROWS, 1), scalars[0].dtype)
    for b, scalar in enumerate(scalars):
        out = jnp.where(rows == b, scalar, out)
    return out


def index_kernel(batches, s_dev, margin, meta_ref, count_ref, first_ref, anc_ref, *outs):
    shard = lax.axis_index("state")
    base = shard * s_dev
    even = lax.rem(shard, 2) == 0
    lanes = lax.broadcasted_iota(I32, (ROWS, LANES), 1)
    for q, batch in enumerate(batches):
        src_ref, src_t_ref, edge_ref, edge_t_ref = outs[4 * q : 4 * q + 4]
        for step in range(STEPS):
            who = [meta_ref[0, batch[b % len(batch)]] for b in range(ROWS)]
            chosen = jnp.concatenate([anc_ref[step, pl.ds(i, 1), :] for i in who], axis=0)
            blocks = [chosen[:, k * LANES : (k + 1) * LANES] for k in range(chosen.shape[1] // LANES)]
            count = column([count_ref[step, i] for i in who])
            shift = column([base - first_ref[step, i] for i in who])
            sources = []
            for o in range(s_dev // LANES):
                relative = o * LANES + lanes + shift
                own = lane_pick(list(enumerate(blocks)), jnp.clip(relative, 0, chosen.shape[1] - 1))
                sources.append(
                    jnp.where(
                        relative < 0,
                        relative + margin,
                        jnp.where(relative < count, margin + own, margin + s_dev + relative - count),
                    )
                )
            source = jnp.concatenate(sources, axis=1)
            src_ref[step] = source
            src_t_ref[step] = source.T
            head = jnp.concatenate(blocks[: margin // LANES], axis=1)
            tail = [
                lane_pick(list(enumerate(blocks)), count - margin + o * LANES + lanes)
                for o in range(margin // LANES)
            ]
            tail = jnp.concatenate(tail, axis=1)
            edge = jnp.concatenate([jnp.where(even, tail, head), jnp.where(even, head, tail)], axis=1)
            edge_ref[step] = edge
            edge_t_ref[step] = edge.T


def one_hot(index, columns):
    index = index.astype(jnp.int16)
    lanes = lax.broadcasted_iota(jnp.int16, (index.shape[0], columns), 1)
    return jnp.where(index == lanes, BF16(1), BF16(0))


def send_edges(batch, margin, cloud_at, vol, edge, edge_t, pair_ref, other_ref):
    s_dev = vol.shape[1]
    blocks = [(k, vol[:, k * LANES : (k + 1) * LANES]) for k in range(s_dev // LANES)]
    width = pair_ref.shape[1]
    for out, start in ((pair_ref, 0), (other_ref, margin)):
        picked = [
            lane_pick(blocks, edge[:, start + o * LANES : start + (o + 1) * LANES])
            for o in range(margin // LANES)
        ]
        picked.append(jnp.zeros((ROWS, width - margin), F32))
        flat = jnp.concatenate(picked, axis=1)
        flat = jnp.concatenate([flat, jnp.zeros((PAD - ROWS, width), F32)], axis=0)
        out[pl.ds(batch * margin, PAD), :] = flat.astype(BF16)
    for b in range(batch):
        rows = jnp.dot(
            one_hot(edge_t[:, b : b + 1], s_dev), cloud_at(b), preferred_element_type=F32
        ).astype(BF16)
        pair_ref[pl.ds(b * margin, margin), :] = rows[:margin]
        other_ref[pl.ds(b * margin, margin), :] = rows[margin:]


def fetch_kernel(batch, first_place, margin, vol_rows, recv_slots, meta_ref, states_ref, vols_ref,
                 edge_ref, edge_t_ref, *rest):
    recv = rest[: len(recv_slots)]
    cloud_ref, vol_ref, pair_ref, other_ref, table, sems = rest[-6:]
    p_dev, s_dev, _ = states_ref.shape
    for b in range(batch):
        place = meta_ref[1, first_place + b]

        @pl.when(place < p_dev)
        def _(b=b, place=place):
            pltpu.make_async_copy(
                states_ref.at[jnp.minimum(place, p_dev - 1)], cloud_ref.at[b], sems.at[b]
            ).start()

        for ref, codes in zip(recv, recv_slots):
            for code, at, _ in codes:

                @pl.when(place == code)
                def _(b=b, ref=ref, at=at):
                    pltpu.make_async_copy(
                        ref.at[pl.ds(at, s_dev)], cloud_ref.at[b], sems.at[b]
                    ).start()

    table[...] = jnp.zeros(table.shape, F32)
    table[pl.ds(0, p_dev), :] = vols_ref[...].astype(F32)
    for ref, codes in zip(recv, recv_slots):
        start = codes[0][2]
        length = -(-len(codes) * vol_rows // PAD) * PAD
        rows = ref[pl.ds(start, length), :].astype(F32)
        for code, _, at in codes:
            pieces = [rows[at - start + r : at - start + r + 1] for r in range(vol_rows)]
            table[pl.ds(code, 1), :] = jnp.concatenate(pieces, axis=1)
    vol = jnp.concatenate(
        [table[pl.ds(meta_ref[1, first_place + b % batch], 1), :] for b in range(ROWS)], axis=0
    )
    vol_ref[...] = vol
    for b in range(batch):
        pltpu.make_async_copy(states_ref.at[0], cloud_ref.at[b], sems.at[b]).wait()
    send_edges(batch, margin, lambda b: cloud_ref[b], vol, edge_ref[0], edge_t_ref[0], pair_ref, other_ref)


def matrix_kernel(p_dev, ways, meta_ref, transition_ref, gathered_ref, out_ref, sems):
    half = p_dev // 2
    per_part = half // ways
    mine = lax.rem(lax.axis_index("state"), ways)
    for b in range(p_dev):
        place = meta_ref[3, b]

        @pl.when(place < p_dev)
        def _(b=b, place=place):
            pltpu.make_async_copy(
                transition_ref.at[jnp.minimum(place, p_dev - 1)], out_ref.at[b], sems.at[b]
            ).start()

        @pl.when(place >= p_dev)
        def _(b=b, place=place):
            moved = jnp.maximum(place - p_dev, 0)
            side, slot = lax.div(moved, half), lax.rem(moved, half)
            apart = lax.div(slot, per_part) ^ mine
            index, size, distance = jnp.int32(0), 1, ways // 2
            while distance:
                index = index + jnp.where((apart & distance) != 0, size, 0)
                size, distance = 2 * size, distance // 2
            at = (index * 2 + side) * per_part + lax.rem(slot, per_part)
            pltpu.make_async_copy(gathered_ref.at[at], out_ref.at[b], sems.at[b]).start()

    for b in range(p_dev):
        pltpu.make_async_copy(transition_ref.at[0], out_ref.at[b], sems.at[b]).wait()


def own_kernel(batch, step, margin, src_t_ref, cloud_ref, out_ref):
    s_dev = cloud_ref.shape[1]
    for b in range(batch):
        index = src_t_ref[step][:, b : b + 1] - margin
        out_ref[b] = jnp.dot(
            one_hot(index, s_dev), cloud_ref[b], preferred_element_type=F32
        ).astype(BF16)


def step_kernel(batch, first_place, step, margin, merge, cols_ref, own_ref, pair_ref, other_ref, vol_ref,
                src_ref, src_t_ref, edge_ref, edge_t_ref, matrix_ref, noise_ref, vnoise_ref,
                loading_ref, wanted_ref, *rest):
    last = step == STEPS - 1
    s_dev = vol_ref.shape[1]
    rest = list(rest)
    stat_in = rest.pop(0) if step else None
    if last:
        meta_ref = rest.pop(0)
        if merge:
            vol_before, stat_before = rest[:2]
            rest = rest[2:]
        cloud_out, vol_out, stat_ref = rest
    else:
        cloud_out, vol_out, stat_ref, pair_out, other_out = rest
    even = lax.rem(lax.axis_index("state"), 2) == 0
    source = src_ref[step]
    vol = vol_ref[...]
    blocks = [(k, vol[:, k * LANES : (k + 1) * LANES]) for k in range(s_dev // LANES)]

    def edge_vols(ref):
        return ref[pl.ds(batch * margin, PAD), :].astype(F32)[:ROWS]

    pair_v, other_v = edge_vols(pair_ref), edge_vols(other_ref)
    low_v, high_v = jnp.where(even, other_v, pair_v), jnp.where(even, pair_v, other_v)
    picked = []
    for o in range(s_dev // LANES):
        index = source[:, o * LANES : (o + 1) * LANES]
        own = lane_pick(blocks, jnp.clip(index - margin, 0, s_dev - 1))
        if o < margin // LANES:
            low = [(k, low_v[:, k * LANES : (k + 1) * LANES]) for k in range(margin // LANES)]
            own = jnp.where(index < margin, lane_pick(low, index), own)
        if o >= (s_dev - margin) // LANES:
            high = [(k, high_v[:, k * LANES : (k + 1) * LANES]) for k in range(margin // LANES)]
            above = jnp.clip(index - margin - s_dev, 0, margin - 1)
            own = jnp.where(index >= margin + s_dev, lane_pick(high, above), own)
        picked.append(own)
    picked = jnp.concatenate(picked, axis=1)

    def param(k):
        return cols_ref[k][:, :1]

    center, persist, spread = param(0), param(1), param(2)
    h = center + persist * (picked - center) + spread * vnoise_ref[pl.ds(step, 1), :]
    scale_t = jnp.exp(0.5 * h).T
    vol_new = h.astype(BF16).astype(F32)
    if not last:
        vol_out[...] = vol_new

    wanted = wanted_ref[pl.ds(step, 1), :]
    tile = s_dev // 2
    lanes = lax.broadcasted_iota(I32, (tile, LANES), 1)
    squares = [jnp.zeros((tile, LANES), F32)] * 2
    for b in range(batch):
        for r in range(2):
            span = pl.ds(r * tile, tile)
            index = src_t_ref[step, span, :][:, b : b + 1]
            own = own_ref[b, span, :]
            pair, other = pair_ref[pl.ds(b * margin, margin), :], other_ref[pl.ds(b * margin, margin), :]
            if r == 0:
                patch = jnp.dot(
                    one_hot(index[:margin], margin),
                    jnp.where(even, other, pair),
                    preferred_element_type=F32,
                )
                cloud = jnp.concatenate(
                    [(own[:margin].astype(F32) + patch).astype(BF16), own[margin:]], axis=0
                )
            else:
                patch = jnp.dot(
                    one_hot(index[tile - margin :] - (margin + s_dev), margin),
                    jnp.where(even, pair, other),
                    preferred_element_type=F32,
                )
                cloud = jnp.concatenate(
                    [own[: tile - margin], (own[tile - margin :].astype(F32) + patch).astype(BF16)],
                    axis=0,
                )
            drift = jnp.dot(cloud, matrix_ref[first_place + b], preferred_element_type=F32)
            noise = noise_ref[step, span, :].astype(F32)
            cloud = (drift + scale_t[r * tile : (r + 1) * tile, b : b + 1] * noise).astype(BF16)
            cloud_out[b, span, :] = cloud
            misfit = wanted - jnp.dot(cloud, loading_ref[...], preferred_element_type=F32)
            square = jnp.sum(misfit * misfit, axis=1, keepdims=True)
            squares[r] = jnp.where(lanes == b, square, squares[r])
    if not last:
        send_edges(
            batch, margin, lambda b: cloud_out[b], vol_new, edge_ref[step + 1], edge_t_ref[step + 1],
            pair_out, other_out,
        )
    square = jnp.concatenate(squares, axis=0).T[:ROWS]
    precision = param(3)
    maturities = wanted_ref.shape[1]
    weights = -0.5 * precision * square + 0.5 * maturities * jnp.log(precision)
    peak = jnp.max(weights, axis=1, keepdims=True)
    mass = jnp.sum(jnp.exp(weights - peak), axis=1, keepdims=True)
    lane = lax.broadcasted_iota(I32, (ROWS, LANES), 1)
    before = [stat_in[0], stat_in[1]] if step else [jnp.zeros((ROWS, LANES), F32)] * 2
    stats = [jnp.where(lane == step, new, old) for new, old in zip((peak, mass), before)]
    if last:
        rows = lax.broadcasted_iota(I32, (ROWS, 1), 0)
        vol_all = vol_before[...].astype(F32) if merge else jnp.zeros(vol_new.shape, F32)
        placed = [stat_before[0], stat_before[1]] if merge else [jnp.zeros((ROWS, LANES), F32)] * 2
        for b in range(batch):
            here = rows == meta_ref[0, first_place + b]
            vol_all = jnp.where(here, vol_new[b : b + 1], vol_all)
            placed = [jnp.where(here, new[b : b + 1], old) for new, old in zip(stats, placed)]
        vol_out[...] = vol_all.astype(BF16)
        stats = placed
    stat_ref[0] = stats[0]
    stat_ref[1] = stats[1]

def write_kernel(batches, meta_ref, *rest):
    clouds, (final_ref, sems) = rest[: len(batches)], rest[len(batches) :]
    copies = []
    for cloud, batch in zip(clouds, batches):
        for k, place in enumerate(batch):
            copy = pltpu.make_async_copy(
                cloud.at[k], final_ref.at[meta_ref[0, place]], sems.at[place]
            )
            copy.start()
            copies.append(copy)
    for copy in copies:
        copy.wait()


def join_kernel(finish, whole_rows, *refs):
    mine_ref, others, (out_ref,) = refs[0], refs[1:-1], refs[-1:]
    if finish:
        prior_ref, others = others[0], others[1:]
    peak, mass = mine_ref[0], mine_ref[1]
    for other in others:
        other_peak = other[0]
        top = jnp.maximum(peak, other_peak)
        mass = mass * jnp.exp(peak - top) + other[1] * jnp.exp(other_peak - top)
        peak = top
    if not finish:
        out_ref[0] = peak
        out_ref[1] = mass
        return
    lane = lax.broadcasted_iota(I32, (ROWS, LANES), 1)
    gained = peak + jnp.log(jnp.where(lane < STEPS, mass, 1.0)) - math.log(whole_rows)
    gained = jnp.sum(jnp.where(lane < STEPS, gained, 0.0), axis=1, keepdims=True)
    total = jnp.broadcast_to(prior_ref[:, :1] + gained, (ROWS, LANES))
    out_ref[...] = total.T[:1, :]


def join(stats, others, whole_rows, prior=None):
    operands = [stats] + ([] if prior is None else [prior]) + list(others)
    shape = stats.shape if prior is None else (1, ROWS)
    return call(
        functools.partial(join_kernel, prior is not None, whole_rows),
        jax.ShapeDtypeStruct(shape, F32),
        [vmem()] * len(operands),
        vmem(),
        "join",
        nbytes=1 << 14,
    )(*operands)


def swaps(count):
    rounds = []
    for offset in (0, 1):
        partner = [(i - offset ^ 1) + offset for i in range(count)]
        rounds.append([(i, p if 0 <= p < count else i) for i, p in enumerate(partner)])
    return rounds


def doubling(count):
    distance = 1
    while distance < count:
        yield distance, [(i, i ^ distance) for i in range(count)]
        distance *= 2


def prefix_counts(number):
    count, here = lax.axis_size("state"), lax.axis_index("state")
    if count & (count - 1):
        every = lax.all_gather(number, "state")
        before = jnp.arange(count) < here
        return jnp.sum(jnp.where(before[:, None, None], every, 0), axis=0)
    before, total = jnp.zeros_like(number), number
    for distance, pairs in doubling(count):
        other = lax.ppermute(total, "state", pairs)
        before = before + jnp.where((here & distance) != 0, other, 0)
        total = total + other
    return before


def combined_mass(stats, prior, whole_rows):
    count = lax.axis_size("state")
    if count & (count - 1):
        every = lax.all_gather(stats, "state")
        return join(every[0], [every[k] for k in range(1, count)], whole_rows, prior)
    if count == 1:
        return join(stats, [], whole_rows, prior)
    distances = [distance for distance, _ in doubling(count)]
    while distances:
        now, distances = distances[:1], distances[1:]
        apart = [sum(d for j, d in enumerate(now) if k >> j & 1) for k in range(1, 1 << len(now))]
        others = [lax.ppermute(stats, "state", [(i, i ^ d) for i in range(count)]) for d in apart]
        stats = join(stats, others, whole_rows, None if distances else prior)
    return stats


def local(
    states,
    log_vol,
    transition,
    loading,
    yields,
    state_noise,
    vol_noise,
    vol_mean,
    vol_persist,
    vol_scale,
    obs_prec,
    prior_loglik,
    ancestors,
    counts,
    local_anc,
):
    p_dev, s_dev, width = states.shape
    maturities = loading.shape[1]
    groups, shards = lax.axis_size("theta"), lax.axis_size("state")
    half = p_dev // 2
    margin = s_dev // 4
    batch = p_dev // 2
    batches = [tuple(range(q * batch, (q + 1) * batch)) for q in range(p_dev // batch)]
    vol_rows = s_dev // width
    ways = next(w for w in (2, 1) if half % w == 0 and shards % w == 0)
    per_part = half // ways

    early = half // 2
    relayed = groups == 4
    tail = -(-half * vol_rows // PAD) * PAD
    block = early * s_dev + tail
    near_rows = block + early * s_dev
    part_rows = per_part * width
    packed_shapes = [
        jax.ShapeDtypeStruct((rows, width), BF16)
        for rows in (near_rows + part_rows, block, block, part_rows)
    ]
    small = ancestors.shape
    first_hop, second_hop, third_hop, far_part, meta, cols, prior = call(
        functools.partial(pack_kernel, groups, relayed, batches, ways, vol_rows),
        packed_shapes
        + [
            jax.ShapeDtypeStruct((4, p_dev), I32),
            jax.ShapeDtypeStruct((len(batches), 4, ROWS, LANES), F32),
            jax.ShapeDtypeStruct((ROWS, LANES), F32),
        ],
        [anywhere()] * 9,
        [vmem()] * 4 + [smem(), vmem(), vmem()],
        "pack",
        [pltpu.SMEM(small, I32)]
        + [pltpu.SMEM(small, F32)] * 5
        + [
            pltpu.SMEM((2, half), I32),
            pltpu.VMEM((p_dev, s_dev), BF16),
            pltpu.SemaphoreType.DMA((7,)),
            pltpu.SemaphoreType.DMA((2, per_part)),
            pltpu.SemaphoreType.DMA((4, early)),
        ],
        nbytes=4 * half * s_dev * width * 2,
        limit=PACK_LIMIT,
    )(ancestors, vol_mean, vol_persist, vol_scale, obs_prec, prior_loglik, log_vol, states, transition)

    near_pairs, far_pairs = swaps(groups)
    far_part = lax.ppermute(far_part, "theta", far_pairs)
    near = lax.ppermute(first_hop, "theta", near_pairs)
    if relayed:
        cross_pairs = [(i, i ^ 2) for i in range(groups)]
        across = lax.ppermute(second_hop, "theta", cross_pairs)
        far_first = lax.ppermute(near[:block], "theta", cross_pairs)
        group = lax.axis_index("theta")
        inner = (group > 0) & (group < groups - 1)
        onward, local_anc = lax.optimization_barrier((jnp.where(inner, third_hop, across), local_anc))
        far_last = lax.ppermute(onward, "theta", near_pairs)
    else:
        far_first = lax.ppermute(second_hop, "theta", far_pairs)
        far_last = lax.ppermute(third_hop, "theta", far_pairs)

    vols_at = early * s_dev
    arrivals = [
        (near, 0, [(k // early) * block + (k % early) * s_dev for k in range(half)]),
        (far_first, half, [k * s_dev for k in range(early)]),
        (far_last, half + early, [k * s_dev for k in range(early)]),
    ]
    arrivals = [
        (x, tuple((p_dev + code + k, at, vols_at + k * vol_rows) for k, at in enumerate(rows)))
        for x, code, rows in arrivals
    ]

    number = counts[:, :, 0]
    first = prefix_counts(number)
    index_shapes = [
        jax.ShapeDtypeStruct((STEPS, ROWS, s_dev), I32),
        jax.ShapeDtypeStruct((STEPS, s_dev, ROWS), I32),
        jax.ShapeDtypeStruct((STEPS, ROWS, 2 * margin), I32),
        jax.ShapeDtypeStruct((STEPS, 2 * margin, ROWS), I32),
    ] * len(batches)
    indices = call(
        functools.partial(index_kernel, batches, s_dev, margin),
        index_shapes,
        [smem()] * 3 + [vmem()],
        [vmem()] * len(index_shapes),
        "indices",
        nbytes=1 << 18,
    )(meta, number, first, local_anc)

    pair_round, other_round = swaps(shards)
    edge_shape = jax.ShapeDtypeStruct((batch * margin + PAD, width), BF16)
    cloud_shape = jax.ShapeDtypeStruct((batch, s_dev, width), BF16)
    vol_shape = jax.ShapeDtypeStruct((ROWS, s_dev), F32)
    stat_shape = jax.ShapeDtypeStruct((2, ROWS, LANES), F32)
    before = []
    done_clouds = []
    follow = []
    for q in range(len(batches)):
        src, src_t, edge, edge_t = indices[4 * q : 4 * q + 4]
        recv, recv_slots = zip(*(arrivals if q else arrivals[:1]))
        cloud, vol, pair, other = call(
            functools.partial(fetch_kernel, batch, q * batch, margin, vol_rows, recv_slots),
            [cloud_shape, vol_shape, edge_shape, edge_shape],
            [smem(), hbm()] + [vmem()] * (3 + len(recv) + len(follow)),
            [vmem()] * 4,
            "fetch",
            [pltpu.VMEM((2 * p_dev, s_dev), F32), pltpu.SemaphoreType.DMA((batch,))],
            flops=2 * batch * 2 * margin * s_dev * width,
            nbytes=2 * batch * s_dev * width * 2,
        )(meta, states, log_vol, edge, edge_t, *recv, *follow)
        if q == 0:
            arrived, far_part, _ = lax.optimization_barrier((near, far_part, vol))
            gathered = jnp.concatenate([arrived[near_rows:], far_part])
            distance = ways // 2
            while distance:
                pairs = [(i, i ^ distance) for i in range(shards)]
                gathered = jnp.concatenate([gathered, lax.ppermute(gathered, "state", pairs)])
                distance //= 2
            gathered = gathered.reshape(2 * half, width, width)

            matrices = call(
                functools.partial(matrix_kernel, p_dev, ways),
                jax.ShapeDtypeStruct((p_dev, width, width), BF16),
                [smem(), hbm(), hbm()],
                vmem(),
                "matrices",
                [pltpu.SemaphoreType.DMA((p_dev,))],
                nbytes=p_dev * width * width * 4,
            )(meta, transition, gathered)
        stat = None
        for step in range(STEPS):
            last = step == STEPS - 1
            other_in = lax.ppermute(other, "state", other_round)
            pair_in = lax.ppermute(pair, "state", pair_round)
            own = call(
                functools.partial(own_kernel, batch, step, margin),
                cloud_shape,
                [vmem(), vmem()],
                vmem(),
                "own_rows",
                flops=2 * batch * s_dev * s_dev * width,
                nbytes=batch * s_dev * width * 4,
            )(src_t, cloud)
            operands = [
                cols[q], own, pair_in, other_in, vol, src, src_t, edge, edge_t, matrices,
                state_noise, vol_noise, loading, yields,
            ]
            specs = [vmem()] * len(operands)
            if step:
                operands.append(stat)
                specs.append(vmem())
            if last:
                operands += [meta] + before
                specs += [smem()] + [vmem()] * len(before)
                out_shape = [cloud_shape, jax.ShapeDtypeStruct(log_vol.shape, BF16), stat_shape]
                out_specs = [vmem()] * 3
            else:
                out_shape = [cloud_shape, vol_shape, stat_shape, edge_shape, edge_shape]
                out_specs = [vmem()] * 5
            results = call(
                functools.partial(step_kernel, batch, q * batch, step, margin, bool(before)),
                out_shape,
                specs,
                out_specs,
                "step",
                flops=2 * batch * s_dev * width * (width + maturities + margin),
                nbytes=batch * s_dev * width * 8,
            )(*operands)
            if last:
                cloud, *before = results
                done_clouds.append(cloud)
            else:
                cloud, vol, stat, pair, other = results
                follow = [stat] if step == 0 else follow
    vols, stats = before
    final = call(
        functools.partial(write_kernel, batches),
        jax.ShapeDtypeStruct(states.shape, BF16),
        [smem()] + [vmem()] * len(batches),
        anywhere(),
        "write",
        [pltpu.SemaphoreType.DMA((p_dev,))],
        nbytes=2 * p_dev * s_dev * width * 2,
    )(meta, *done_clouds)
    total = combined_mass(stats, prior, s_dev * shards)
    return (final, vols, total.reshape(p_dev))


def solution(mesh):
    placed = (
        P("theta", "state", None),
        P("theta", "state"),
        P("theta", None, None),
        P(),
        P(),
        P(None, "state", None),
        P(None, "state"),
        P(),
        P(),
        P(),
        P(),
        P(),
        P(),
        P(None, "theta", "state"),
        P(None, "theta", "state"),
    )
    return jax.shard_map(
        local,
        mesh=mesh,
        in_specs=placed,
        out_specs=(P("theta", "state", None), P("theta", "state"), P("theta")),
        check_vma=False,
    )
```

```python
import functools
import math

import jax
import jax.numpy as jnp
from jax import lax
from jax.experimental import pallas as pl
from jax.experimental.pallas import tpu as pltpu
from jax.sharding import PartitionSpec as P

STEPS = 3
LANES = 128
ROWS = 8
PAD = 16
VLIMIT = 8 * 1024 * 1024
PACK_LIMIT = 64 * 1024 * 1024

VM = pltpu.VMEM
SM = pltpu.SMEM
F32 = jnp.float32
BF16 = jnp.bfloat16
I32 = jnp.int32


def vmem():
    return pl.BlockSpec(memory_space=pltpu.VMEM)


def smem():
    return pl.BlockSpec(memory_space=pltpu.SMEM)


def anywhere():
    return pl.BlockSpec(memory_space=pl.ANY)


def hbm():
    return pl.BlockSpec(memory_space=pltpu.HBM)


def call(kernel, out_shape, in_specs, out_specs, name, scratch=(), flops=0, nbytes=0, aliases=None,
         limit=VLIMIT):
    return pl.pallas_call(
        kernel,
        out_shape=out_shape,
        in_specs=in_specs,
        out_specs=out_specs,
        scratch_shapes=list(scratch),
        input_output_aliases=aliases or {},
        compiler_params=pltpu.CompilerParams(vmem_limit_bytes=limit),
        cost_estimate=pl.CostEstimate(flops=flops // 64, bytes_accessed=nbytes // 64, transcendentals=0),
        name=name,
    )


def pack_kernel(groups, relayed, batches, ways, vol_rows, anc_hbm, *rest):
    tables_hbm, (vols_hbm, states_ref, transition_ref), rest = rest[:5], rest[5:8], rest[8:]
    first_out, second_out, third_out, part_out = rest[:4]
    rest = rest[4:]
    meta_ref, cols_ref, prior_ref, anc_ref, *rest = rest
    tables, (names, vols_ref, load_sems, part_sems, sems) = rest[:5], rest[5:]
    p_dev, s_dev, width = states_ref.shape
    half = p_dev // 2
    per_part = half // ways
    group, shard = lax.axis_index("theta"), lax.axis_index("state")
    loads = [(anc_hbm, anc_ref), (vols_hbm, vols_ref)] + list(zip(tables_hbm, tables))
    loads = [pltpu.make_async_copy(src, dst, load_sems.at[k]) for k, (src, dst) in enumerate(loads)]
    for load in loads:
        load.start()
    loads[0].wait()

    odd = lax.rem(group, 2)
    for side in range(2):
        other = group + (1 - 2 * odd if side == 0 else 2 * odd - 1)
        valid = (other >= 0) & (other < groups)
        other = jnp.clip(other, 0, groups - 1)
        for k in range(half):
            names[side, k] = 0
        rank = jnp.int32(0)
        for i in range(p_dev):
            a = anc_ref[other * p_dev + i]
            hit = valid & (lax.div(a, p_dev) == group) & (rank < half)

            @pl.when(hit)
            def _(side=side, rank=rank, a=a):
                names[side, rank] = lax.rem(a, p_dev)

            rank = rank + hit.astype(I32)

    early = half // 2
    inner = (group > 0) & (group < groups - 1)
    if relayed:
        takes = [((1, 0), (0, 0)), ((0, 0), (0, early)), ((1, early), (0, 0)), ((0, early), (0, 0))]
    else:
        takes = [((0, 0),) * 2, ((0, early),) * 2, ((1, 0),) * 2, ((1, early),) * 2]
    takes = [
        (jnp.where(inner, ours[0], theirs[0]), jnp.where(inner, ours[1], theirs[1]))
        for ours, theirs in takes
    ]
    copies = []
    tail = -(-half * vol_rows // PAD) * PAD
    block = early * s_dev + tail
    outs = [(first_out, 0), (first_out, block), (second_out, 0), (third_out, 0)]
    for hop, ((out, at), (side, first)) in enumerate(zip(outs, takes)):
        for k in range(early):
            copies.append(
                pltpu.make_async_copy(
                    states_ref.at[names[side, first + k]],
                    out.at[pl.ds(at + k * s_dev, s_dev)],
                    sems.at[hop, k],
                )
            )
    for side in range(2):
        parts, at = (first_out, block + early * s_dev) if side == 0 else (part_out, 0)
        for k in range(per_part):
            copies.append(
                pltpu.make_async_copy(
                    transition_ref.at[names[side, lax.rem(shard, ways) * per_part + k]],
                    parts.at[pl.ds(at + k * width, width)],
                    part_sems.at[side, k],
                )
            )
    for copy in copies:
        copy.start()

    for load in loads[1:]:
        load.wait()
    rows = lax.broadcasted_iota(I32, (p_dev, 1), 0)
    table = vols_ref[...].astype(F32)
    for out, hops in ((first_out, takes[:2]), (second_out, takes[2:3]), (third_out, takes[3:])):
        pieces = []
        for side, first in hops:
            for k in range(early):
                here = rows == names[side, first + k]
                row = jnp.sum(jnp.where(here, table, 0.0), axis=0, keepdims=True)
                pieces += [row[:, r * width : (r + 1) * width] for r in range(vol_rows)]
        pieces += [jnp.zeros((1, width), F32)] * (tail - len(pieces))
        out[pl.ds(early * s_dev, tail), :] = jnp.concatenate(pieces, axis=0).astype(BF16)

    even = odd == 0
    rank_near, rank_far = jnp.int32(0), jnp.int32(0)
    front, back = jnp.int32(0), jnp.int32(p_dev - 1)
    for i in range(p_dev):
        a = anc_ref[group * p_dev + i]
        offset = lax.div(a, p_dev) - group
        near = jnp.where(even, offset == 1, offset == -1)
        far = jnp.where(even, offset == -1, offset == 1)
        late = far
        came = rank_near
        if relayed:
            late = far | (near & ~inner)
            came = jnp.where(inner, rank_near, rank_near + jnp.where(rank_near < early, early, half))
        came = jnp.where(far, half + rank_far, came)
        moved = jnp.where(far, half + rank_far, rank_near)
        position = jnp.where(late, back, front)
        meta_ref[0, position] = i
        meta_ref[1, position] = jnp.where(near | far, p_dev + came, lax.rem(a, p_dev))
        meta_ref[2, position] = a
        meta_ref[3, position] = jnp.where(near | far, p_dev + moved, lax.rem(a, p_dev))
        front = front + jnp.where(late, 0, 1)
        back = back - jnp.where(late, 1, 0)
        rank_near = rank_near + near.astype(I32)
        rank_far = rank_far + far.astype(I32)
    for q, batch in enumerate(batches):
        for k in range(4):
            value = column([tables[k][meta_ref[2, batch[b % len(batch)]]] for b in range(ROWS)])
            cols_ref[q, k] = jnp.broadcast_to(value, (ROWS, LANES))
    prior = column([tables[4][anc_ref[group * p_dev + i]] for i in range(p_dev)])
    prior_ref[...] = jnp.broadcast_to(prior, (ROWS, LANES))
    for copy in copies:
        copy.wait()


def lane_pick(blocks, index):
    low = index & (LANES - 1)
    high = index >> 7
    out = None
    for k, block in blocks:
        got = jnp.take_along_axis(block, low, axis=1, mode="promise_in_bounds")
        out = got if out is None else jnp.where(high == k, got, out)
    return out


def column(scalars):
    rows = lax.broadcasted_iota(I32, (ROWS, 1), 0)
    out = jnp.zeros((ROWS, 1), scalars[0].dtype)
    for b, scalar in enumerate(scalars):
        out = jnp.where(rows == b, scalar, out)
    return out


def index_kernel(batches, s_dev, margin, meta_ref, count_ref, first_ref, anc_ref,
                 states_ref, vols_ref, *outs):
    *outs, table, sems = outs
    bases, outs = outs[: 2 * len(batches)], outs[2 * len(batches) :]
    p_dev = states_ref.shape[0]
    for q, batch in enumerate(batches):
        for k, at in enumerate(batch):
            place = meta_ref[1, at]

            @pl.when(place < p_dev)
            def _(k=k, at=at, place=place, out=bases[2 * q]):
                pltpu.make_async_copy(
                    states_ref.at[jnp.minimum(place, p_dev - 1)], out.at[k], sems.at[at]
                ).start()

    table[...] = vols_ref[...].astype(F32)
    for q, batch in enumerate(batches):
        places = [jnp.minimum(meta_ref[1, batch[b % len(batch)]], p_dev - 1) for b in range(ROWS)]
        bases[2 * q + 1][...] = jnp.concatenate([table[pl.ds(p, 1), :] for p in places], axis=0)
    shard = lax.axis_index("state")
    base = shard * s_dev
    even = lax.rem(shard, 2) == 0
    lanes = lax.broadcasted_iota(I32, (ROWS, LANES), 1)
    for q, batch in enumerate(batches):
        src_ref, src_t_ref, edge_ref, edge_t_ref = outs[4 * q : 4 * q + 4]
        for step in range(STEPS):
            who = [meta_ref[0, batch[b % len(batch)]] for b in range(ROWS)]
            chosen = jnp.concatenate([anc_ref[step, pl.ds(i, 1), :] for i in who], axis=0)
            blocks = [chosen[:, k * LANES : (k + 1) * LANES] for k in range(chosen.shape[1] // LANES)]
            count = column([count_ref[step, i] for i in who])
            shift = column([base - first_ref[step, i] for i in who])
            sources = []
            for o in range(s_dev // LANES):
                relative = o * LANES + lanes + shift
                own = lane_pick(list(enumerate(blocks)), jnp.clip(relative, 0, chosen.shape[1] - 1))
                sources.append(
                    jnp.where(
                        relative < 0,
                        relative + margin,
                        jnp.where(relative < count, margin + own, margin + s_dev + relative - count),
                    )
                )
            source = jnp.concatenate(sources, axis=1)
            src_ref[step] = source
            src_t_ref[step] = source.T
            head = jnp.concatenate(blocks[: margin // LANES], axis=1)
            tail = [
                lane_pick(list(enumerate(blocks)), count - margin + o * LANES + lanes)
                for o in range(margin // LANES)
            ]
            tail = jnp.concatenate(tail, axis=1)
            edge = jnp.concatenate([jnp.where(even, tail, head), jnp.where(even, head, tail)], axis=1)
            edge_ref[step] = edge
            edge_t_ref[step] = edge.T
    for q, batch in enumerate(batches):
        for k, at in enumerate(batch):

            @pl.when(meta_ref[1, at] < p_dev)
            def _(k=k, at=at, out=bases[2 * q]):
                pltpu.make_async_copy(states_ref.at[0], out.at[k], sems.at[at]).wait()


def one_hot(index, columns):
    index = index.astype(jnp.int16)
    lanes = lax.broadcasted_iota(jnp.int16, (index.shape[0], columns), 1)
    return jnp.where(index == lanes, BF16(1), BF16(0))


def send_edges(batch, margin, cloud_at, vol, edge, edge_t, pair_ref, other_ref):
    s_dev = vol.shape[1]
    blocks = [(k, vol[:, k * LANES : (k + 1) * LANES]) for k in range(s_dev // LANES)]
    width = pair_ref.shape[1]
    for out, start in ((pair_ref, 0), (other_ref, margin)):
        picked = [
            lane_pick(blocks, edge[:, start + o * LANES : start + (o + 1) * LANES])
            for o in range(margin // LANES)
        ]
        picked.append(jnp.zeros((ROWS, width - margin), F32))
        flat = jnp.concatenate(picked, axis=1)
        flat = jnp.concatenate([flat, jnp.zeros((PAD - ROWS, width), F32)], axis=0)
        out[pl.ds(batch * margin, PAD), :] = flat.astype(BF16)
    for b in range(batch):
        rows = jnp.dot(
            one_hot(edge_t[:, b : b + 1], s_dev), cloud_at(b), preferred_element_type=F32
        ).astype(BF16)
        pair_ref[pl.ds(b * margin, margin), :] = rows[:margin]
        other_ref[pl.ds(b * margin, margin), :] = rows[margin:]


def fetch_kernel(batch, first_place, p_dev, margin, vol_rows, recv_slots, meta_ref, base_ref, base_vol_ref,
                 edge_ref, edge_t_ref, *rest):
    recv = rest[: len(recv_slots)]
    cloud_ref, vol_ref, pair_ref, other_ref, table, sems = rest[-6:]
    s_dev = vol_ref.shape[1]
    places = [meta_ref[1, first_place + b % batch] for b in range(ROWS)]
    for b in range(batch):
        for ref, codes in zip(recv, recv_slots):
            for code, at, _ in codes:

                @pl.when(places[b] == code)
                def _(b=b, ref=ref, at=at):
                    pltpu.make_async_copy(
                        ref.at[pl.ds(at, s_dev)], cloud_ref.at[b], sems.at[b]
                    ).start()

    table[...] = jnp.zeros(table.shape, F32)
    for ref, codes in zip(recv, recv_slots):
        start = codes[0][2]
        length = -(-len(codes) * vol_rows // PAD) * PAD
        rows = ref[pl.ds(start, length), :].astype(F32)
        for code, _, at in codes:
            pieces = [rows[at - start + r : at - start + r + 1] for r in range(vol_rows)]
            table[pl.ds(code, 1), :] = jnp.concatenate(pieces, axis=1)
    vol = jnp.concatenate([table[pl.ds(place, 1), :] for place in places], axis=0)
    vol = jnp.where(column(places) < p_dev, base_vol_ref[...], vol)
    vol_ref[...] = vol
    for b in range(batch):

        @pl.when(places[b] >= p_dev)
        def _(b=b):
            pltpu.make_async_copy(recv[0].at[pl.ds(0, s_dev)], cloud_ref.at[b], sems.at[b]).wait()

    send_edges(batch, margin, lambda b: cloud_ref[b], vol, edge_ref[0], edge_t_ref[0], pair_ref, other_ref)


def matrix_kernel(batch, first_place, half, ways, sides, meta_ref, transition_ref, *rest):
    pieces, (out_ref, sems) = rest[: sides * ways], rest[-2:]
    p_dev, width, _ = transition_ref.shape
    per_part = half // ways
    mine = lax.rem(lax.axis_index("state"), ways)
    for b in range(batch):
        place = meta_ref[3, first_place + b]
        moved = jnp.maximum(place - p_dev, 0)
        slot = lax.rem(moved, half)
        chosen = jnp.where(place < p_dev, -1, lax.div(moved, half) * ways + (lax.div(slot, per_part) ^ mine))

        @pl.when(place < p_dev)
        def _(b=b, place=place):
            pltpu.make_async_copy(
                transition_ref.at[jnp.minimum(place, p_dev - 1)], out_ref.at[b], sems.at[b]
            ).start()

        for k, piece in enumerate(pieces):

            @pl.when(chosen == k)
            def _(b=b, piece=piece, slot=slot):
                at = pl.multiple_of(lax.rem(slot, per_part) * width, width)
                pltpu.make_async_copy(piece.at[pl.ds(at, width)], out_ref.at[b], sems.at[b]).start()

    for b in range(batch):
        pltpu.make_async_copy(transition_ref.at[0], out_ref.at[b], sems.at[b]).wait()


def own_kernel(batch, step, margin, src_t_ref, cloud_ref, out_ref):
    s_dev = cloud_ref.shape[1]
    for b in range(batch):
        index = src_t_ref[step][:, b : b + 1] - margin
        out_ref[b] = jnp.dot(
            one_hot(index, s_dev), cloud_ref[b], preferred_element_type=F32
        ).astype(BF16)


def step_kernel(batch, first_place, step, margin, merge, cols_ref, own_ref, pair_ref, other_ref, vol_ref,
                src_ref, src_t_ref, edge_ref, edge_t_ref, matrix_ref, noise_ref, vnoise_ref,
                loading_ref, wanted_ref, *rest):
    last = step == STEPS - 1
    s_dev = vol_ref.shape[1]
    rest = list(rest)
    stat_in = rest.pop(0) if step else None
    if last:
        meta_ref = rest.pop(0)
        if merge:
            vol_before, stat_before = rest[:2]
            rest = rest[2:]
        cloud_out, vol_out, stat_ref = rest
    else:
        cloud_out, vol_out, stat_ref, pair_out, other_out = rest
    even = lax.rem(lax.axis_index("state"), 2) == 0
    source = src_ref[step]
    vol = vol_ref[...]
    blocks = [(k, vol[:, k * LANES : (k + 1) * LANES]) for k in range(s_dev // LANES)]

    def edge_vols(ref):
        return ref[pl.ds(batch * margin, PAD), :].astype(F32)[:ROWS]

    pair_v, other_v = edge_vols(pair_ref), edge_vols(other_ref)
    low_v, high_v = jnp.where(even, other_v, pair_v), jnp.where(even, pair_v, other_v)
    picked = []
    for o in range(s_dev // LANES):
        index = source[:, o * LANES : (o + 1) * LANES]
        own = lane_pick(blocks, jnp.clip(index - margin, 0, s_dev - 1))
        if o < margin // LANES:
            low = [(k, low_v[:, k * LANES : (k + 1) * LANES]) for k in range(margin // LANES)]
            own = jnp.where(index < margin, lane_pick(low, index), own)
        if o >= (s_dev - margin) // LANES:
            high = [(k, high_v[:, k * LANES : (k + 1) * LANES]) for k in range(margin // LANES)]
            above = jnp.clip(index - margin - s_dev, 0, margin - 1)
            own = jnp.where(index >= margin + s_dev, lane_pick(high, above), own)
        picked.append(own)
    picked = jnp.concatenate(picked, axis=1)

    def param(k):
        return cols_ref[k][:, :1]

    center, persist, spread = param(0), param(1), param(2)
    h = center + persist * (picked - center) + spread * vnoise_ref[pl.ds(step, 1), :]
    scale_t = jnp.exp(0.5 * h).T
    vol_new = h.astype(BF16).astype(F32)
    if not last:
        vol_out[...] = vol_new

    wanted = wanted_ref[pl.ds(step, 1), :]
    tile = s_dev // 2
    lanes = lax.broadcasted_iota(I32, (tile, LANES), 1)
    squares = [jnp.zeros((tile, LANES), F32)] * 2
    for b in range(batch):
        for r in range(2):
            span = pl.ds(r * tile, tile)
            index = src_t_ref[step, span, :][:, b : b + 1]
            own = own_ref[b, span, :]
            pair, other = pair_ref[pl.ds(b * margin, margin), :], other_ref[pl.ds(b * margin, margin), :]
            if r == 0:
                patch = jnp.dot(
                    one_hot(index[:margin], margin),
                    jnp.where(even, other, pair),
                    preferred_element_type=F32,
                )
                cloud = jnp.concatenate(
                    [(own[:margin].astype(F32) + patch).astype(BF16), own[margin:]], axis=0
                )
            else:
                patch = jnp.dot(
                    one_hot(index[tile - margin :] - (margin + s_dev), margin),
                    jnp.where(even, pair, other),
                    preferred_element_type=F32,
                )
                cloud = jnp.concatenate(
                    [own[: tile - margin], (own[tile - margin :].astype(F32) + patch).astype(BF16)],
                    axis=0,
                )
            drift = jnp.dot(cloud, matrix_ref[b], preferred_element_type=F32)
            noise = noise_ref[step, span, :].astype(F32)
            cloud = (drift + scale_t[r * tile : (r + 1) * tile, b : b + 1] * noise).astype(BF16)
            cloud_out[b, span, :] = cloud
            misfit = wanted - jnp.dot(cloud, loading_ref[...], preferred_element_type=F32)
            square = jnp.sum(misfit * misfit, axis=1, keepdims=True)
            squares[r] = jnp.where(lanes == b, square, squares[r])
    if not last:
        send_edges(
            batch, margin, lambda b: cloud_out[b], vol_new, edge_ref[step + 1], edge_t_ref[step + 1],
            pair_out, other_out,
        )
    square = jnp.concatenate(squares, axis=0).T[:ROWS]
    precision = param(3)
    maturities = wanted_ref.shape[1]
    weights = -0.5 * precision * square + 0.5 * maturities * jnp.log(precision)
    peak = jnp.max(weights, axis=1, keepdims=True)
    mass = jnp.sum(jnp.exp(weights - peak), axis=1, keepdims=True)
    lane = lax.broadcasted_iota(I32, (ROWS, LANES), 1)
    before = [stat_in[0], stat_in[1]] if step else [jnp.zeros((ROWS, LANES), F32)] * 2
    stats = [jnp.where(lane == step, new, old) for new, old in zip((peak, mass), before)]
    if last:
        rows = lax.broadcasted_iota(I32, (ROWS, 1), 0)
        vol_all = vol_before[...].astype(F32) if merge else jnp.zeros(vol_new.shape, F32)
        placed = [stat_before[0], stat_before[1]] if merge else [jnp.zeros((ROWS, LANES), F32)] * 2
        for b in range(batch):
            here = rows == meta_ref[0, first_place + b]
            vol_all = jnp.where(here, vol_new[b : b + 1], vol_all)
            placed = [jnp.where(here, new[b : b + 1], old) for new, old in zip(stats, placed)]
        vol_out[...] = vol_all.astype(BF16)
        stats = placed
    stat_ref[0] = stats[0]
    stat_ref[1] = stats[1]

def write_kernel(batches, meta_ref, *rest):
    clouds, (final_ref, sems) = rest[: len(batches)], rest[len(batches) :]
    copies = []
    for cloud, batch in zip(clouds, batches):
        for k, place in enumerate(batch):
            copy = pltpu.make_async_copy(
                cloud.at[k], final_ref.at[meta_ref[0, place]], sems.at[place]
            )
            copy.start()
            copies.append(copy)
    for copy in copies:
        copy.wait()


def join_kernel(finish, whole_rows, *refs):
    mine_ref, others, (out_ref,) = refs[0], refs[1:-1], refs[-1:]
    if finish:
        prior_ref, others = others[0], others[1:]
    peak, mass = mine_ref[0], mine_ref[1]
    for other in others:
        other_peak = other[0]
        top = jnp.maximum(peak, other_peak)
        mass = mass * jnp.exp(peak - top) + other[1] * jnp.exp(other_peak - top)
        peak = top
    if not finish:
        out_ref[0] = peak
        out_ref[1] = mass
        return
    lane = lax.broadcasted_iota(I32, (ROWS, LANES), 1)
    gained = peak + jnp.log(jnp.where(lane < STEPS, mass, 1.0)) - math.log(whole_rows)
    gained = jnp.sum(jnp.where(lane < STEPS, gained, 0.0), axis=1, keepdims=True)
    total = jnp.broadcast_to(prior_ref[:, :1] + gained, (ROWS, LANES))
    out_ref[...] = total.T[:1, :]


def join(stats, others, whole_rows, prior=None):
    operands = [stats] + ([] if prior is None else [prior]) + list(others)
    shape = stats.shape if prior is None else (1, ROWS)
    return call(
        functools.partial(join_kernel, prior is not None, whole_rows),
        jax.ShapeDtypeStruct(shape, F32),
        [vmem()] * len(operands),
        vmem(),
        "join",
        nbytes=1 << 14,
    )(*operands)


def swaps(count):
    rounds = []
    for offset in (0, 1):
        partner = [(i - offset ^ 1) + offset for i in range(count)]
        rounds.append([(i, p if 0 <= p < count else i) for i, p in enumerate(partner)])
    return rounds


def doubling(count):
    distance = 1
    while distance < count:
        yield distance, [(i, i ^ distance) for i in range(count)]
        distance *= 2


def prefix_counts(number):
    count, here = lax.axis_size("state"), lax.axis_index("state")
    if count & (count - 1):
        every = lax.all_gather(number, "state")
        before = jnp.arange(count) < here
        return jnp.sum(jnp.where(before[:, None, None], every, 0), axis=0)
    before, total = jnp.zeros_like(number), number
    for distance, pairs in doubling(count):
        other = lax.ppermute(total, "state", pairs)
        before = before + jnp.where((here & distance) != 0, other, 0)
        total = total + other
    return before


def combined_mass(stats, prior, whole_rows):
    count = lax.axis_size("state")
    if count & (count - 1):
        every = lax.all_gather(stats, "state")
        return join(every[0], [every[k] for k in range(1, count)], whole_rows, prior)
    if count == 1:
        return join(stats, [], whole_rows, prior)
    distances = [distance for distance, _ in doubling(count)]
    size = 1
    while distances:
        now, distances = distances[:size], distances[size:]
        size = 2
        apart = [sum(d for j, d in enumerate(now) if k >> j & 1) for k in range(1, 1 << len(now))]
        others = [lax.ppermute(stats, "state", [(i, i ^ d) for i in range(count)]) for d in apart]
        stats = join(stats, others, whole_rows, None if distances else prior)
    return stats


def local(
    states,
    log_vol,
    transition,
    loading,
    yields,
    state_noise,
    vol_noise,
    vol_mean,
    vol_persist,
    vol_scale,
    obs_prec,
    prior_loglik,
    ancestors,
    counts,
    local_anc,
):
    p_dev, s_dev, width = states.shape
    maturities = loading.shape[1]
    groups, shards = lax.axis_size("theta"), lax.axis_size("state")
    half = p_dev // 2
    margin = s_dev // 4
    batch = p_dev // 2
    batches = [tuple(range(q * batch, (q + 1) * batch)) for q in range(p_dev // batch)]
    vol_rows = s_dev // width
    ways = next(w for w in (2, 1) if half % w == 0 and shards % w == 0)
    per_part = half // ways

    early = half // 2
    relayed = groups == 4
    tail = -(-half * vol_rows // PAD) * PAD
    block = early * s_dev + tail
    near_rows = block + early * s_dev
    part_rows = per_part * width
    packed_shapes = [
        jax.ShapeDtypeStruct((rows, width), BF16)
        for rows in (near_rows + part_rows, block, block, part_rows)
    ]
    small = ancestors.shape
    first_hop, second_hop, third_hop, far_part, meta, cols, prior = call(
        functools.partial(pack_kernel, groups, relayed, batches, ways, vol_rows),
        packed_shapes
        + [
            jax.ShapeDtypeStruct((4, p_dev), I32),
            jax.ShapeDtypeStruct((len(batches), 4, ROWS, LANES), F32),
            jax.ShapeDtypeStruct((ROWS, LANES), F32),
        ],
        [anywhere()] * 9,
        [vmem()] * 4 + [smem(), vmem(), vmem()],
        "pack",
        [pltpu.SMEM(small, I32)]
        + [pltpu.SMEM(small, F32)] * 5
        + [
            pltpu.SMEM((2, half), I32),
            pltpu.VMEM((p_dev, s_dev), BF16),
            pltpu.SemaphoreType.DMA((7,)),
            pltpu.SemaphoreType.DMA((2, per_part)),
            pltpu.SemaphoreType.DMA((4, early)),
        ],
        nbytes=4 * half * s_dev * width * 2,
        limit=PACK_LIMIT,
    )(ancestors, vol_mean, vol_persist, vol_scale, obs_prec, prior_loglik, log_vol, states, transition)

    near_pairs, far_pairs = swaps(groups)
    far_part = lax.ppermute(far_part, "theta", far_pairs)
    near = lax.ppermute(first_hop, "theta", near_pairs)
    if relayed:
        cross_pairs = [(i, i ^ 2) for i in range(groups)]
        across = lax.ppermute(second_hop, "theta", cross_pairs)
        group = lax.axis_index("theta")
        inner = (group > 0) & (group < groups - 1)
        onward, local_anc = lax.optimization_barrier((jnp.where(inner, third_hop, across), local_anc))
        far_last = lax.ppermute(onward, "theta", near_pairs)
    else:
        far_first = lax.ppermute(second_hop, "theta", far_pairs)
        far_last = lax.ppermute(third_hop, "theta", far_pairs)

    number = counts[:, :, 0]
    first = prefix_counts(number)
    cloud_shape = jax.ShapeDtypeStruct((batch, s_dev, width), BF16)
    vol_shape = jax.ShapeDtypeStruct((ROWS, s_dev), F32)
    index_shapes = [cloud_shape, vol_shape] * len(batches) + [
        jax.ShapeDtypeStruct((STEPS, ROWS, s_dev), I32),
        jax.ShapeDtypeStruct((STEPS, s_dev, ROWS), I32),
        jax.ShapeDtypeStruct((STEPS, ROWS, 2 * margin), I32),
        jax.ShapeDtypeStruct((STEPS, 2 * margin, ROWS), I32),
    ] * len(batches)
    indices = call(
        functools.partial(index_kernel, batches, s_dev, margin),
        index_shapes,
        [smem()] * 3 + [vmem(), anywhere(), vmem()],
        [vmem()] * len(index_shapes),
        "indices",
        [pltpu.VMEM((p_dev, s_dev), F32), pltpu.SemaphoreType.DMA((p_dev,))],
        nbytes=1 << 18,
    )(meta, number, first, local_anc, states, log_vol)
    bases, indices = indices[: 2 * len(batches)], indices[2 * len(batches) :]

    near, _ = lax.optimization_barrier((near, indices[-1]))
    if relayed:
        far_first = lax.ppermute(near[:block], "theta", cross_pairs)

    vols_at = early * s_dev
    arrivals = [
        (near, 0, [(k // early) * block + (k % early) * s_dev for k in range(half)]),
        (far_first, half, [k * s_dev for k in range(early)]),
        (far_last, half + early, [k * s_dev for k in range(early)]),
    ]
    arrivals = [
        (x, tuple((p_dev + code + k, at, vols_at + k * vol_rows) for k, at in enumerate(rows)))
        for x, code, rows in arrivals
    ]

    pair_round, other_round = swaps(shards)
    edge_shape = jax.ShapeDtypeStruct((batch * margin + PAD, width), BF16)
    stat_shape = jax.ShapeDtypeStruct((2, ROWS, LANES), F32)
    before = []
    done_clouds = []
    pieces = []
    follow = []
    for q in range(len(batches)):
        src, src_t, edge, edge_t = indices[4 * q : 4 * q + 4]
        recv, recv_slots = zip(*(arrivals if q else arrivals[:1]))
        cloud, vol, pair, other = call(
            functools.partial(fetch_kernel, batch, q * batch, p_dev, margin, vol_rows, recv_slots),
            [cloud_shape, vol_shape, edge_shape, edge_shape],
            [smem()] + [vmem()] * (4 + len(recv) + len(follow)),
            [vmem()] * 4,
            "fetch",
            [pltpu.VMEM((2 * p_dev, s_dev), F32), pltpu.SemaphoreType.DMA((batch,))],
            flops=2 * batch * 2 * margin * s_dev * width,
            nbytes=2 * batch * s_dev * width * 2,
            aliases={1: 0},
        )(meta, *bases[2 * q : 2 * q + 2], edge, edge_t, *recv, *follow)
        stat = None
        for step in range(STEPS):
            last = step == STEPS - 1
            other_in = lax.ppermute(other, "state", other_round)
            pair_in = lax.ppermute(pair, "state", pair_round)
            own = call(
                functools.partial(own_kernel, batch, step, margin),
                cloud_shape,
                [vmem(), vmem()],
                vmem(),
                "own_rows",
                flops=2 * batch * s_dev * s_dev * width,
                nbytes=batch * s_dev * width * 4,
            )(src_t, cloud)
            if step == 0:
                if q == 0:
                    part = near[near_rows:]
                else:
                    part, _ = lax.optimization_barrier((far_part, *follow))
                pieces.append(part)
                if ways == 2:
                    pieces.append(lax.ppermute(part, "state", [(i, i ^ 1) for i in range(shards)]))
                matrices = call(
                    functools.partial(matrix_kernel, batch, q * batch, half, ways, q + 1),
                    jax.ShapeDtypeStruct((batch, width, width), BF16),
                    [smem()] + [anywhere()] * (1 + len(pieces)),
                    vmem(),
                    "matrices",
                    [pltpu.SemaphoreType.DMA((batch,))],
                    nbytes=batch * width * width * 4,
                )(meta, transition, *pieces)
            operands = [
                cols[q], own, pair_in, other_in, vol, src, src_t, edge, edge_t, matrices,
                state_noise, vol_noise, loading, yields,
            ]
            specs = [vmem()] * len(operands)
            if step:
                operands.append(stat)
                specs.append(vmem())
            if last:
                operands += [meta] + before
                specs += [smem()] + [vmem()] * len(before)
                out_shape = [cloud_shape, jax.ShapeDtypeStruct(log_vol.shape, BF16), stat_shape]
                out_specs = [vmem()] * 3
            else:
                out_shape = [cloud_shape, vol_shape, stat_shape, edge_shape, edge_shape]
                out_specs = [vmem()] * 5
            results = call(
                functools.partial(step_kernel, batch, q * batch, step, margin, bool(before)),
                out_shape,
                specs,
                out_specs,
                "step",
                flops=2 * batch * s_dev * width * (width + maturities + margin),
                nbytes=batch * s_dev * width * 8,
            )(*operands)
            if last:
                cloud, *before = results
                done_clouds.append(cloud)
            else:
                cloud, vol, stat, pair, other = results
                follow = [stat] if step == 0 else follow
    vols, stats = before
    final = call(
        functools.partial(write_kernel, batches),
        jax.ShapeDtypeStruct(states.shape, BF16),
        [smem()] + [vmem()] * len(batches),
        anywhere(),
        "write",
        [pltpu.SemaphoreType.DMA((p_dev,))],
        nbytes=2 * p_dev * s_dev * width * 2,
    )(meta, *done_clouds)
    total = combined_mass(stats, prior, s_dev * shards)
    return (final, vols, total.reshape(p_dev))


def solution(mesh):
    placed = (
        P("theta", "state", None),
        P("theta", "state"),
        P("theta", None, None),
        P(),
        P(),
        P(None, "state", None),
        P(None, "state"),
        P(),
        P(),
        P(),
        P(),
        P(),
        P(),
        P(None, "theta", "state"),
        P(None, "theta", "state"),
    )
    return jax.shard_map(
        local,
        mesh=mesh,
        in_specs=placed,
        out_specs=(P("theta", "state", None), P("theta", "state"), P("theta")),
        check_vma=False,
    )
```

```python
import functools
import math

import jax
import jax.numpy as jnp
from jax import lax
from jax.experimental import pallas as pl
from jax.experimental.pallas import tpu as pltpu
from jax.sharding import PartitionSpec as P

STEPS = 3
LANES = 128
ROWS = 8
PAD = 16
VLIMIT = 8 * 1024 * 1024
PACK_LIMIT = 64 * 1024 * 1024

VM = pltpu.VMEM
SM = pltpu.SMEM
F32 = jnp.float32
BF16 = jnp.bfloat16
I32 = jnp.int32


def vmem():
    return pl.BlockSpec(memory_space=pltpu.VMEM)


def smem():
    return pl.BlockSpec(memory_space=pltpu.SMEM)


def anywhere():
    return pl.BlockSpec(memory_space=pl.ANY)


def hbm():
    return pl.BlockSpec(memory_space=pltpu.HBM)


def call(kernel, out_shape, in_specs, out_specs, name, scratch=(), flops=0, nbytes=0, aliases=None,
         limit=VLIMIT):
    return pl.pallas_call(
        kernel,
        out_shape=out_shape,
        in_specs=in_specs,
        out_specs=out_specs,
        scratch_shapes=list(scratch),
        input_output_aliases=aliases or {},
        compiler_params=pltpu.CompilerParams(vmem_limit_bytes=limit),
        cost_estimate=pl.CostEstimate(flops=flops // 64, bytes_accessed=nbytes // 64, transcendentals=0),
        name=name,
    )


def find_names(groups, p_dev, anc_ref, names):
    half = p_dev // 2
    group = lax.axis_index("theta")
    odd = lax.rem(group, 2)
    for side in range(2):
        other = group + (1 - 2 * odd if side == 0 else 2 * odd - 1)
        valid = (other >= 0) & (other < groups)
        other = jnp.clip(other, 0, groups - 1)
        for k in range(half):
            names[side, k] = 0
        rank = jnp.int32(0)
        for i in range(p_dev):
            a = anc_ref[other * p_dev + i]
            hit = valid & (lax.div(a, p_dev) == group) & (rank < half)

            @pl.when(hit)
            def _(side=side, rank=rank, a=a):
                names[side, rank] = lax.rem(a, p_dev)

            rank = rank + hit.astype(I32)


def taken(groups, take):
    group = lax.axis_index("theta")
    inner = (group > 0) & (group < groups - 1)
    (our_side, our_first), (their_side, their_first) = take
    return jnp.where(inner, our_side, their_side), jnp.where(inner, our_first, their_first)


def cloud_copies(early, names, states_ref, out, side, first, sems):
    s_dev = states_ref.shape[1]
    return [
        pltpu.make_async_copy(
            states_ref.at[names[side, first + k]], out.at[pl.ds(k * s_dev, s_dev)], sems.at[k]
        )
        for k in range(early)
    ]


def add_vols(early, tail, vol_rows, names, table, out, side, first, s_dev):
    width = out.shape[1]
    rows = lax.broadcasted_iota(I32, (table.shape[0], 1), 0)
    pieces = []
    for k in range(early):
        here = rows == names[side, first + k]
        row = jnp.sum(jnp.where(here, table, 0.0), axis=0, keepdims=True)
        pieces += [row[:, r * width : (r + 1) * width] for r in range(vol_rows)]
    pieces += [jnp.zeros((1, width), F32)] * (tail - len(pieces))
    out[pl.ds(early * s_dev, tail), :] = jnp.concatenate(pieces, axis=0).astype(BF16)


def pack_kernel(groups, relayed, takes, tail, batches, ways, vol_rows, anc_hbm, *rest):
    tables_hbm, (vols_hbm, states_ref, transition_ref), rest = rest[:5], rest[5:8], rest[8:]
    *hop_outs, part_out = rest[:5]
    rest = rest[5:]
    meta_ref, cols_ref, prior_ref, anc_ref, *rest = rest
    tables, (names, vols_ref, load_sems, part_sems, sems) = rest[:5], rest[5:]
    p_dev, s_dev, width = states_ref.shape
    half = p_dev // 2
    early = half // 2
    per_part = half // ways
    group, shard = lax.axis_index("theta"), lax.axis_index("state")
    loads = [(anc_hbm, anc_ref), (vols_hbm, vols_ref)] + list(zip(tables_hbm, tables))
    loads = [pltpu.make_async_copy(src, dst, load_sems.at[k]) for k, (src, dst) in enumerate(loads)]
    for load in loads:
        load.start()
    loads[0].wait()
    find_names(groups, p_dev, anc_ref, names)
    takes = [taken(groups, take) for take in takes]
    copies = []
    for hop, (out, (side, first)) in enumerate(zip(hop_outs, takes)):
        copies += cloud_copies(early, names, states_ref, out, side, first, sems.at[hop])
    for side in range(2):
        parts, at = (hop_outs[1], early * s_dev + tail) if side == 0 else (part_out, 0)
        for k in range(per_part):
            copies.append(
                pltpu.make_async_copy(
                    transition_ref.at[names[side, lax.rem(shard, ways) * per_part + k]],
                    parts.at[pl.ds(at + k * width, width)],
                    part_sems.at[side, k],
                )
            )
    for copy in copies:
        copy.start()

    for load in loads[1:]:
        load.wait()
    table = vols_ref[...].astype(F32)
    for out, (side, first) in zip(hop_outs, takes):
        add_vols(early, tail, vol_rows, names, table, out, side, first, s_dev)

    inner = (group > 0) & (group < groups - 1)
    even = lax.rem(group, 2) == 0
    rank_near, rank_far = jnp.int32(0), jnp.int32(0)
    front, back = jnp.int32(0), jnp.int32(p_dev - 1)
    for i in range(p_dev):
        a = anc_ref[group * p_dev + i]
        offset = lax.div(a, p_dev) - group
        near = jnp.where(even, offset == 1, offset == -1)
        far = jnp.where(even, offset == -1, offset == 1)
        late = far
        came = rank_near
        if relayed:
            late = far | (near & ~inner)
            came = jnp.where(inner, rank_near, rank_near + jnp.where(rank_near < early, early, half))
        came = jnp.where(far, half + rank_far, came)
        moved = jnp.where(far, half + rank_far, rank_near)
        position = jnp.where(late, back, front)
        meta_ref[0, position] = i
        meta_ref[1, position] = jnp.where(near | far, p_dev + came, lax.rem(a, p_dev))
        meta_ref[2, position] = a
        meta_ref[3, position] = jnp.where(near | far, p_dev + moved, lax.rem(a, p_dev))
        front = front + jnp.where(late, 0, 1)
        back = back - jnp.where(late, 1, 0)
        rank_near = rank_near + near.astype(I32)
        rank_far = rank_far + far.astype(I32)
    for q, batch in enumerate(batches):
        for k in range(4):
            value = column([tables[k][meta_ref[2, batch[b % len(batch)]]] for b in range(ROWS)])
            cols_ref[q, k] = jnp.broadcast_to(value, (ROWS, LANES))
    prior = column([tables[4][anc_ref[group * p_dev + i]] for i in range(p_dev)])
    prior_ref[...] = jnp.broadcast_to(prior, (ROWS, LANES))
    for copy in copies:
        copy.wait()


def lane_pick(blocks, index):
    low = index & (LANES - 1)
    high = index >> 7
    out = None
    for k, block in blocks:
        got = jnp.take_along_axis(block, low, axis=1, mode="promise_in_bounds")
        out = got if out is None else jnp.where(high == k, got, out)
    return out


def column(scalars):
    rows = lax.broadcasted_iota(I32, (ROWS, 1), 0)
    out = jnp.zeros((ROWS, 1), scalars[0].dtype)
    for b, scalar in enumerate(scalars):
        out = jnp.where(rows == b, scalar, out)
    return out


def index_kernel(batches, s_dev, margin, meta_ref, count_ref, first_ref, anc_ref,
                 states_ref, vols_ref, *outs):
    *outs, table, sems = outs
    bases, outs = outs[: 2 * len(batches)], outs[2 * len(batches) :]
    p_dev = states_ref.shape[0]
    for q, batch in enumerate(batches):
        for k, at in enumerate(batch):
            place = meta_ref[1, at]

            @pl.when(place < p_dev)
            def _(k=k, at=at, place=place, out=bases[2 * q]):
                pltpu.make_async_copy(
                    states_ref.at[jnp.minimum(place, p_dev - 1)], out.at[k], sems.at[at]
                ).start()

    table[...] = vols_ref[...].astype(F32)
    for q, batch in enumerate(batches):
        places = [jnp.minimum(meta_ref[1, batch[b % len(batch)]], p_dev - 1) for b in range(ROWS)]
        bases[2 * q + 1][...] = jnp.concatenate([table[pl.ds(p, 1), :] for p in places], axis=0)
    shard = lax.axis_index("state")
    base = shard * s_dev
    even = lax.rem(shard, 2) == 0
    lanes = lax.broadcasted_iota(I32, (ROWS, LANES), 1)
    for q, batch in enumerate(batches):
        src_ref, src_t_ref, edge_ref, edge_t_ref = outs[4 * q : 4 * q + 4]
        for step in range(STEPS):
            who = [meta_ref[0, batch[b % len(batch)]] for b in range(ROWS)]
            chosen = jnp.concatenate([anc_ref[step, pl.ds(i, 1), :] for i in who], axis=0)
            blocks = [chosen[:, k * LANES : (k + 1) * LANES] for k in range(chosen.shape[1] // LANES)]
            count = column([count_ref[step, i] for i in who])
            shift = column([base - first_ref[step, i] for i in who])
            sources = []
            for o in range(s_dev // LANES):
                relative = o * LANES + lanes + shift
                own = lane_pick(list(enumerate(blocks)), jnp.clip(relative, 0, chosen.shape[1] - 1))
                sources.append(
                    jnp.where(
                        relative < 0,
                        relative + margin,
                        jnp.where(relative < count, margin + own, margin + s_dev + relative - count),
                    )
                )
            source = jnp.concatenate(sources, axis=1)
            src_ref[step] = source
            src_t_ref[step] = source.T
            head = jnp.concatenate(blocks[: margin // LANES], axis=1)
            tail = [
                lane_pick(list(enumerate(blocks)), count - margin + o * LANES + lanes)
                for o in range(margin // LANES)
            ]
            tail = jnp.concatenate(tail, axis=1)
            edge = jnp.concatenate([jnp.where(even, tail, head), jnp.where(even, head, tail)], axis=1)
            edge_ref[step] = edge
            edge_t_ref[step] = edge.T
    for q, batch in enumerate(batches):
        for k, at in enumerate(batch):

            @pl.when(meta_ref[1, at] < p_dev)
            def _(k=k, at=at, out=bases[2 * q]):
                pltpu.make_async_copy(states_ref.at[0], out.at[k], sems.at[at]).wait()


def one_hot(index, columns):
    index = index.astype(jnp.int16)
    lanes = lax.broadcasted_iota(jnp.int16, (index.shape[0], columns), 1)
    return jnp.where(index == lanes, BF16(1), BF16(0))


def send_edges(batch, margin, cloud_at, vol, edge, edge_t, pair_ref, other_ref):
    s_dev = vol.shape[1]
    blocks = [(k, vol[:, k * LANES : (k + 1) * LANES]) for k in range(s_dev // LANES)]
    width = pair_ref.shape[1]
    for out, start in ((pair_ref, 0), (other_ref, margin)):
        picked = [
            lane_pick(blocks, edge[:, start + o * LANES : start + (o + 1) * LANES])
            for o in range(margin // LANES)
        ]
        picked.append(jnp.zeros((ROWS, width - margin), F32))
        flat = jnp.concatenate(picked, axis=1)
        flat = jnp.concatenate([flat, jnp.zeros((PAD - ROWS, width), F32)], axis=0)
        out[pl.ds(batch * margin, PAD), :] = flat.astype(BF16)
    for b in range(batch):
        rows = jnp.dot(
            one_hot(edge_t[:, b : b + 1], s_dev), cloud_at(b), preferred_element_type=F32
        ).astype(BF16)
        pair_ref[pl.ds(b * margin, margin), :] = rows[:margin]
        other_ref[pl.ds(b * margin, margin), :] = rows[margin:]


def fetch_kernel(batch, first_place, p_dev, margin, vol_rows, recv_slots, meta_ref, base_ref, base_vol_ref,
                 edge_ref, edge_t_ref, *rest):
    recv = rest[: len(recv_slots)]
    cloud_ref, vol_ref, pair_ref, other_ref, table, sems = rest[-6:]
    s_dev = vol_ref.shape[1]
    places = [meta_ref[1, first_place + b % batch] for b in range(ROWS)]
    for b in range(batch):
        for ref, codes in zip(recv, recv_slots):
            for code, at, _ in codes:

                @pl.when(places[b] == code)
                def _(b=b, ref=ref, at=at):
                    pltpu.make_async_copy(
                        ref.at[pl.ds(at, s_dev)], cloud_ref.at[b], sems.at[b]
                    ).start()

    table[...] = jnp.zeros(table.shape, F32)
    for ref, codes in zip(recv, recv_slots):
        start = codes[0][2]
        length = -(-len(codes) * vol_rows // PAD) * PAD
        rows = ref[pl.ds(start, length), :].astype(F32)
        for code, _, at in codes:
            pieces = [rows[at - start + r : at - start + r + 1] for r in range(vol_rows)]
            table[pl.ds(code, 1), :] = jnp.concatenate(pieces, axis=1)
    vol = jnp.concatenate([table[pl.ds(place, 1), :] for place in places], axis=0)
    vol = jnp.where(column(places) < p_dev, base_vol_ref[...], vol)
    vol_ref[...] = vol
    for b in range(batch):

        @pl.when(places[b] >= p_dev)
        def _(b=b):
            pltpu.make_async_copy(recv[0].at[pl.ds(0, s_dev)], cloud_ref.at[b], sems.at[b]).wait()

    send_edges(batch, margin, lambda b: cloud_ref[b], vol, edge_ref[0], edge_t_ref[0], pair_ref, other_ref)


def matrix_kernel(batch, first_place, half, ways, sides, meta_ref, transition_ref, *rest):
    pieces, (out_ref, sems) = rest[: sides * ways], rest[-2:]
    p_dev, width, _ = transition_ref.shape
    per_part = half // ways
    mine = lax.rem(lax.axis_index("state"), ways)
    for b in range(batch):
        place = meta_ref[3, first_place + b]
        moved = jnp.maximum(place - p_dev, 0)
        slot = lax.rem(moved, half)
        chosen = jnp.where(place < p_dev, -1, lax.div(moved, half) * ways + (lax.div(slot, per_part) ^ mine))

        @pl.when(place < p_dev)
        def _(b=b, place=place):
            pltpu.make_async_copy(
                transition_ref.at[jnp.minimum(place, p_dev - 1)], out_ref.at[b], sems.at[b]
            ).start()

        for k, piece in enumerate(pieces):

            @pl.when(chosen == k)
            def _(b=b, piece=piece, slot=slot):
                at = pl.multiple_of(lax.rem(slot, per_part) * width, width)
                pltpu.make_async_copy(piece.at[pl.ds(at, width)], out_ref.at[b], sems.at[b]).start()

    for b in range(batch):
        pltpu.make_async_copy(transition_ref.at[0], out_ref.at[b], sems.at[b]).wait()


def own_kernel(batch, step, margin, src_t_ref, cloud_ref, out_ref):
    s_dev = cloud_ref.shape[1]
    for b in range(batch):
        index = src_t_ref[step][:, b : b + 1] - margin
        out_ref[b] = jnp.dot(
            one_hot(index, s_dev), cloud_ref[b], preferred_element_type=F32
        ).astype(BF16)


def step_kernel(batch, first_place, step, margin, merge, cols_ref, own_ref, pair_ref, other_ref, vol_ref,
                src_ref, src_t_ref, edge_ref, edge_t_ref, matrix_ref, noise_ref, vnoise_ref,
                loading_ref, wanted_ref, *rest):
    last = step == STEPS - 1
    s_dev = vol_ref.shape[1]
    rest = list(rest)
    stat_in = rest.pop(0) if step else None
    if last:
        meta_ref = rest.pop(0)
        if merge:
            vol_before, stat_before = rest[:2]
            rest = rest[2:]
        cloud_out, vol_out, stat_ref = rest
    else:
        cloud_out, vol_out, stat_ref, pair_out, other_out = rest
    even = lax.rem(lax.axis_index("state"), 2) == 0
    source = src_ref[step]
    vol = vol_ref[...]
    blocks = [(k, vol[:, k * LANES : (k + 1) * LANES]) for k in range(s_dev // LANES)]

    def edge_vols(ref):
        return ref[pl.ds(batch * margin, PAD), :].astype(F32)[:ROWS]

    pair_v, other_v = edge_vols(pair_ref), edge_vols(other_ref)
    low_v, high_v = jnp.where(even, other_v, pair_v), jnp.where(even, pair_v, other_v)
    picked = []
    for o in range(s_dev // LANES):
        index = source[:, o * LANES : (o + 1) * LANES]
        own = lane_pick(blocks, jnp.clip(index - margin, 0, s_dev - 1))
        if o < margin // LANES:
            low = [(k, low_v[:, k * LANES : (k + 1) * LANES]) for k in range(margin // LANES)]
            own = jnp.where(index < margin, lane_pick(low, index), own)
        if o >= (s_dev - margin) // LANES:
            high = [(k, high_v[:, k * LANES : (k + 1) * LANES]) for k in range(margin // LANES)]
            above = jnp.clip(index - margin - s_dev, 0, margin - 1)
            own = jnp.where(index >= margin + s_dev, lane_pick(high, above), own)
        picked.append(own)
    picked = jnp.concatenate(picked, axis=1)

    def param(k):
        return cols_ref[k][:, :1]

    center, persist, spread = param(0), param(1), param(2)
    h = center + persist * (picked - center) + spread * vnoise_ref[pl.ds(step, 1), :]
    scale_t = jnp.exp(0.5 * h).T
    vol_new = h.astype(BF16).astype(F32)
    if not last:
        vol_out[...] = vol_new

    wanted = wanted_ref[pl.ds(step, 1), :]
    tile = s_dev // 2
    lanes = lax.broadcasted_iota(I32, (tile, LANES), 1)
    squares = [jnp.zeros((tile, LANES), F32)] * 2
    for b in range(batch):
        for r in range(2):
            span = pl.ds(r * tile, tile)
            index = src_t_ref[step, span, :][:, b : b + 1]
            own = own_ref[b, span, :]
            pair, other = pair_ref[pl.ds(b * margin, margin), :], other_ref[pl.ds(b * margin, margin), :]
            if r == 0:
                patch = jnp.dot(
                    one_hot(index[:margin], margin),
                    jnp.where(even, other, pair),
                    preferred_element_type=F32,
                )
                cloud = jnp.concatenate(
                    [(own[:margin].astype(F32) + patch).astype(BF16), own[margin:]], axis=0
                )
            else:
                patch = jnp.dot(
                    one_hot(index[tile - margin :] - (margin + s_dev), margin),
                    jnp.where(even, pair, other),
                    preferred_element_type=F32,
                )
                cloud = jnp.concatenate(
                    [own[: tile - margin], (own[tile - margin :].astype(F32) + patch).astype(BF16)],
                    axis=0,
                )
            drift = jnp.dot(cloud, matrix_ref[b], preferred_element_type=F32)
            noise = noise_ref[step, span, :].astype(F32)
            cloud = (drift + scale_t[r * tile : (r + 1) * tile, b : b + 1] * noise).astype(BF16)
            cloud_out[b, span, :] = cloud
            misfit = wanted - jnp.dot(cloud, loading_ref[...], preferred_element_type=F32)
            square = jnp.sum(misfit * misfit, axis=1, keepdims=True)
            squares[r] = jnp.where(lanes == b, square, squares[r])
    if not last:
        send_edges(
            batch, margin, lambda b: cloud_out[b], vol_new, edge_ref[step + 1], edge_t_ref[step + 1],
            pair_out, other_out,
        )
    square = jnp.concatenate(squares, axis=0).T[:ROWS]
    precision = param(3)
    maturities = wanted_ref.shape[1]
    weights = -0.5 * precision * square + 0.5 * maturities * jnp.log(precision)
    peak = jnp.max(weights, axis=1, keepdims=True)
    mass = jnp.sum(jnp.exp(weights - peak), axis=1, keepdims=True)
    lane = lax.broadcasted_iota(I32, (ROWS, LANES), 1)
    before = [stat_in[0], stat_in[1]] if step else [jnp.zeros((ROWS, LANES), F32)] * 2
    stats = [jnp.where(lane == step, new, old) for new, old in zip((peak, mass), before)]
    if last:
        rows = lax.broadcasted_iota(I32, (ROWS, 1), 0)
        vol_all = vol_before[...].astype(F32) if merge else jnp.zeros(vol_new.shape, F32)
        placed = [stat_before[0], stat_before[1]] if merge else [jnp.zeros((ROWS, LANES), F32)] * 2
        for b in range(batch):
            here = rows == meta_ref[0, first_place + b]
            vol_all = jnp.where(here, vol_new[b : b + 1], vol_all)
            placed = [jnp.where(here, new[b : b + 1], old) for new, old in zip(stats, placed)]
        vol_out[...] = vol_all.astype(BF16)
        stats = placed
    stat_ref[0] = stats[0]
    stat_ref[1] = stats[1]

def write_kernel(batches, meta_ref, *rest):
    clouds, (final_ref, sems) = rest[: len(batches)], rest[len(batches) :]
    copies = []
    for cloud, batch in zip(clouds, batches):
        for k, place in enumerate(batch):
            copy = pltpu.make_async_copy(
                cloud.at[k], final_ref.at[meta_ref[0, place]], sems.at[place]
            )
            copy.start()
            copies.append(copy)
    for copy in copies:
        copy.wait()


def join_kernel(finish, whole_rows, *refs):
    mine_ref, others, (out_ref,) = refs[0], refs[1:-1], refs[-1:]
    if finish:
        prior_ref, others = others[0], others[1:]
    peak, mass = mine_ref[0], mine_ref[1]
    for other in others:
        other_peak = other[0]
        top = jnp.maximum(peak, other_peak)
        mass = mass * jnp.exp(peak - top) + other[1] * jnp.exp(other_peak - top)
        peak = top
    if not finish:
        out_ref[0] = peak
        out_ref[1] = mass
        return
    lane = lax.broadcasted_iota(I32, (ROWS, LANES), 1)
    gained = peak + jnp.log(jnp.where(lane < STEPS, mass, 1.0)) - math.log(whole_rows)
    gained = jnp.sum(jnp.where(lane < STEPS, gained, 0.0), axis=1, keepdims=True)
    total = jnp.broadcast_to(prior_ref[:, :1] + gained, (ROWS, LANES))
    out_ref[...] = total.T[:1, :]


def join(stats, others, whole_rows, prior=None):
    operands = [stats] + ([] if prior is None else [prior]) + list(others)
    shape = stats.shape if prior is None else (1, ROWS)
    return call(
        functools.partial(join_kernel, prior is not None, whole_rows),
        jax.ShapeDtypeStruct(shape, F32),
        [vmem()] * len(operands),
        vmem(),
        "join",
        nbytes=1 << 14,
    )(*operands)


def swaps(count):
    rounds = []
    for offset in (0, 1):
        partner = [(i - offset ^ 1) + offset for i in range(count)]
        rounds.append([(i, p if 0 <= p < count else i) for i, p in enumerate(partner)])
    return rounds


def doubling(count):
    distance = 1
    while distance < count:
        yield distance, [(i, i ^ distance) for i in range(count)]
        distance *= 2


def prefix_counts(number):
    count, here = lax.axis_size("state"), lax.axis_index("state")
    if count & (count - 1):
        every = lax.all_gather(number, "state")
        before = jnp.arange(count) < here
        return jnp.sum(jnp.where(before[:, None, None], every, 0), axis=0)
    before, total = jnp.zeros_like(number), number
    for distance, pairs in doubling(count):
        other = lax.ppermute(total, "state", pairs)
        before = before + jnp.where((here & distance) != 0, other, 0)
        total = total + other
    return before


def combined_mass(stats, prior, whole_rows):
    count = lax.axis_size("state")
    if count & (count - 1):
        every = lax.all_gather(stats, "state")
        return join(every[0], [every[k] for k in range(1, count)], whole_rows, prior)
    if count == 1:
        return join(stats, [], whole_rows, prior)
    distances = [distance for distance, _ in doubling(count)]
    size = 1
    while distances:
        now, distances = distances[:size], distances[size:]
        size = 2
        apart = [sum(d for j, d in enumerate(now) if k >> j & 1) for k in range(1, 1 << len(now))]
        others = [lax.ppermute(stats, "state", [(i, i ^ d) for i in range(count)]) for d in apart]
        stats = join(stats, others, whole_rows, None if distances else prior)
    return stats


def local(
    states,
    log_vol,
    transition,
    loading,
    yields,
    state_noise,
    vol_noise,
    vol_mean,
    vol_persist,
    vol_scale,
    obs_prec,
    prior_loglik,
    ancestors,
    counts,
    local_anc,
):
    p_dev, s_dev, width = states.shape
    maturities = loading.shape[1]
    groups, shards = lax.axis_size("theta"), lax.axis_size("state")
    half = p_dev // 2
    margin = s_dev // 4
    batch = p_dev // 2
    batches = [tuple(range(q * batch, (q + 1) * batch)) for q in range(p_dev // batch)]
    vol_rows = s_dev // width
    ways = next(w for w in (2, 1) if half % w == 0 and shards % w == 0)
    per_part = half // ways

    early = half // 2
    relayed = groups == 4
    tail = -(-early * vol_rows // PAD) * PAD
    block = early * s_dev + tail
    part_rows = per_part * width
    if relayed:
        takes = [((1, 0), (0, 0)), ((0, 0), (0, early)), ((1, early), (0, 0)), ((0, early), (0, 0))]
    else:
        takes = [((0, 0),) * 2, ((0, early),) * 2, ((1, 0),) * 2, ((1, early),) * 2]
    packed_shapes = [
        jax.ShapeDtypeStruct((rows, width), BF16)
        for rows in (block, block + part_rows, block, block, part_rows)
    ]
    small = ancestors.shape
    first_hop, near_hop, second_hop, third_hop, far_part, meta, cols, prior = call(
        functools.partial(pack_kernel, groups, relayed, takes, tail, batches, ways, vol_rows),
        packed_shapes
        + [
            jax.ShapeDtypeStruct((4, p_dev), I32),
            jax.ShapeDtypeStruct((len(batches), 4, ROWS, LANES), F32),
            jax.ShapeDtypeStruct((ROWS, LANES), F32),
        ],
        [anywhere()] * 9,
        [vmem()] * 5 + [smem(), vmem(), vmem()],
        "pack",
        [pltpu.SMEM(small, I32)]
        + [pltpu.SMEM(small, F32)] * 5
        + [
            pltpu.SMEM((2, half), I32),
            pltpu.VMEM((p_dev, s_dev), BF16),
            pltpu.SemaphoreType.DMA((7,)),
            pltpu.SemaphoreType.DMA((2, per_part)),
            pltpu.SemaphoreType.DMA((4, early)),
        ],
        nbytes=4 * half * s_dev * width * 2,
        limit=PACK_LIMIT,
    )(ancestors, vol_mean, vol_persist, vol_scale, obs_prec, prior_loglik, log_vol, states, transition)

    near_pairs, far_pairs = swaps(groups)
    far_part = lax.ppermute(far_part, "theta", far_pairs)
    first_in = lax.ppermute(first_hop, "theta", near_pairs)
    near = lax.ppermute(near_hop, "theta", near_pairs)
    if relayed:
        cross_pairs = [(i, i ^ 2) for i in range(groups)]
        far_first = lax.ppermute(first_in, "theta", cross_pairs)
        across = lax.ppermute(second_hop, "theta", cross_pairs)
        group = lax.axis_index("theta")
        inner = (group > 0) & (group < groups - 1)
        onward, local_anc = lax.optimization_barrier((jnp.where(inner, third_hop, across), local_anc))
        far_last = lax.ppermute(onward, "theta", near_pairs)
    else:
        far_first = lax.ppermute(second_hop, "theta", far_pairs)
        far_last = lax.ppermute(third_hop, "theta", far_pairs)

    number = counts[:, :, 0]
    first = prefix_counts(number)
    cloud_shape = jax.ShapeDtypeStruct((batch, s_dev, width), BF16)
    vol_shape = jax.ShapeDtypeStruct((ROWS, s_dev), F32)
    index_shapes = [cloud_shape, vol_shape] * len(batches) + [
        jax.ShapeDtypeStruct((STEPS, ROWS, s_dev), I32),
        jax.ShapeDtypeStruct((STEPS, s_dev, ROWS), I32),
        jax.ShapeDtypeStruct((STEPS, ROWS, 2 * margin), I32),
        jax.ShapeDtypeStruct((STEPS, 2 * margin, ROWS), I32),
    ] * len(batches)
    indices = call(
        functools.partial(index_kernel, batches, s_dev, margin),
        index_shapes,
        [smem()] * 3 + [vmem(), anywhere(), vmem()],
        [vmem()] * len(index_shapes),
        "indices",
        [pltpu.VMEM((p_dev, s_dev), F32), pltpu.SemaphoreType.DMA((p_dev,))],
        nbytes=1 << 18,
    )(meta, number, first, local_anc, states, log_vol)
    bases, indices = indices[: 2 * len(batches)], indices[2 * len(batches) :]

    near, _ = lax.optimization_barrier((near, indices[-1]))
    vols_at = early * s_dev
    arrivals = [(first_in, 0), (near, early), (far_first, half), (far_last, half + early)]
    arrivals = [
        (x, tuple((p_dev + code + k, k * s_dev, vols_at + k * vol_rows) for k in range(early)))
        for x, code in arrivals
    ]
    pair_round, other_round = swaps(shards)
    edge_shape = jax.ShapeDtypeStruct((batch * margin + PAD, width), BF16)
    stat_shape = jax.ShapeDtypeStruct((2, ROWS, LANES), F32)
    before = []
    done_clouds = []
    pieces = []
    follow = []
    for q in range(len(batches)):
        src, src_t, edge, edge_t = indices[4 * q : 4 * q + 4]
        recv, recv_slots = zip(*(arrivals if q else arrivals[:2]))
        cloud, vol, pair, other = call(
            functools.partial(fetch_kernel, batch, q * batch, p_dev, margin, vol_rows, recv_slots),
            [cloud_shape, vol_shape, edge_shape, edge_shape],
            [smem()] + [vmem()] * (4 + len(recv) + len(follow)),
            [vmem()] * 4,
            "fetch",
            [pltpu.VMEM((2 * p_dev, s_dev), F32), pltpu.SemaphoreType.DMA((batch,))],
            flops=2 * batch * 2 * margin * s_dev * width,
            nbytes=2 * batch * s_dev * width * 2,
            aliases={1: 0},
        )(meta, *bases[2 * q : 2 * q + 2], edge, edge_t, *recv, *follow)
        stat = None
        for step in range(STEPS):
            last = step == STEPS - 1
            other_in = lax.ppermute(other, "state", other_round)
            pair_in = lax.ppermute(pair, "state", pair_round)
            own = call(
                functools.partial(own_kernel, batch, step, margin),
                cloud_shape,
                [vmem(), vmem()],
                vmem(),
                "own_rows",
                flops=2 * batch * s_dev * s_dev * width,
                nbytes=batch * s_dev * width * 4,
            )(src_t, cloud)
            if step == 0:
                if q == 0:
                    part = near[block:]
                else:
                    part, _ = lax.optimization_barrier((far_part, *follow))
                pieces.append(part)
                if ways == 2:
                    pieces.append(lax.ppermute(part, "state", [(i, i ^ 1) for i in range(shards)]))
                matrices = call(
                    functools.partial(matrix_kernel, batch, q * batch, half, ways, q + 1),
                    jax.ShapeDtypeStruct((batch, width, width), BF16),
                    [smem()] + [anywhere()] * (1 + len(pieces)),
                    vmem(),
                    "matrices",
                    [pltpu.SemaphoreType.DMA((batch,))],
                    nbytes=batch * width * width * 4,
                )(meta, transition, *pieces)
            operands = [
                cols[q], own, pair_in, other_in, vol, src, src_t, edge, edge_t, matrices,
                state_noise, vol_noise, loading, yields,
            ]
            specs = [vmem()] * len(operands)
            if step:
                operands.append(stat)
                specs.append(vmem())
            if last:
                operands += [meta] + before
                specs += [smem()] + [vmem()] * len(before)
                out_shape = [cloud_shape, jax.ShapeDtypeStruct(log_vol.shape, BF16), stat_shape]
                out_specs = [vmem()] * 3
            else:
                out_shape = [cloud_shape, vol_shape, stat_shape, edge_shape, edge_shape]
                out_specs = [vmem()] * 5
            results = call(
                functools.partial(step_kernel, batch, q * batch, step, margin, bool(before)),
                out_shape,
                specs,
                out_specs,
                "step",
                flops=2 * batch * s_dev * width * (width + maturities + margin),
                nbytes=batch * s_dev * width * 8,
            )(*operands)
            if last:
                cloud, *before = results
                done_clouds.append(cloud)
            else:
                cloud, vol, stat, pair, other = results
                follow = [stat] if step == 0 else follow
    vols, stats = before
    final = call(
        functools.partial(write_kernel, batches),
        jax.ShapeDtypeStruct(states.shape, BF16),
        [smem()] + [vmem()] * len(batches),
        anywhere(),
        "write",
        [pltpu.SemaphoreType.DMA((p_dev,))],
        nbytes=2 * p_dev * s_dev * width * 2,
    )(meta, *done_clouds)
    total = combined_mass(stats, prior, s_dev * shards)
    return (final, vols, total.reshape(p_dev))


def solution(mesh):
    placed = (
        P("theta", "state", None),
        P("theta", "state"),
        P("theta", None, None),
        P(),
        P(),
        P(None, "state", None),
        P(None, "state"),
        P(),
        P(),
        P(),
        P(),
        P(),
        P(),
        P(None, "theta", "state"),
        P(None, "theta", "state"),
    )
    return jax.shard_map(
        local,
        mesh=mesh,
        in_specs=placed,
        out_specs=(P("theta", "state", None), P("theta", "state"), P("theta")),
        check_vma=False,
    )
```

```python
import functools
import math

import jax
import jax.numpy as jnp
from jax import lax
from jax.experimental import pallas as pl
from jax.experimental.pallas import tpu as pltpu
from jax.sharding import PartitionSpec as P

STEPS = 3
LANES = 128
ROWS = 8
PAD = 16
VLIMIT = 8 * 1024 * 1024
PACK_LIMIT = 64 * 1024 * 1024

VM = pltpu.VMEM
SM = pltpu.SMEM
F32 = jnp.float32
BF16 = jnp.bfloat16
I32 = jnp.int32


def vmem():
    return pl.BlockSpec(memory_space=pltpu.VMEM)


def smem():
    return pl.BlockSpec(memory_space=pltpu.SMEM)


def anywhere():
    return pl.BlockSpec(memory_space=pl.ANY)


def hbm():
    return pl.BlockSpec(memory_space=pltpu.HBM)


def call(kernel, out_shape, in_specs, out_specs, name, scratch=(), flops=0, nbytes=0, aliases=None,
         limit=VLIMIT):
    return pl.pallas_call(
        kernel,
        out_shape=out_shape,
        in_specs=in_specs,
        out_specs=out_specs,
        scratch_shapes=list(scratch),
        input_output_aliases=aliases or {},
        compiler_params=pltpu.CompilerParams(vmem_limit_bytes=limit),
        cost_estimate=pl.CostEstimate(flops=flops // 64, bytes_accessed=nbytes // 64, transcendentals=0),
        name=name,
    )


def find_names(groups, p_dev, anc_ref, names):
    half = p_dev // 2
    group = lax.axis_index("theta")
    odd = lax.rem(group, 2)
    for side in range(2):
        other = group + (1 - 2 * odd if side == 0 else 2 * odd - 1)
        valid = (other >= 0) & (other < groups)
        other = jnp.clip(other, 0, groups - 1)
        for k in range(half):
            names[side, k] = 0
        rank = jnp.int32(0)
        for i in range(p_dev):
            a = anc_ref[other * p_dev + i]
            hit = valid & (lax.div(a, p_dev) == group) & (rank < half)

            @pl.when(hit)
            def _(side=side, rank=rank, a=a):
                names[side, rank] = lax.rem(a, p_dev)

            rank = rank + hit.astype(I32)


def taken(groups, take):
    group = lax.axis_index("theta")
    inner = (group > 0) & (group < groups - 1)
    (our_side, our_first), (their_side, their_first) = take
    return jnp.where(inner, our_side, their_side), jnp.where(inner, our_first, their_first)


def cloud_copies(early, names, states_ref, out, side, first, sems):
    s_dev = states_ref.shape[1]
    return [
        pltpu.make_async_copy(
            states_ref.at[names[side, first + k]], out.at[pl.ds(k * s_dev, s_dev)], sems.at[k]
        )
        for k in range(early)
    ]


def add_vols(early, tail, vol_rows, names, table, out, side, first, s_dev):
    width = out.shape[1]
    rows = lax.broadcasted_iota(I32, (table.shape[0], 1), 0)
    pieces = []
    for k in range(early):
        here = rows == names[side, first + k]
        row = jnp.sum(jnp.where(here, table, 0.0), axis=0, keepdims=True)
        pieces += [row[:, r * width : (r + 1) * width] for r in range(vol_rows)]
    pieces += [jnp.zeros((1, width), F32)] * (tail - len(pieces))
    out[pl.ds(early * s_dev, tail), :] = jnp.concatenate(pieces, axis=0).astype(BF16)


def pack_kernel(groups, relayed, takes, tail, batches, ways, vol_rows, anc_hbm, *rest):
    tables_hbm, (vols_hbm, states_ref, transition_ref), rest = rest[:5], rest[5:8], rest[8:]
    *hop_outs, part_out = rest[:5]
    rest = rest[5:]
    meta_ref, cols_ref, prior_ref, anc_ref, *rest = rest
    tables, (names, vols_ref, load_sems, part_sems, sems) = rest[:5], rest[5:]
    p_dev, s_dev, width = states_ref.shape
    half = p_dev // 2
    early = half // 2
    per_part = half // ways
    group, shard = lax.axis_index("theta"), lax.axis_index("state")
    loads = [(anc_hbm, anc_ref), (vols_hbm, vols_ref)] + list(zip(tables_hbm, tables))
    loads = [pltpu.make_async_copy(src, dst, load_sems.at[k]) for k, (src, dst) in enumerate(loads)]
    for load in loads:
        load.start()
    loads[0].wait()
    find_names(groups, p_dev, anc_ref, names)
    takes = [taken(groups, take) for take in takes]
    copies = []
    for hop, (out, (side, first)) in enumerate(zip(hop_outs, takes)):
        copies += cloud_copies(early, names, states_ref, out, side, first, sems.at[hop])
    for side in range(2):
        parts, at = (hop_outs[1], early * s_dev + tail) if side == 0 else (part_out, 0)
        for k in range(per_part):
            copies.append(
                pltpu.make_async_copy(
                    transition_ref.at[names[side, lax.rem(shard, ways) * per_part + k]],
                    parts.at[pl.ds(at + k * width, width)],
                    part_sems.at[side, k],
                )
            )
    for copy in copies:
        copy.start()

    for load in loads[1:]:
        load.wait()
    table = vols_ref[...].astype(F32)
    for out, (side, first) in zip(hop_outs, takes):
        add_vols(early, tail, vol_rows, names, table, out, side, first, s_dev)

    inner = (group > 0) & (group < groups - 1)
    even = lax.rem(group, 2) == 0
    rank_near, rank_far = jnp.int32(0), jnp.int32(0)
    front, back = jnp.int32(0), jnp.int32(p_dev - 1)
    for i in range(p_dev):
        a = anc_ref[group * p_dev + i]
        offset = lax.div(a, p_dev) - group
        near = jnp.where(even, offset == 1, offset == -1)
        far = jnp.where(even, offset == -1, offset == 1)
        late = far
        came = rank_near
        if relayed:
            late = far | (near & ~inner)
            came = jnp.where(inner, rank_near, rank_near + jnp.where(rank_near < early, early, half))
        came = jnp.where(far, half + rank_far, came)
        moved = jnp.where(far, half + rank_far, rank_near)
        position = jnp.where(late, back, front)
        meta_ref[0, position] = i
        meta_ref[1, position] = jnp.where(near | far, p_dev + came, lax.rem(a, p_dev))
        meta_ref[2, position] = a
        meta_ref[3, position] = jnp.where(near | far, p_dev + moved, lax.rem(a, p_dev))
        front = front + jnp.where(late, 0, 1)
        back = back - jnp.where(late, 1, 0)
        rank_near = rank_near + near.astype(I32)
        rank_far = rank_far + far.astype(I32)
    for q, batch in enumerate(batches):
        for k in range(4):
            value = column([tables[k][meta_ref[2, batch[b % len(batch)]]] for b in range(ROWS)])
            cols_ref[q, k] = jnp.broadcast_to(value, (ROWS, LANES))
        order = column([meta_ref[0, batch[b % len(batch)]] for b in range(ROWS)]).astype(F32)
        cols_ref[q, 4] = jnp.broadcast_to(order, (ROWS, LANES))
    prior = column([tables[4][anc_ref[group * p_dev + i]] for i in range(p_dev)])
    prior_ref[...] = jnp.broadcast_to(prior, (ROWS, LANES))
    for copy in copies:
        copy.wait()


def lane_pick(blocks, index):
    low = index & (LANES - 1)
    high = index >> 7
    out = None
    for k, block in blocks:
        got = jnp.take_along_axis(block, low, axis=1, mode="promise_in_bounds")
        out = got if out is None else jnp.where(high == k, got, out)
    return out


def column(scalars):
    rows = lax.broadcasted_iota(I32, (ROWS, 1), 0)
    out = jnp.zeros((ROWS, 1), scalars[0].dtype)
    for b, scalar in enumerate(scalars):
        out = jnp.where(rows == b, scalar, out)
    return out


def index_kernel(batches, s_dev, margin, meta_ref, count_ref, first_ref, anc_ref,
                 states_ref, vols_ref, *outs):
    *outs, table, sems = outs
    bases, outs = outs[: 2 * len(batches)], outs[2 * len(batches) :]
    p_dev = states_ref.shape[0]
    for q, batch in enumerate(batches):
        for k, at in enumerate(batch):
            place = meta_ref[1, at]

            @pl.when(place < p_dev)
            def _(k=k, at=at, place=place, out=bases[2 * q]):
                pltpu.make_async_copy(
                    states_ref.at[jnp.minimum(place, p_dev - 1)], out.at[k], sems.at[at]
                ).start()

    table[...] = vols_ref[...].astype(F32)
    for q, batch in enumerate(batches):
        places = [jnp.minimum(meta_ref[1, batch[b % len(batch)]], p_dev - 1) for b in range(ROWS)]
        bases[2 * q + 1][...] = jnp.concatenate([table[pl.ds(p, 1), :] for p in places], axis=0)
    shard = lax.axis_index("state")
    base = shard * s_dev
    even = lax.rem(shard, 2) == 0
    lanes = lax.broadcasted_iota(I32, (ROWS, LANES), 1)
    for q, batch in enumerate(batches):
        src_ref, src_t_ref, edge_ref, edge_t_ref = outs[4 * q : 4 * q + 4]
        for step in range(STEPS):
            who = [meta_ref[0, batch[b % len(batch)]] for b in range(ROWS)]
            chosen = jnp.concatenate([anc_ref[step, pl.ds(i, 1), :] for i in who], axis=0)
            blocks = [chosen[:, k * LANES : (k + 1) * LANES] for k in range(chosen.shape[1] // LANES)]
            count = column([count_ref[step, i] for i in who])
            shift = column([base - first_ref[step, i] for i in who])
            sources = []
            for o in range(s_dev // LANES):
                relative = o * LANES + lanes + shift
                own = lane_pick(list(enumerate(blocks)), jnp.clip(relative, 0, chosen.shape[1] - 1))
                sources.append(
                    jnp.where(
                        relative < 0,
                        relative + margin,
                        jnp.where(relative < count, margin + own, margin + s_dev + relative - count),
                    )
                )
            source = jnp.concatenate(sources, axis=1)
            src_ref[step] = source
            column_form = source.T
            for k, start in enumerate((0, margin, margin + s_dev)):
                src_t_ref[step, k] = (column_form - start).astype(jnp.int16)
            head = jnp.concatenate(blocks[: margin // LANES], axis=1)
            tail = [
                lane_pick(list(enumerate(blocks)), count - margin + o * LANES + lanes)
                for o in range(margin // LANES)
            ]
            tail = jnp.concatenate(tail, axis=1)
            edge = jnp.concatenate([jnp.where(even, tail, head), jnp.where(even, head, tail)], axis=1)
            edge_ref[step] = edge
            edge_t_ref[step] = edge.T.astype(jnp.int16)
    for q, batch in enumerate(batches):
        for k, at in enumerate(batch):

            @pl.when(meta_ref[1, at] < p_dev)
            def _(k=k, at=at, out=bases[2 * q]):
                pltpu.make_async_copy(states_ref.at[0], out.at[k], sems.at[at]).wait()


def one_hot(index, columns):
    lanes = lax.broadcasted_iota(jnp.int16, (index.shape[0], columns), 1)
    return jnp.where(index == lanes, BF16(1), BF16(0))


def send_edges(batch, margin, cloud_at, vol, edge, edge_t, pair_ref, other_ref):
    s_dev = vol.shape[1]
    blocks = [(k, vol[:, k * LANES : (k + 1) * LANES]) for k in range(s_dev // LANES)]
    width = pair_ref.shape[1]
    for out, start in ((pair_ref, 0), (other_ref, margin)):
        picked = [
            lane_pick(blocks, edge[:, start + o * LANES : start + (o + 1) * LANES])
            for o in range(margin // LANES)
        ]
        picked.append(jnp.zeros((ROWS, width - margin), F32))
        flat = jnp.concatenate(picked, axis=1)
        flat = jnp.concatenate([flat, jnp.zeros((PAD - ROWS, width), F32)], axis=0)
        out[pl.ds(batch * margin, PAD), :] = flat.astype(BF16)
    for b in range(batch):
        rows = jnp.dot(
            one_hot(edge_t[:, b : b + 1], s_dev), cloud_at(b), preferred_element_type=F32
        ).astype(BF16)
        pair_ref[pl.ds(b * margin, margin), :] = rows[:margin]
        other_ref[pl.ds(b * margin, margin), :] = rows[margin:]


def fetch_kernel(batch, first_place, p_dev, margin, vol_rows, recv_slots, meta_ref, base_ref, base_vol_ref,
                 edge_ref, edge_t_ref, *rest):
    recv = rest[: len(recv_slots)]
    cloud_ref, vol_ref, pair_ref, other_ref, table, sems = rest[-6:]
    s_dev = vol_ref.shape[1]
    places = [meta_ref[1, first_place + b % batch] for b in range(ROWS)]
    for b in range(batch):
        for ref, codes in zip(recv, recv_slots):
            for code, at, _ in codes:

                @pl.when(places[b] == code)
                def _(b=b, ref=ref, at=at):
                    pltpu.make_async_copy(
                        ref.at[pl.ds(at, s_dev)], cloud_ref.at[b], sems.at[b]
                    ).start()

    table[...] = jnp.zeros(table.shape, F32)
    for ref, codes in zip(recv, recv_slots):
        start = codes[0][2]
        length = -(-len(codes) * vol_rows // PAD) * PAD
        rows = ref[pl.ds(start, length), :].astype(F32)
        for code, _, at in codes:
            pieces = [rows[at - start + r : at - start + r + 1] for r in range(vol_rows)]
            table[pl.ds(code, 1), :] = jnp.concatenate(pieces, axis=1)
    vol = jnp.concatenate([table[pl.ds(place, 1), :] for place in places], axis=0)
    vol = jnp.where(column(places) < p_dev, base_vol_ref[...], vol)
    vol_ref[...] = vol
    for b in range(batch):

        @pl.when(places[b] >= p_dev)
        def _(b=b):
            pltpu.make_async_copy(recv[0].at[pl.ds(0, s_dev)], cloud_ref.at[b], sems.at[b]).wait()

    send_edges(batch, margin, lambda b: cloud_ref[b], vol, edge_ref[0], edge_t_ref[0], pair_ref, other_ref)


def matrix_kernel(batch, first_place, half, ways, sides, meta_ref, transition_ref, *rest):
    pieces, (out_ref, sems) = rest[: sides * ways], rest[-2:]
    p_dev, width, _ = transition_ref.shape
    per_part = half // ways
    mine = lax.rem(lax.axis_index("state"), ways)
    for b in range(batch):
        place = meta_ref[3, first_place + b]
        moved = jnp.maximum(place - p_dev, 0)
        slot = lax.rem(moved, half)
        chosen = jnp.where(place < p_dev, -1, lax.div(moved, half) * ways + (lax.div(slot, per_part) ^ mine))

        @pl.when(place < p_dev)
        def _(b=b, place=place):
            pltpu.make_async_copy(
                transition_ref.at[jnp.minimum(place, p_dev - 1)], out_ref.at[b], sems.at[b]
            ).start()

        for k, piece in enumerate(pieces):

            @pl.when(chosen == k)
            def _(b=b, piece=piece, slot=slot):
                at = pl.multiple_of(lax.rem(slot, per_part) * width, width)
                pltpu.make_async_copy(piece.at[pl.ds(at, width)], out_ref.at[b], sems.at[b]).start()

    for b in range(batch):
        pltpu.make_async_copy(transition_ref.at[0], out_ref.at[b], sems.at[b]).wait()


def own_kernel(batch, step, margin, src_t_ref, cloud_ref, out_ref):
    s_dev = cloud_ref.shape[1]
    for b in range(batch):
        index = src_t_ref[step, 1][:, b : b + 1]
        out_ref[b] = jnp.dot(
            one_hot(index, s_dev), cloud_ref[b], preferred_element_type=F32
        ).astype(BF16)


def step_kernel(batch, first_place, step, margin, merge, cols_ref, own_ref, pair_ref, other_ref, vol_ref,
                src_ref, src_t_ref, edge_ref, edge_t_ref, matrix_ref, noise_ref, vnoise_ref,
                loading_ref, wanted_ref, *rest):
    last = step == STEPS - 1
    s_dev = vol_ref.shape[1]
    rest = list(rest)
    stat_in = rest.pop(0) if step else None
    if last:
        if merge:
            vol_before, stat_before = rest[:2]
            rest = rest[2:]
        cloud_out, vol_out, stat_ref = rest
    else:
        cloud_out, vol_out, stat_ref, pair_out, other_out = rest
    even = lax.rem(lax.axis_index("state"), 2) == 0
    source = src_ref[step]
    vol = vol_ref[...]
    blocks = [(k, vol[:, k * LANES : (k + 1) * LANES]) for k in range(s_dev // LANES)]

    def edge_vols(ref):
        return ref[pl.ds(batch * margin, PAD), :].astype(F32)[:ROWS]

    pair_v, other_v = edge_vols(pair_ref), edge_vols(other_ref)
    low_v, high_v = jnp.where(even, other_v, pair_v), jnp.where(even, pair_v, other_v)
    picked = []
    for o in range(s_dev // LANES):
        index = source[:, o * LANES : (o + 1) * LANES]
        own = lane_pick(blocks, jnp.clip(index - margin, 0, s_dev - 1))
        if o < margin // LANES:
            low = [(k, low_v[:, k * LANES : (k + 1) * LANES]) for k in range(margin // LANES)]
            own = jnp.where(index < margin, lane_pick(low, index), own)
        if o >= (s_dev - margin) // LANES:
            high = [(k, high_v[:, k * LANES : (k + 1) * LANES]) for k in range(margin // LANES)]
            above = jnp.clip(index - margin - s_dev, 0, margin - 1)
            own = jnp.where(index >= margin + s_dev, lane_pick(high, above), own)
        picked.append(own)
    picked = jnp.concatenate(picked, axis=1)

    def param(k):
        return cols_ref[k][:, :1]

    center, persist, spread = param(0), param(1), param(2)
    h = center + persist * (picked - center) + spread * vnoise_ref[pl.ds(step, 1), :]
    scale_t = jnp.exp(0.5 * h).T
    vol_new = h.astype(BF16).astype(F32)
    if not last:
        vol_out[...] = vol_new

    wanted = wanted_ref[pl.ds(step, 1), :]
    tile = s_dev // 2
    lanes = lax.broadcasted_iota(I32, (tile, LANES), 1)
    squares = [jnp.zeros((tile, LANES), F32)] * 2
    for b in range(batch):
        for r in range(2):
            span = pl.ds(r * tile, tile)
            own = own_ref[b, span, :]
            pair, other = pair_ref[pl.ds(b * margin, margin), :], other_ref[pl.ds(b * margin, margin), :]
            if r == 0:
                patch = jnp.dot(
                    one_hot(src_t_ref[step, 0, pl.ds(0, margin), :][:, b : b + 1], margin),
                    jnp.where(even, other, pair),
                    preferred_element_type=F32,
                )
                cloud = jnp.concatenate(
                    [(own[:margin].astype(F32) + patch).astype(BF16), own[margin:]], axis=0
                )
            else:
                patch = jnp.dot(
                    one_hot(src_t_ref[step, 2, pl.ds(s_dev - margin, margin), :][:, b : b + 1], margin),
                    jnp.where(even, pair, other),
                    preferred_element_type=F32,
                )
                cloud = jnp.concatenate(
                    [own[: tile - margin], (own[tile - margin :].astype(F32) + patch).astype(BF16)],
                    axis=0,
                )
            drift = jnp.dot(cloud, matrix_ref[b], preferred_element_type=F32)
            noise = noise_ref[step, span, :].astype(F32)
            cloud = (drift + scale_t[r * tile : (r + 1) * tile, b : b + 1] * noise).astype(BF16)
            cloud_out[b, span, :] = cloud
            misfit = wanted - jnp.dot(cloud, loading_ref[...], preferred_element_type=F32)
            square = jnp.sum(misfit * misfit, axis=1, keepdims=True)
            squares[r] = jnp.where(lanes == b, square, squares[r])
    if not last:
        send_edges(
            batch, margin, lambda b: cloud_out[b], vol_new, edge_ref[step + 1], edge_t_ref[step + 1],
            pair_out, other_out,
        )
    square = jnp.concatenate(squares, axis=0).T[:ROWS]
    precision = param(3)
    maturities = wanted_ref.shape[1]
    weights = -0.5 * precision * square + 0.5 * maturities * jnp.log(precision)
    peak = jnp.max(weights, axis=1, keepdims=True)
    mass = jnp.sum(jnp.exp(weights - peak), axis=1, keepdims=True)
    lane = lax.broadcasted_iota(I32, (ROWS, LANES), 1)
    before = [stat_in[0], stat_in[1]] if step else [jnp.zeros((ROWS, LANES), F32)] * 2
    stats = [jnp.where(lane == step, new, old) for new, old in zip((peak, mass), before)]
    if last:
        rows = lax.broadcasted_iota(I32, (ROWS, 1), 0).astype(F32)
        order = param(4)
        vol_all = vol_before[...].astype(F32) if merge else jnp.zeros(vol_new.shape, F32)
        placed = [stat_before[0], stat_before[1]] if merge else [jnp.zeros((ROWS, LANES), F32)] * 2
        for b in range(batch):
            here = rows == order[b : b + 1]
            vol_all = jnp.where(here, vol_new[b : b + 1], vol_all)
            placed = [jnp.where(here, new[b : b + 1], old) for new, old in zip(stats, placed)]
        vol_out[...] = vol_all.astype(BF16)
        stats = placed
    stat_ref[0] = stats[0]
    stat_ref[1] = stats[1]

def write_kernel(batches, meta_ref, *rest):
    clouds, (final_ref, sems) = rest[: len(batches)], rest[len(batches) :]
    copies = []
    for cloud, batch in zip(clouds, batches):
        for k, place in enumerate(batch):
            copy = pltpu.make_async_copy(
                cloud.at[k], final_ref.at[meta_ref[0, place]], sems.at[place]
            )
            copy.start()
            copies.append(copy)
    for copy in copies:
        copy.wait()


def join_kernel(finish, whole_rows, *refs):
    mine_ref, others, (out_ref,) = refs[0], refs[1:-1], refs[-1:]
    if finish:
        prior_ref, others = others[0], others[1:]
    peak, mass = mine_ref[0], mine_ref[1]
    for other in others:
        other_peak = other[0]
        top = jnp.maximum(peak, other_peak)
        mass = mass * jnp.exp(peak - top) + other[1] * jnp.exp(other_peak - top)
        peak = top
    if not finish:
        out_ref[0] = peak
        out_ref[1] = mass
        return
    lane = lax.broadcasted_iota(I32, (ROWS, LANES), 1)
    gained = peak + jnp.log(jnp.where(lane < STEPS, mass, 1.0)) - math.log(whole_rows)
    gained = jnp.sum(jnp.where(lane < STEPS, gained, 0.0), axis=1, keepdims=True)
    total = jnp.broadcast_to(prior_ref[:, :1] + gained, (ROWS, LANES))
    out_ref[...] = total.T[:1, :]


def join(stats, others, whole_rows, prior=None):
    operands = [stats] + ([] if prior is None else [prior]) + list(others)
    shape = stats.shape if prior is None else (1, ROWS)
    return call(
        functools.partial(join_kernel, prior is not None, whole_rows),
        jax.ShapeDtypeStruct(shape, F32),
        [vmem()] * len(operands),
        vmem(),
        "join",
        nbytes=1 << 14,
    )(*operands)


def swaps(count):
    rounds = []
    for offset in (0, 1):
        partner = [(i - offset ^ 1) + offset for i in range(count)]
        rounds.append([(i, p if 0 <= p < count else i) for i, p in enumerate(partner)])
    return rounds


def doubling(count):
    distance = 1
    while distance < count:
        yield distance, [(i, i ^ distance) for i in range(count)]
        distance *= 2


def prefix_counts(number):
    count, here = lax.axis_size("state"), lax.axis_index("state")
    if count & (count - 1):
        every = lax.all_gather(number, "state")
        before = jnp.arange(count) < here
        return jnp.sum(jnp.where(before[:, None, None], every, 0), axis=0)
    before, total = jnp.zeros_like(number), number
    for distance, pairs in doubling(count):
        other = lax.ppermute(total, "state", pairs)
        before = before + jnp.where((here & distance) != 0, other, 0)
        total = total + other
    return before


def combined_mass(stats, prior, whole_rows):
    count = lax.axis_size("state")
    if count & (count - 1):
        every = lax.all_gather(stats, "state")
        return join(every[0], [every[k] for k in range(1, count)], whole_rows, prior)
    if count == 1:
        return join(stats, [], whole_rows, prior)
    distances = [distance for distance, _ in doubling(count)]
    size = 1
    while distances:
        now, distances = distances[:size], distances[size:]
        size = 2
        apart = [sum(d for j, d in enumerate(now) if k >> j & 1) for k in range(1, 1 << len(now))]
        others = [lax.ppermute(stats, "state", [(i, i ^ d) for i in range(count)]) for d in apart]
        stats = join(stats, others, whole_rows, None if distances else prior)
    return stats


def local(
    states,
    log_vol,
    transition,
    loading,
    yields,
    state_noise,
    vol_noise,
    vol_mean,
    vol_persist,
    vol_scale,
    obs_prec,
    prior_loglik,
    ancestors,
    counts,
    local_anc,
):
    p_dev, s_dev, width = states.shape
    maturities = loading.shape[1]
    groups, shards = lax.axis_size("theta"), lax.axis_size("state")
    half = p_dev // 2
    margin = s_dev // 4
    batch = p_dev // 2
    batches = [tuple(range(q * batch, (q + 1) * batch)) for q in range(p_dev // batch)]
    vol_rows = s_dev // width
    ways = next(w for w in (2, 1) if half % w == 0 and shards % w == 0)
    per_part = half // ways

    early = half // 2
    relayed = groups == 4
    tail = -(-early * vol_rows // PAD) * PAD
    block = early * s_dev + tail
    part_rows = per_part * width
    if relayed:
        takes = [((1, 0), (0, 0)), ((0, 0), (0, early)), ((1, early), (0, 0)), ((0, early), (0, 0))]
    else:
        takes = [((0, 0),) * 2, ((0, early),) * 2, ((1, 0),) * 2, ((1, early),) * 2]
    packed_shapes = [
        jax.ShapeDtypeStruct((rows, width), BF16)
        for rows in (block, block + part_rows, block, block, part_rows)
    ]
    small = ancestors.shape
    first_hop, near_hop, second_hop, third_hop, far_part, meta, cols, prior = call(
        functools.partial(pack_kernel, groups, relayed, takes, tail, batches, ways, vol_rows),
        packed_shapes
        + [
            jax.ShapeDtypeStruct((4, p_dev), I32),
            jax.ShapeDtypeStruct((len(batches), 5, ROWS, LANES), F32),
            jax.ShapeDtypeStruct((ROWS, LANES), F32),
        ],
        [anywhere()] * 9,
        [vmem()] * 5 + [smem(), vmem(), vmem()],
        "pack",
        [pltpu.SMEM(small, I32)]
        + [pltpu.SMEM(small, F32)] * 5
        + [
            pltpu.SMEM((2, half), I32),
            pltpu.VMEM((p_dev, s_dev), BF16),
            pltpu.SemaphoreType.DMA((7,)),
            pltpu.SemaphoreType.DMA((2, per_part)),
            pltpu.SemaphoreType.DMA((4, early)),
        ],
        nbytes=4 * half * s_dev * width * 2,
        limit=PACK_LIMIT,
    )(ancestors, vol_mean, vol_persist, vol_scale, obs_prec, prior_loglik, log_vol, states, transition)

    near_pairs, far_pairs = swaps(groups)
    far_part = lax.ppermute(far_part, "theta", far_pairs)
    first_in = lax.ppermute(first_hop, "theta", near_pairs)
    near = lax.ppermute(near_hop, "theta", near_pairs)
    if relayed:
        cross_pairs = [(i, i ^ 2) for i in range(groups)]
        far_first = lax.ppermute(first_in, "theta", cross_pairs)
        across = lax.ppermute(second_hop, "theta", cross_pairs)
        group = lax.axis_index("theta")
        inner = (group > 0) & (group < groups - 1)
        onward, local_anc = lax.optimization_barrier((jnp.where(inner, third_hop, across), local_anc))
        far_last = lax.ppermute(onward, "theta", near_pairs)
    else:
        far_first = lax.ppermute(second_hop, "theta", far_pairs)
        far_last = lax.ppermute(third_hop, "theta", far_pairs)

    number = counts[:, :, 0]
    first = prefix_counts(number)
    cloud_shape = jax.ShapeDtypeStruct((batch, s_dev, width), BF16)
    vol_shape = jax.ShapeDtypeStruct((ROWS, s_dev), F32)
    index_shapes = [cloud_shape, vol_shape] * len(batches) + [
        jax.ShapeDtypeStruct((STEPS, ROWS, s_dev), I32),
        jax.ShapeDtypeStruct((STEPS, 3, s_dev, ROWS), jnp.int16),
        jax.ShapeDtypeStruct((STEPS, ROWS, 2 * margin), I32),
        jax.ShapeDtypeStruct((STEPS, 2 * margin, ROWS), jnp.int16),
    ] * len(batches)
    indices = call(
        functools.partial(index_kernel, batches, s_dev, margin),
        index_shapes,
        [smem()] * 3 + [vmem(), anywhere(), vmem()],
        [vmem()] * len(index_shapes),
        "indices",
        [pltpu.VMEM((p_dev, s_dev), F32), pltpu.SemaphoreType.DMA((p_dev,))],
        nbytes=1 << 18,
    )(meta, number, first, local_anc, states, log_vol)
    bases, indices = indices[: 2 * len(batches)], indices[2 * len(batches) :]

    near, _ = lax.optimization_barrier((near, indices[-1]))
    vols_at = early * s_dev
    arrivals = [(first_in, 0), (near, early), (far_first, half), (far_last, half + early)]
    arrivals = [
        (x, tuple((p_dev + code + k, k * s_dev, vols_at + k * vol_rows) for k in range(early)))
        for x, code in arrivals
    ]
    pair_round, other_round = swaps(shards)
    edge_shape = jax.ShapeDtypeStruct((batch * margin + PAD, width), BF16)
    stat_shape = jax.ShapeDtypeStruct((2, ROWS, LANES), F32)
    before = []
    done_clouds = []
    pieces = []
    follow = []
    for q in range(len(batches)):
        src, src_t, edge, edge_t = indices[4 * q : 4 * q + 4]
        recv, recv_slots = zip(*(arrivals if q else arrivals[:2]))
        cloud, vol, pair, other = call(
            functools.partial(fetch_kernel, batch, q * batch, p_dev, margin, vol_rows, recv_slots),
            [cloud_shape, vol_shape, edge_shape, edge_shape],
            [smem()] + [vmem()] * (4 + len(recv) + len(follow)),
            [vmem()] * 4,
            "fetch",
            [pltpu.VMEM((2 * p_dev, s_dev), F32), pltpu.SemaphoreType.DMA((batch,))],
            flops=2 * batch * 2 * margin * s_dev * width,
            nbytes=2 * batch * s_dev * width * 2,
            aliases={1: 0},
        )(meta, *bases[2 * q : 2 * q + 2], edge, edge_t, *recv, *follow)
        stat = None
        for step in range(STEPS):
            last = step == STEPS - 1
            other_in = lax.ppermute(other, "state", other_round)
            pair_in = lax.ppermute(pair, "state", pair_round)
            own = call(
                functools.partial(own_kernel, batch, step, margin),
                cloud_shape,
                [vmem(), vmem()],
                vmem(),
                "own_rows",
                flops=2 * batch * s_dev * s_dev * width,
                nbytes=batch * s_dev * width * 4,
            )(src_t, cloud)
            if step == 0:
                if q == 0:
                    part = near[block:]
                else:
                    part, _ = lax.optimization_barrier((far_part, *follow))
                pieces.append(part)
                if ways == 2:
                    pieces.append(lax.ppermute(part, "state", [(i, i ^ 1) for i in range(shards)]))
                matrices = call(
                    functools.partial(matrix_kernel, batch, q * batch, half, ways, q + 1),
                    jax.ShapeDtypeStruct((batch, width, width), BF16),
                    [smem()] + [anywhere()] * (1 + len(pieces)),
                    vmem(),
                    "matrices",
                    [pltpu.SemaphoreType.DMA((batch,))],
                    nbytes=batch * width * width * 4,
                )(meta, transition, *pieces)
            operands = [
                cols[q], own, pair_in, other_in, vol, src, src_t, edge, edge_t, matrices,
                state_noise, vol_noise, loading, yields,
            ]
            specs = [vmem()] * len(operands)
            if step:
                operands.append(stat)
                specs.append(vmem())
            if last:
                operands += before
                specs += [vmem()] * len(before)
                out_shape = [cloud_shape, jax.ShapeDtypeStruct(log_vol.shape, BF16), stat_shape]
                out_specs = [vmem()] * 3
            else:
                out_shape = [cloud_shape, vol_shape, stat_shape, edge_shape, edge_shape]
                out_specs = [vmem()] * 5
            results = call(
                functools.partial(step_kernel, batch, q * batch, step, margin, bool(before)),
                out_shape,
                specs,
                out_specs,
                "step",
                flops=2 * batch * s_dev * width * (width + maturities + margin),
                nbytes=batch * s_dev * width * 8,
            )(*operands)
            if last:
                cloud, *before = results
                done_clouds.append(cloud)
            else:
                cloud, vol, stat, pair, other = results
                follow = [stat] if step == 0 else follow
    vols, stats = before
    final = call(
        functools.partial(write_kernel, batches),
        jax.ShapeDtypeStruct(states.shape, BF16),
        [smem()] + [vmem()] * len(batches),
        anywhere(),
        "write",
        [pltpu.SemaphoreType.DMA((p_dev,))],
        nbytes=2 * p_dev * s_dev * width * 2,
    )(meta, *done_clouds)
    total = combined_mass(stats, prior, s_dev * shards)
    return (final, vols, total.reshape(p_dev))


def solution(mesh):
    placed = (
        P("theta", "state", None),
        P("theta", "state"),
        P("theta", None, None),
        P(),
        P(),
        P(None, "state", None),
        P(None, "state"),
        P(),
        P(),
        P(),
        P(),
        P(),
        P(),
        P(None, "theta", "state"),
        P(None, "theta", "state"),
    )
    return jax.shard_map(
        local,
        mesh=mesh,
        in_specs=placed,
        out_specs=(P("theta", "state", None), P("theta", "state"), P("theta")),
        check_vma=False,
    )
```

```python
import functools
import math

import jax
import jax.numpy as jnp
from jax import lax
from jax.experimental import pallas as pl
from jax.experimental.pallas import tpu as pltpu
from jax.sharding import PartitionSpec as P

STEPS = 3
LANES = 128
ROWS = 8
PAD = 16
VLIMIT = 8 * 1024 * 1024
PACK_LIMIT = 64 * 1024 * 1024

VM = pltpu.VMEM
SM = pltpu.SMEM
F32 = jnp.float32
BF16 = jnp.bfloat16
I32 = jnp.int32


def vmem():
    return pl.BlockSpec(memory_space=pltpu.VMEM)


def smem():
    return pl.BlockSpec(memory_space=pltpu.SMEM)


def anywhere():
    return pl.BlockSpec(memory_space=pl.ANY)


def hbm():
    return pl.BlockSpec(memory_space=pltpu.HBM)


def call(kernel, out_shape, in_specs, out_specs, name, scratch=(), flops=0, nbytes=0, aliases=None,
         limit=VLIMIT):
    return pl.pallas_call(
        kernel,
        out_shape=out_shape,
        in_specs=in_specs,
        out_specs=out_specs,
        scratch_shapes=list(scratch),
        input_output_aliases=aliases or {},
        compiler_params=pltpu.CompilerParams(vmem_limit_bytes=limit),
        cost_estimate=pl.CostEstimate(flops=flops // 64, bytes_accessed=nbytes // 64, transcendentals=0),
        name=name,
    )


def find_names(groups, p_dev, anc_ref, names):
    half = p_dev // 2
    group = lax.axis_index("theta")
    odd = lax.rem(group, 2)
    for side in range(2):
        other = group + (1 - 2 * odd if side == 0 else 2 * odd - 1)
        valid = (other >= 0) & (other < groups)
        other = jnp.clip(other, 0, groups - 1)
        for k in range(half):
            names[side, k] = 0
        rank = jnp.int32(0)
        for i in range(p_dev):
            a = anc_ref[other * p_dev + i]
            hit = valid & (lax.div(a, p_dev) == group) & (rank < half)

            @pl.when(hit)
            def _(side=side, rank=rank, a=a):
                names[side, rank] = lax.rem(a, p_dev)

            rank = rank + hit.astype(I32)


def taken(groups, take):
    group = lax.axis_index("theta")
    inner = (group > 0) & (group < groups - 1)
    (our_side, our_first), (their_side, their_first) = take
    return jnp.where(inner, our_side, their_side), jnp.where(inner, our_first, their_first)


def cloud_copies(early, names, states_ref, out, side, first, sems):
    s_dev = states_ref.shape[1]
    return [
        pltpu.make_async_copy(
            states_ref.at[names[side, first + k]], out.at[pl.ds(k * s_dev, s_dev)], sems.at[k]
        )
        for k in range(early)
    ]


def add_vols(early, tail, vol_rows, names, table, out, side, first, s_dev):
    width = out.shape[1]
    rows = lax.broadcasted_iota(I32, (table.shape[0], 1), 0)
    pieces = []
    for k in range(early):
        here = rows == names[side, first + k]
        row = jnp.sum(jnp.where(here, table, 0.0), axis=0, keepdims=True)
        pieces += [row[:, r * width : (r + 1) * width] for r in range(vol_rows)]
    pieces += [jnp.zeros((1, width), F32)] * (tail - len(pieces))
    out[pl.ds(early * s_dev, tail), :] = jnp.concatenate(pieces, axis=0).astype(BF16)


def pack_kernel(groups, relayed, takes, tail, batches, ways, vol_rows, anc_hbm, *rest):
    tables_hbm, (vols_hbm, states_ref, transition_ref), rest = rest[:5], rest[5:8], rest[8:]
    *hop_outs, part_out = rest[:5]
    rest = rest[5:]
    meta_ref, cols_ref, prior_ref, anc_ref, *rest = rest
    tables, (names, vols_ref, load_sems, part_sems, sems) = rest[:5], rest[5:]
    p_dev, s_dev, width = states_ref.shape
    half = p_dev // 2
    early = half // 2
    per_part = half // ways
    group, shard = lax.axis_index("theta"), lax.axis_index("state")
    loads = [(anc_hbm, anc_ref), (vols_hbm, vols_ref)] + list(zip(tables_hbm, tables))
    loads = [pltpu.make_async_copy(src, dst, load_sems.at[k]) for k, (src, dst) in enumerate(loads)]
    for load in loads:
        load.start()
    loads[0].wait()
    find_names(groups, p_dev, anc_ref, names)
    takes = [taken(groups, take) for take in takes]
    copies = []
    for hop, (out, (side, first)) in enumerate(zip(hop_outs, takes)):
        copies += cloud_copies(early, names, states_ref, out, side, first, sems.at[hop])
    for side in range(2):
        parts, at = (hop_outs[1], early * s_dev + tail) if side == 0 else (part_out, 0)
        for k in range(per_part):
            copies.append(
                pltpu.make_async_copy(
                    transition_ref.at[names[side, lax.rem(shard, ways) * per_part + k]],
                    parts.at[pl.ds(at + k * width, width)],
                    part_sems.at[side, k],
                )
            )
    for copy in copies:
        copy.start()

    for load in loads[1:]:
        load.wait()
    table = vols_ref[...].astype(F32)
    for out, (side, first) in zip(hop_outs, takes):
        add_vols(early, tail, vol_rows, names, table, out, side, first, s_dev)

    inner = (group > 0) & (group < groups - 1)
    even = lax.rem(group, 2) == 0
    rank_near, rank_far = jnp.int32(0), jnp.int32(0)
    front, back = jnp.int32(0), jnp.int32(p_dev - 1)
    for i in range(p_dev):
        a = anc_ref[group * p_dev + i]
        offset = lax.div(a, p_dev) - group
        near = jnp.where(even, offset == 1, offset == -1)
        far = jnp.where(even, offset == -1, offset == 1)
        late = far
        came = rank_near
        if relayed:
            late = far | (near & ~inner)
            came = jnp.where(inner, rank_near, rank_near + jnp.where(rank_near < early, early, half))
        came = jnp.where(far, half + rank_far, came)
        moved = jnp.where(far, half + rank_far, rank_near)
        position = jnp.where(late, back, front)
        meta_ref[0, position] = i
        meta_ref[1, position] = jnp.where(near | far, p_dev + came, lax.rem(a, p_dev))
        meta_ref[2, position] = a
        meta_ref[3, position] = jnp.where(near | far, p_dev + moved, lax.rem(a, p_dev))
        front = front + jnp.where(late, 0, 1)
        back = back - jnp.where(late, 1, 0)
        rank_near = rank_near + near.astype(I32)
        rank_far = rank_far + far.astype(I32)
    for q, batch in enumerate(batches):
        for k in range(4):
            value = column([tables[k][meta_ref[2, batch[b % len(batch)]]] for b in range(ROWS)])
            cols_ref[q, k] = jnp.broadcast_to(value, (ROWS, LANES))
        order = column([meta_ref[0, batch[b % len(batch)]] for b in range(ROWS)]).astype(F32)
        cols_ref[q, 4] = jnp.broadcast_to(order, (ROWS, LANES))
    prior = column([tables[4][anc_ref[group * p_dev + i]] for i in range(p_dev)])
    prior_ref[...] = jnp.broadcast_to(prior, (ROWS, LANES))
    for copy in copies:
        copy.wait()


def lane_pick(blocks, index):
    low = index & (LANES - 1)
    high = index >> 7
    out = None
    for k, block in blocks:
        got = jnp.take_along_axis(block, low, axis=1, mode="promise_in_bounds")
        out = got if out is None else jnp.where(high == k, got, out)
    return out


def column(scalars):
    rows = lax.broadcasted_iota(I32, (ROWS, 1), 0)
    out = jnp.zeros((ROWS, 1), scalars[0].dtype)
    for b, scalar in enumerate(scalars):
        out = jnp.where(rows == b, scalar, out)
    return out


def index_kernel(batches, s_dev, margin, meta_ref, count_ref, first_ref, anc_ref,
                 states_ref, vols_ref, *outs):
    *outs, table, sems = outs
    bases, outs = outs[: 2 * len(batches)], outs[2 * len(batches) :]
    p_dev = states_ref.shape[0]
    for q, batch in enumerate(batches):
        for k, at in enumerate(batch):
            place = meta_ref[1, at]

            @pl.when(place < p_dev)
            def _(k=k, at=at, place=place, out=bases[2 * q]):
                pltpu.make_async_copy(
                    states_ref.at[jnp.minimum(place, p_dev - 1)], out.at[k], sems.at[at]
                ).start()

    table[...] = vols_ref[...].astype(F32)
    for q, batch in enumerate(batches):
        places = [jnp.minimum(meta_ref[1, batch[b % len(batch)]], p_dev - 1) for b in range(ROWS)]
        bases[2 * q + 1][...] = jnp.concatenate([table[pl.ds(p, 1), :] for p in places], axis=0)
    shard = lax.axis_index("state")
    base = shard * s_dev
    even = lax.rem(shard, 2) == 0
    lanes = lax.broadcasted_iota(I32, (ROWS, LANES), 1)
    for q, batch in enumerate(batches):
        src_ref, src_t_ref, edge_ref, edge_t_ref = outs[4 * q : 4 * q + 4]
        for step in range(STEPS):
            who = [meta_ref[0, batch[b % len(batch)]] for b in range(ROWS)]
            chosen = jnp.concatenate([anc_ref[step, pl.ds(i, 1), :] for i in who], axis=0)
            blocks = [chosen[:, k * LANES : (k + 1) * LANES] for k in range(chosen.shape[1] // LANES)]
            count = column([count_ref[step, i] for i in who])
            shift = column([base - first_ref[step, i] for i in who])
            sources = []
            for o in range(s_dev // LANES):
                relative = o * LANES + lanes + shift
                own = lane_pick(list(enumerate(blocks)), jnp.clip(relative, 0, chosen.shape[1] - 1))
                sources.append(
                    jnp.where(
                        relative < 0,
                        relative + margin,
                        jnp.where(relative < count, margin + own, margin + s_dev + relative - count),
                    )
                )
            source = jnp.concatenate(sources, axis=1)
            src_ref[step] = source
            src_t_ref[step] = source.T
            head = jnp.concatenate(blocks[: margin // LANES], axis=1)
            tail = [
                lane_pick(list(enumerate(blocks)), count - margin + o * LANES + lanes)
                for o in range(margin // LANES)
            ]
            tail = jnp.concatenate(tail, axis=1)
            edge = jnp.concatenate([jnp.where(even, tail, head), jnp.where(even, head, tail)], axis=1)
            edge_ref[step] = edge
            edge_t_ref[step] = edge.T
    for q, batch in enumerate(batches):
        for k, at in enumerate(batch):

            @pl.when(meta_ref[1, at] < p_dev)
            def _(k=k, at=at, out=bases[2 * q]):
                pltpu.make_async_copy(states_ref.at[0], out.at[k], sems.at[at]).wait()


def one_hot(index, columns):
    index = index.astype(jnp.int16)
    lanes = lax.broadcasted_iota(jnp.int16, (index.shape[0], columns), 1)
    return jnp.where(index == lanes, BF16(1), BF16(0))


def send_edges(batch, margin, cloud_at, vol, edge, edge_t, pair_ref, other_ref):
    s_dev = vol.shape[1]
    blocks = [(k, vol[:, k * LANES : (k + 1) * LANES]) for k in range(s_dev // LANES)]
    width = pair_ref.shape[1]
    for out, start in ((pair_ref, 0), (other_ref, margin)):
        picked = [
            lane_pick(blocks, edge[:, start + o * LANES : start + (o + 1) * LANES])
            for o in range(margin // LANES)
        ]
        picked.append(jnp.zeros((ROWS, width - margin), F32))
        flat = jnp.concatenate(picked, axis=1)
        flat = jnp.concatenate([flat, jnp.zeros((PAD - ROWS, width), F32)], axis=0)
        out[pl.ds(batch * margin, PAD), :] = flat.astype(BF16)
    for b in range(batch):
        rows = jnp.dot(
            one_hot(edge_t[:, b : b + 1], s_dev), cloud_at(b), preferred_element_type=F32
        ).astype(BF16)
        pair_ref[pl.ds(b * margin, margin), :] = rows[:margin]
        other_ref[pl.ds(b * margin, margin), :] = rows[margin:]


def fetch_kernel(batch, first_place, p_dev, margin, vol_rows, recv_slots, meta_ref, base_ref, base_vol_ref,
                 edge_ref, edge_t_ref, *rest):
    recv = rest[: len(recv_slots)]
    cloud_ref, vol_ref, pair_ref, other_ref, table, sems = rest[-6:]
    s_dev = vol_ref.shape[1]
    places = [meta_ref[1, first_place + b % batch] for b in range(ROWS)]
    for b in range(batch):
        for ref, codes in zip(recv, recv_slots):
            for code, at, _ in codes:

                @pl.when(places[b] == code)
                def _(b=b, ref=ref, at=at):
                    pltpu.make_async_copy(
                        ref.at[pl.ds(at, s_dev)], cloud_ref.at[b], sems.at[b]
                    ).start()

    table[...] = jnp.zeros(table.shape, F32)
    for ref, codes in zip(recv, recv_slots):
        start = codes[0][2]
        length = -(-len(codes) * vol_rows // PAD) * PAD
        rows = ref[pl.ds(start, length), :].astype(F32)
        for code, _, at in codes:
            pieces = [rows[at - start + r : at - start + r + 1] for r in range(vol_rows)]
            table[pl.ds(code, 1), :] = jnp.concatenate(pieces, axis=1)
    vol = jnp.concatenate([table[pl.ds(place, 1), :] for place in places], axis=0)
    vol = jnp.where(column(places) < p_dev, base_vol_ref[...], vol)
    vol_ref[...] = vol
    for b in range(batch):

        @pl.when(places[b] >= p_dev)
        def _(b=b):
            pltpu.make_async_copy(recv[0].at[pl.ds(0, s_dev)], cloud_ref.at[b], sems.at[b]).wait()

    send_edges(batch, margin, lambda b: cloud_ref[b], vol, edge_ref[0], edge_t_ref[0], pair_ref, other_ref)


def matrix_kernel(batch, first_place, half, ways, sides, meta_ref, transition_ref, *rest):
    pieces, (out_ref, sems) = rest[: sides * ways], rest[-2:]
    p_dev, width, _ = transition_ref.shape
    per_part = half // ways
    mine = lax.rem(lax.axis_index("state"), ways)
    for b in range(batch):
        place = meta_ref[3, first_place + b]
        moved = jnp.maximum(place - p_dev, 0)
        slot = lax.rem(moved, half)
        chosen = jnp.where(place < p_dev, -1, lax.div(moved, half) * ways + (lax.div(slot, per_part) ^ mine))

        @pl.when(place < p_dev)
        def _(b=b, place=place):
            pltpu.make_async_copy(
                transition_ref.at[jnp.minimum(place, p_dev - 1)], out_ref.at[b], sems.at[b]
            ).start()

        for k, piece in enumerate(pieces):

            @pl.when(chosen == k)
            def _(b=b, piece=piece, slot=slot):
                at = pl.multiple_of(lax.rem(slot, per_part) * width, width)
                pltpu.make_async_copy(piece.at[pl.ds(at, width)], out_ref.at[b], sems.at[b]).start()

    for b in range(batch):
        pltpu.make_async_copy(transition_ref.at[0], out_ref.at[b], sems.at[b]).wait()


def own_kernel(batch, step, margin, src_t_ref, cloud_ref, out_ref):
    s_dev = cloud_ref.shape[1]
    for b in range(batch):
        index = src_t_ref[step][:, b : b + 1] - margin
        out_ref[b] = jnp.dot(
            one_hot(index, s_dev), cloud_ref[b], preferred_element_type=F32
        ).astype(BF16)


def step_kernel(batch, first_place, step, margin, merge, cols_ref, own_ref, pair_ref, other_ref, vol_ref,
                src_ref, src_t_ref, edge_ref, edge_t_ref, matrix_ref, noise_ref, vnoise_ref,
                loading_ref, wanted_ref, *rest):
    last = step == STEPS - 1
    s_dev = vol_ref.shape[1]
    rest = list(rest)
    stat_in = rest.pop(0) if step else None
    if last:
        if merge:
            vol_before, stat_before = rest[:2]
            rest = rest[2:]
        cloud_out, vol_out, stat_ref = rest
    else:
        cloud_out, vol_out, stat_ref, pair_out, other_out = rest
    even = lax.rem(lax.axis_index("state"), 2) == 0
    source = src_ref[step]
    vol = vol_ref[...]
    blocks = [(k, vol[:, k * LANES : (k + 1) * LANES]) for k in range(s_dev // LANES)]

    def edge_vols(ref):
        return ref[pl.ds(batch * margin, PAD), :].astype(F32)[:ROWS]

    pair_v, other_v = edge_vols(pair_ref), edge_vols(other_ref)
    low_v, high_v = jnp.where(even, other_v, pair_v), jnp.where(even, pair_v, other_v)
    picked = []
    for o in range(s_dev // LANES):
        index = source[:, o * LANES : (o + 1) * LANES]
        own = lane_pick(blocks, jnp.clip(index - margin, 0, s_dev - 1))
        if o < margin // LANES:
            low = [(k, low_v[:, k * LANES : (k + 1) * LANES]) for k in range(margin // LANES)]
            own = jnp.where(index < margin, lane_pick(low, index), own)
        if o >= (s_dev - margin) // LANES:
            high = [(k, high_v[:, k * LANES : (k + 1) * LANES]) for k in range(margin // LANES)]
            above = jnp.clip(index - margin - s_dev, 0, margin - 1)
            own = jnp.where(index >= margin + s_dev, lane_pick(high, above), own)
        picked.append(own)
    picked = jnp.concatenate(picked, axis=1)

    def param(k):
        return cols_ref[k][:, :1]

    center, persist, spread = param(0), param(1), param(2)
    h = center + persist * (picked - center) + spread * vnoise_ref[pl.ds(step, 1), :]
    scale_t = jnp.exp(0.5 * h).T
    vol_new = h.astype(BF16).astype(F32)
    if not last:
        vol_out[...] = vol_new

    wanted = wanted_ref[pl.ds(step, 1), :]
    tile = s_dev // 2
    lanes = lax.broadcasted_iota(I32, (tile, LANES), 1)
    squares = [jnp.zeros((tile, LANES), F32)] * 2
    for b in range(batch):
        for r in range(2):
            span = pl.ds(r * tile, tile)
            index = src_t_ref[step, span, :][:, b : b + 1]
            own = own_ref[b, span, :]
            pair, other = pair_ref[pl.ds(b * margin, margin), :], other_ref[pl.ds(b * margin, margin), :]
            if r == 0:
                patch = jnp.dot(
                    one_hot(index[:margin], margin),
                    jnp.where(even, other, pair),
                    preferred_element_type=F32,
                )
                cloud = jnp.concatenate(
                    [(own[:margin].astype(F32) + patch).astype(BF16), own[margin:]], axis=0
                )
            else:
                patch = jnp.dot(
                    one_hot(index[tile - margin :] - (margin + s_dev), margin),
                    jnp.where(even, pair, other),
                    preferred_element_type=F32,
                )
                cloud = jnp.concatenate(
                    [own[: tile - margin], (own[tile - margin :].astype(F32) + patch).astype(BF16)],
                    axis=0,
                )
            drift = jnp.dot(cloud, matrix_ref[b], preferred_element_type=F32)
            noise = noise_ref[step, span, :].astype(F32)
            cloud = (drift + scale_t[r * tile : (r + 1) * tile, b : b + 1] * noise).astype(BF16)
            cloud_out[b, span, :] = cloud
            misfit = wanted - jnp.dot(cloud, loading_ref[...], preferred_element_type=F32)
            square = jnp.sum(misfit * misfit, axis=1, keepdims=True)
            squares[r] = jnp.where(lanes == b, square, squares[r])
    if not last:
        send_edges(
            batch, margin, lambda b: cloud_out[b], vol_new, edge_ref[step + 1], edge_t_ref[step + 1],
            pair_out, other_out,
        )
    square = jnp.concatenate(squares, axis=0).T[:ROWS]
    precision = param(3)
    maturities = wanted_ref.shape[1]
    weights = -0.5 * precision * square + 0.5 * maturities * jnp.log(precision)
    peak = jnp.max(weights, axis=1, keepdims=True)
    mass = jnp.sum(jnp.exp(weights - peak), axis=1, keepdims=True)
    lane = lax.broadcasted_iota(I32, (ROWS, LANES), 1)
    before = [stat_in[0], stat_in[1]] if step else [jnp.zeros((ROWS, LANES), F32)] * 2
    stats = [jnp.where(lane == step, new, old) for new, old in zip((peak, mass), before)]
    if last:
        rows = lax.broadcasted_iota(I32, (ROWS, 1), 0).astype(F32)
        order = param(4)
        vol_all = vol_before[...].astype(F32) if merge else jnp.zeros(vol_new.shape, F32)
        placed = [stat_before[0], stat_before[1]] if merge else [jnp.zeros((ROWS, LANES), F32)] * 2
        for b in range(batch):
            here = rows == order[b : b + 1]
            vol_all = jnp.where(here, vol_new[b : b + 1], vol_all)
            placed = [jnp.where(here, new[b : b + 1], old) for new, old in zip(stats, placed)]
        vol_out[...] = vol_all.astype(BF16)
        stats = placed
    stat_ref[0] = stats[0]
    stat_ref[1] = stats[1]

def write_kernel(batches, meta_ref, *rest):
    clouds, (final_ref, sems) = rest[: len(batches)], rest[len(batches) :]
    copies = []
    for cloud, batch in zip(clouds, batches):
        for k, place in enumerate(batch):
            copy = pltpu.make_async_copy(
                cloud.at[k], final_ref.at[meta_ref[0, place]], sems.at[place]
            )
            copy.start()
            copies.append(copy)
    for copy in copies:
        copy.wait()


def join_kernel(finish, whole_rows, *refs):
    mine_ref, others, (out_ref,) = refs[0], refs[1:-1], refs[-1:]
    if finish:
        prior_ref, others = others[0], others[1:]
    peak, mass = mine_ref[0], mine_ref[1]
    for other in others:
        other_peak = other[0]
        top = jnp.maximum(peak, other_peak)
        mass = mass * jnp.exp(peak - top) + other[1] * jnp.exp(other_peak - top)
        peak = top
    if not finish:
        out_ref[0] = peak
        out_ref[1] = mass
        return
    lane = lax.broadcasted_iota(I32, (ROWS, LANES), 1)
    gained = peak + jnp.log(jnp.where(lane < STEPS, mass, 1.0)) - math.log(whole_rows)
    gained = jnp.sum(jnp.where(lane < STEPS, gained, 0.0), axis=1, keepdims=True)
    total = jnp.broadcast_to(prior_ref[:, :1] + gained, (ROWS, LANES))
    out_ref[...] = total.T[:1, :]


def join(stats, others, whole_rows, prior=None):
    operands = [stats] + ([] if prior is None else [prior]) + list(others)
    shape = stats.shape if prior is None else (1, ROWS)
    return call(
        functools.partial(join_kernel, prior is not None, whole_rows),
        jax.ShapeDtypeStruct(shape, F32),
        [vmem()] * len(operands),
        vmem(),
        "join",
        nbytes=1 << 14,
    )(*operands)


def swaps(count):
    rounds = []
    for offset in (0, 1):
        partner = [(i - offset ^ 1) + offset for i in range(count)]
        rounds.append([(i, p if 0 <= p < count else i) for i, p in enumerate(partner)])
    return rounds


def doubling(count):
    distance = 1
    while distance < count:
        yield distance, [(i, i ^ distance) for i in range(count)]
        distance *= 2


def prefix_counts(number):
    count, here = lax.axis_size("state"), lax.axis_index("state")
    if count & (count - 1):
        every = lax.all_gather(number, "state")
        before = jnp.arange(count) < here
        return jnp.sum(jnp.where(before[:, None, None], every, 0), axis=0)
    before, total = jnp.zeros_like(number), number
    for distance, pairs in doubling(count):
        other = lax.ppermute(total, "state", pairs)
        before = before + jnp.where((here & distance) != 0, other, 0)
        total = total + other
    return before


def combined_mass(stats, prior, whole_rows):
    count = lax.axis_size("state")
    if count & (count - 1):
        every = lax.all_gather(stats, "state")
        return join(every[0], [every[k] for k in range(1, count)], whole_rows, prior)
    if count == 1:
        return join(stats, [], whole_rows, prior)
    distances = [distance for distance, _ in doubling(count)]
    size = 1
    while distances:
        now, distances = distances[:size], distances[size:]
        size = 2
        apart = [sum(d for j, d in enumerate(now) if k >> j & 1) for k in range(1, 1 << len(now))]
        others = [lax.ppermute(stats, "state", [(i, i ^ d) for i in range(count)]) for d in apart]
        stats = join(stats, others, whole_rows, None if distances else prior)
    return stats


def local(
    states,
    log_vol,
    transition,
    loading,
    yields,
    state_noise,
    vol_noise,
    vol_mean,
    vol_persist,
    vol_scale,
    obs_prec,
    prior_loglik,
    ancestors,
    counts,
    local_anc,
):
    p_dev, s_dev, width = states.shape
    maturities = loading.shape[1]
    groups, shards = lax.axis_size("theta"), lax.axis_size("state")
    half = p_dev // 2
    margin = s_dev // 4
    batch = p_dev // 2
    batches = [tuple(range(q * batch, (q + 1) * batch)) for q in range(p_dev // batch)]
    vol_rows = s_dev // width
    ways = next(w for w in (2, 1) if half % w == 0 and shards % w == 0)
    per_part = half // ways

    early = half // 2
    relayed = groups == 4
    tail = -(-early * vol_rows // PAD) * PAD
    block = early * s_dev + tail
    part_rows = per_part * width
    if relayed:
        takes = [((1, 0), (0, 0)), ((0, 0), (0, early)), ((1, early), (0, 0)), ((0, early), (0, 0))]
    else:
        takes = [((0, 0),) * 2, ((0, early),) * 2, ((1, 0),) * 2, ((1, early),) * 2]
    packed_shapes = [
        jax.ShapeDtypeStruct((rows, width), BF16)
        for rows in (block, block + part_rows, block, block, part_rows)
    ]
    small = ancestors.shape
    first_hop, near_hop, second_hop, third_hop, far_part, meta, cols, prior = call(
        functools.partial(pack_kernel, groups, relayed, takes, tail, batches, ways, vol_rows),
        packed_shapes
        + [
            jax.ShapeDtypeStruct((4, p_dev), I32),
            jax.ShapeDtypeStruct((len(batches), 5, ROWS, LANES), F32),
            jax.ShapeDtypeStruct((ROWS, LANES), F32),
        ],
        [anywhere()] * 9,
        [vmem()] * 5 + [smem(), vmem(), vmem()],
        "pack",
        [pltpu.SMEM(small, I32)]
        + [pltpu.SMEM(small, F32)] * 5
        + [
            pltpu.SMEM((2, half), I32),
            pltpu.VMEM((p_dev, s_dev), BF16),
            pltpu.SemaphoreType.DMA((7,)),
            pltpu.SemaphoreType.DMA((2, per_part)),
            pltpu.SemaphoreType.DMA((4, early)),
        ],
        nbytes=4 * half * s_dev * width * 2,
        limit=PACK_LIMIT,
    )(ancestors, vol_mean, vol_persist, vol_scale, obs_prec, prior_loglik, log_vol, states, transition)

    near_pairs, far_pairs = swaps(groups)
    far_part = lax.ppermute(far_part, "theta", far_pairs)
    first_in = lax.ppermute(first_hop, "theta", near_pairs)
    near = lax.ppermute(near_hop, "theta", near_pairs)
    if relayed:
        cross_pairs = [(i, i ^ 2) for i in range(groups)]
        far_first = lax.ppermute(first_in, "theta", cross_pairs)
        across = lax.ppermute(second_hop, "theta", cross_pairs)
        group = lax.axis_index("theta")
        inner = (group > 0) & (group < groups - 1)
        onward, local_anc = lax.optimization_barrier((jnp.where(inner, third_hop, across), local_anc))
        far_last = lax.ppermute(onward, "theta", near_pairs)
    else:
        far_first = lax.ppermute(second_hop, "theta", far_pairs)
        far_last = lax.ppermute(third_hop, "theta", far_pairs)

    number = counts[:, :, 0]
    first = prefix_counts(number)
    cloud_shape = jax.ShapeDtypeStruct((batch, s_dev, width), BF16)
    vol_shape = jax.ShapeDtypeStruct((ROWS, s_dev), F32)
    index_shapes = [cloud_shape, vol_shape] * len(batches) + [
        jax.ShapeDtypeStruct((STEPS, ROWS, s_dev), I32),
        jax.ShapeDtypeStruct((STEPS, s_dev, ROWS), I32),
        jax.ShapeDtypeStruct((STEPS, ROWS, 2 * margin), I32),
        jax.ShapeDtypeStruct((STEPS, 2 * margin, ROWS), I32),
    ] * len(batches)
    indices = call(
        functools.partial(index_kernel, batches, s_dev, margin),
        index_shapes,
        [smem()] * 3 + [vmem(), anywhere(), vmem()],
        [vmem()] * len(index_shapes),
        "indices",
        [pltpu.VMEM((p_dev, s_dev), F32), pltpu.SemaphoreType.DMA((p_dev,))],
        nbytes=1 << 18,
    )(meta, number, first, local_anc, states, log_vol)
    bases, indices = indices[: 2 * len(batches)], indices[2 * len(batches) :]

    near, _ = lax.optimization_barrier((near, indices[-1]))
    vols_at = early * s_dev
    arrivals = [(first_in, 0), (near, early), (far_first, half), (far_last, half + early)]
    arrivals = [
        (x, tuple((p_dev + code + k, k * s_dev, vols_at + k * vol_rows) for k in range(early)))
        for x, code in arrivals
    ]
    pair_round, other_round = swaps(shards)
    edge_shape = jax.ShapeDtypeStruct((batch * margin + PAD, width), BF16)
    stat_shape = jax.ShapeDtypeStruct((2, ROWS, LANES), F32)
    before = []
    done_clouds = []
    pieces = []
    follow = []
    for q in range(len(batches)):
        src, src_t, edge, edge_t = indices[4 * q : 4 * q + 4]
        recv, recv_slots = zip(*(arrivals if q else arrivals[:2]))
        cloud, vol, pair, other = call(
            functools.partial(fetch_kernel, batch, q * batch, p_dev, margin, vol_rows, recv_slots),
            [cloud_shape, vol_shape, edge_shape, edge_shape],
            [smem()] + [vmem()] * (4 + len(recv) + len(follow)),
            [vmem()] * 4,
            "fetch",
            [pltpu.VMEM((2 * p_dev, s_dev), F32), pltpu.SemaphoreType.DMA((batch,))],
            flops=2 * batch * 2 * margin * s_dev * width,
            nbytes=2 * batch * s_dev * width * 2,
            aliases={1: 0},
        )(meta, *bases[2 * q : 2 * q + 2], edge, edge_t, *recv, *follow)
        stat = None
        for step in range(STEPS):
            last = step == STEPS - 1
            other_in = lax.ppermute(other, "state", other_round)
            pair_in = lax.ppermute(pair, "state", pair_round)
            own = call(
                functools.partial(own_kernel, batch, step, margin),
                cloud_shape,
                [vmem(), vmem()],
                vmem(),
                "own_rows",
                flops=2 * batch * s_dev * s_dev * width,
                nbytes=batch * s_dev * width * 4,
            )(src_t, cloud)
            if step == 0:
                if q == 0:
                    part = near[block:]
                else:
                    part, _ = lax.optimization_barrier((far_part, *follow))
                pieces.append(part)
                if ways == 2:
                    pieces.append(lax.ppermute(part, "state", [(i, i ^ 1) for i in range(shards)]))
                matrices = call(
                    functools.partial(matrix_kernel, batch, q * batch, half, ways, q + 1),
                    jax.ShapeDtypeStruct((batch, width, width), BF16),
                    [smem()] + [anywhere()] * (1 + len(pieces)),
                    vmem(),
                    "matrices",
                    [pltpu.SemaphoreType.DMA((batch,))],
                    nbytes=batch * width * width * 4,
                )(meta, transition, *pieces)
            operands = [
                cols[q], own, pair_in, other_in, vol, src, src_t, edge, edge_t, matrices,
                state_noise, vol_noise, loading, yields,
            ]
            specs = [vmem()] * len(operands)
            if step:
                operands.append(stat)
                specs.append(vmem())
            if last:
                operands += before
                specs += [vmem()] * len(before)
                out_shape = [cloud_shape, jax.ShapeDtypeStruct(log_vol.shape, BF16), stat_shape]
                out_specs = [vmem()] * 3
            else:
                out_shape = [cloud_shape, vol_shape, stat_shape, edge_shape, edge_shape]
                out_specs = [vmem()] * 5
            results = call(
                functools.partial(step_kernel, batch, q * batch, step, margin, bool(before)),
                out_shape,
                specs,
                out_specs,
                "step",
                flops=2 * batch * s_dev * width * (width + maturities + margin),
                nbytes=batch * s_dev * width * 8,
            )(*operands)
            if last:
                cloud, *before = results
                done_clouds.append(cloud)
            else:
                cloud, vol, stat, pair, other = results
                follow = [stat] if step == 0 else follow
    vols, stats = before
    final = call(
        functools.partial(write_kernel, batches),
        jax.ShapeDtypeStruct(states.shape, BF16),
        [smem()] + [vmem()] * len(batches),
        anywhere(),
        "write",
        [pltpu.SemaphoreType.DMA((p_dev,))],
        nbytes=2 * p_dev * s_dev * width * 2,
    )(meta, *done_clouds)
    total = combined_mass(stats, prior, s_dev * shards)
    return (final, vols, total.reshape(p_dev))


def solution(mesh):
    placed = (
        P("theta", "state", None),
        P("theta", "state"),
        P("theta", None, None),
        P(),
        P(),
        P(None, "state", None),
        P(None, "state"),
        P(),
        P(),
        P(),
        P(),
        P(),
        P(),
        P(None, "theta", "state"),
        P(None, "theta", "state"),
    )
    return jax.shard_map(
        local,
        mesh=mesh,
        in_specs=placed,
        out_specs=(P("theta", "state", None), P("theta", "state"), P("theta")),
        check_vma=False,
    )
```
